32 devices in a mesh: ctx: 16 (over z, y, x), tp: 2 (over core).
Axes of the slice: x: 2, y: 2, z: 4, core: 2. Of those that a mesh axis runs over, the one named last changes fastest.
Arguments:
- queries: bfloat16 [4096, 1536], P('ctx', 'tp'), may hold values from -8 to 8
- key_vectors: bfloat16 [4096, 1536], P('ctx', 'tp'), may hold values from -8 to 8
- value_vectors: bfloat16 [4096, 1536], P('ctx', 'tp'), may hold values from -6 to 6
- out_weight: bfloat16 [1536, 3072], P('tp'), may hold values from -0.15625 to 0.15625
- out_grad: bfloat16 [4096, 3072], P('ctx', 'tp'), may hold values from -6 to 6
- block_segment: int32 [32], replicated, may hold values from 0 to 5, as said below
Outputs:
- attention_out: bfloat16 [4096, 3072], P('ctx', 'tp')
- grad_queries: bfloat16 [4096, 1536], P('ctx', 'tp')
- grad_keys: bfloat16 [4096, 1536], P('ctx', 'tp')
- grad_values: bfloat16 [4096, 1536], P('ctx', 'tp')
- grad_weight: float32 [1536, 3072], P('tp')
The draws below stay inside these ranges and needn't reach their ends.
Inputs may be any that keep to these rules, and one draw needn't show every extreme that they name: `block_segment`: blocks 0 to 3 hold 0; the other blocks form five runs of consecutive blocks, one run for each of 1 to 5, run lengths within one of each other, in an order that varies from draw to draw.
All inputs are finite; a program needn't handle non-finite values.
Results may differ from the reference program's by a relative error of at most 0.02.
Values may be sent and summed in bfloat16 or wider, within the bound.
No kernel may reach another device: no remote copies, remote signals or barrier semaphores. Data moves between devices by JAX's collectives and lax.ppermute only.
A program may use at most 128 MiB of HBM per device.

```python
import jax
import jax.numpy as jnp
from jax import lax

D = 3072
HEADS = 12
HEAD = 128
BLK = 128
TXT_BLK = 4
TOK_DEV = 256
TOKENS = 4096
NBLK = 32
N_CTX = 16


def draw_queries(key, part):
    key = jax.random.fold_in(key, 3)
    base = jnp.clip(jax.random.normal(key, (TOKENS, HEADS * HEAD), jnp.float32), -8.0, 8.0)
    return base.astype(jnp.bfloat16)


def draw_key_vectors(key, part):
    key = jax.random.fold_in(key, 7)
    base = jnp.clip(jax.random.normal(key, (TOKENS, HEADS * HEAD), jnp.float32), -8.0, 8.0)
    return base.astype(jnp.bfloat16)


def draw_block_segment(key, part):
    key = jax.random.fold_in(key, 11)
    order = jax.random.permutation(key, 5).astype(jnp.int32) + 1
    rest = NBLK - TXT_BLK
    lengths = rest // 5 + (jnp.arange(5) < rest % 5).astype(jnp.int32)
    ends = TXT_BLK + jnp.cumsum(lengths)
    index = jnp.arange(NBLK)
    run = jnp.sum((index[:, None] >= ends[None, :]).astype(jnp.int32), axis=1)
    run = jnp.minimum(run, 4)
    return jnp.where(index < TXT_BLK, 0, order[run]).astype(jnp.int32)


def levels(rng, extent, split, least, largest):
    loudness, own = 1.0, jax.random.fold_in(rng, 6)
    for position, parts in split:
        heights = jnp.exp(jax.random.uniform(jax.random.fold_in(own, position), (parts,), jnp.float32, least / len(split), largest / len(split)))
        loudness = loudness * jnp.repeat(heights, extent[position] // parts).reshape([-1 if axis == position else 1 for axis in range(len(extent))])
    return loudness


def noise(own_key, dims, width, bound, pieces=(), kind=jnp.bfloat16):
    result = jax.random.normal(own_key, dims, jnp.float32) * width
    if len(pieces) > 0:
        result = levels(own_key, dims, pieces, -0.22, 0.18) * result
    return jnp.clip(result, min=-bound, max=bound).astype(kind)


def setup_inputs(seed: int = 0) -> dict:
    key_list = jax.random.split(jax.random.key(seed), 7)
    queries = draw_queries(jax.random.fold_in(key_list[6], 71), 0)
    key_vectors = draw_key_vectors(jax.random.fold_in(key_list[6], 71), 0)
    value_vectors = noise(key_list[2], (TOKENS, HEADS * HEAD), 1.0, 6.0, ((0, 16), (1, 2)))
    out_weight = noise(key_list[3], (HEADS * HEAD, D), (HEADS * HEAD) ** -0.5, 0.15625, ((0, 2),))
    out_grad = noise(key_list[4], (TOKENS, D), 1.0, 6.0, ((0, 16), (1, 2)))
    block_segment = draw_block_segment(jax.random.fold_in(key_list[6], 71), 0)
    return dict(queries=queries, key_vectors=key_vectors, value_vectors=value_vectors, out_weight=out_weight, out_grad=out_grad, block_segment=block_segment)


neg_big = -1.0e30
target_id = 5


def permitted_mask(query_seg, key_seg):
    query_col = query_seg[:, None]
    key_row = key_seg[None, :]
    return (query_col == 0) | (query_col == target_id) | (key_row == 0) | (query_col == key_row)


def reference(queries, key_vectors, value_vectors, out_weight, out_grad, block_segment):
    score_scale = HEAD ** -0.5
    seg_rows = jnp.repeat(block_segment, BLK, total_repeat_length=TOKENS)
    seg_shards = seg_rows.reshape(N_CTX, TOK_DEV)

    def split_heads(matrix):
        return matrix.reshape(TOKENS, HEADS, HEAD).transpose(1, 0, 2)

    def join_heads(stack):
        return stack.reshape(HEADS, TOKENS, HEAD).transpose(1, 0, 2).reshape(TOKENS, HEADS * HEAD)

    q_heads = split_heads(queries)
    k_heads = split_heads(key_vectors)
    v_heads = split_heads(value_vectors)
    q_shards = q_heads.reshape(HEADS, N_CTX, TOK_DEV, HEAD)

    def probabilities(q_shard, k_head, shard_seg):
        scores = jnp.dot(q_shard, k_head.T, preferred_element_type=jnp.float32) * score_scale
        permitted = permitted_mask(shard_seg, seg_rows)
        scores = jnp.where(permitted, scores, neg_big)
        row_top = jnp.max(scores, axis=1, keepdims=True)
        expo = jnp.where(permitted, jnp.exp(scores - row_top), 0.0)
        return expo / jnp.sum(expo, axis=1, keepdims=True)

    def forward_head(operands):
        q_head_shards, k_head, v_head = operands

        def one_shard(shard_ops):
            q_shard, shard_seg = shard_ops
            weights = probabilities(q_shard, k_head, shard_seg).astype(jnp.bfloat16)
            return jnp.dot(weights, v_head, preferred_element_type=jnp.float32).astype(jnp.bfloat16)

        return lax.map(one_shard, (q_head_shards, seg_shards))

    attn_heads = lax.map(forward_head, (q_shards, k_heads, v_heads))
    attention = join_heads(attn_heads)
    attention_out = jnp.dot(attention, out_weight, preferred_element_type=jnp.float32).astype(jnp.bfloat16)
    grad_attn = lax.dot_general(out_grad, out_weight, (((1,), (1,)), ((), ())),
                                preferred_element_type=jnp.float32).astype(jnp.bfloat16)
    grad_weight = lax.dot_general(attention, out_grad, (((0,), (0,)), ((), ())),
                                  preferred_element_type=jnp.float32)
    g_shards = split_heads(grad_attn).reshape(HEADS, N_CTX, TOK_DEV, HEAD)

    def backward_head(operands):
        q_head_shards, k_head, v_head, g_head_shards, a_head_shards = operands

        def one_shard(totals, shard_ops):
            q_shard, g_shard, a_shard, shard_seg = shard_ops
            prob_rows = probabilities(q_shard, k_head, shard_seg)
            prob_grads = jnp.dot(g_shard, v_head.T, preferred_element_type=jnp.float32)
            row_delta = jnp.sum(g_shard.astype(jnp.float32) * a_shard.astype(jnp.float32), axis=1, keepdims=True)
            score_grads = (prob_rows * (prob_grads - row_delta)).astype(jnp.bfloat16)
            query_grad = (score_scale * jnp.dot(score_grads, k_head, preferred_element_type=jnp.float32)).astype(jnp.bfloat16)
            key_part = (score_scale * lax.dot_general(score_grads, q_shard, (((0,), (0,)), ((), ())),
                                                      preferred_element_type=jnp.float32)).astype(jnp.bfloat16)
            value_part = lax.dot_general(prob_rows.astype(jnp.bfloat16), g_shard, (((0,), (0,)), ((), ())),
                                         preferred_element_type=jnp.float32).astype(jnp.bfloat16)
            return (totals[0] + key_part.astype(jnp.float32), totals[1] + value_part.astype(jnp.float32)), query_grad

        zero_rows = jnp.zeros((TOKENS, HEAD), jnp.float32)
        (key_sum, value_sum), query_grads = lax.scan(
            one_shard, (zero_rows, zero_rows), (q_head_shards, g_head_shards, a_head_shards, seg_shards))
        return query_grads, key_sum.astype(jnp.bfloat16), value_sum.astype(jnp.bfloat16)

    grad_q, grad_k, grad_v = lax.map(backward_head, (q_shards, k_heads, v_heads, g_shards, attn_heads))
    return attention_out, join_heads(grad_q), join_heads(grad_k), join_heads(grad_v), grad_weight
```

```python
import functools
import math

import jax
import jax.numpy as jnp
from jax import lax
from jax.experimental import pallas as pl
from jax.experimental.pallas import tpu as pltpu
from jax.sharding import PartitionSpec as P

HEAD = 128
BLK = 128
TXT_BLK = 4
RUNS = 5
TARGET = 5
LOG2E = math.log2(math.e)
NEG_BIG = -1e30

NT = (((1,), (1,)), ((), ()))
TN = (((0,), (0,)), ((), ()))
F32 = jnp.float32
BF16 = jnp.bfloat16


def dot(a, b, dims=(((1,), (0,)), ((), ()))):
    return lax.dot_general(a, b, dims, preferred_element_type=F32)


def gather_tiles(k_ref, kidx_ref, row, dst, tile, count):
    for j in range(count):
        dst[pl.ds(j * tile, tile), :] = k_ref[kidx_ref[row, j]]


def forward_kernel(tile, count, full_ref, kcnt_ref, kidx_ref, q_ref, k_ref, v_ref, out_ref, lse_ref, k_few, v_few):
    row = pl.program_id(0)
    q = q_ref[0, 0]

    def finish(s, v):
        top = jnp.max(s, axis=1, keepdims=True)
        p = jnp.exp2(s - top)
        mass = jnp.sum(p, axis=1, keepdims=True)
        out = dot(p.astype(BF16), v)
        out_ref[0, 0] = (out / mass).astype(BF16)
        lse_ref[...] = jnp.broadcast_to(top + jnp.log2(mass), lse_ref.shape)

    scale = HEAD ** -0.5 * LOG2E

    @pl.when(full_ref[row] == 1)
    def _():
        keys = k_ref[...].reshape(-1, HEAD)
        finish(dot(q, keys, NT) * scale, v_ref[...].reshape(-1, HEAD))

    @pl.when(full_ref[row] == 0)
    def _():
        gather_tiles(k_ref, kidx_ref, row, k_few, tile, count)
        gather_tiles(v_ref, kidx_ref, row, v_few, tile, count)
        s = dot(q, k_few[...], NT) * scale
        column = lax.broadcasted_iota(jnp.int32, s.shape, 1)
        s = jnp.where(column < kcnt_ref[row] * tile, s, NEG_BIG)
        finish(s, v_few[...])


def backward_kernel(tile, count, full_ref, kcnt_ref, kidx_ref, q_ref, g_ref, o_ref, lse_ref, k_ref, v_ref,
                    dq_ref, dkv_ref, k_few, v_few, dk_acc, dv_acc):
    row = pl.program_id(0)
    last = pl.num_programs(0) - 1

    @pl.when(row == 0)
    def _():
        dk_acc[...] = jnp.zeros_like(dk_acc)
        dv_acc[...] = jnp.zeros_like(dv_acc)

    q = q_ref[0, 0]
    g = g_ref[0, 0]
    delta = jnp.sum(g.astype(F32) * o_ref[0, 0].astype(F32), axis=1, keepdims=True)
    lse = lse_ref[:, :1]
    unit = HEAD ** -0.5
    scale = unit * LOG2E

    def gradients(keys, values, mask):
        s = dot(q, keys, NT)
        p = jnp.exp2(s * scale - lse)
        if mask is not None:
            p = jnp.where(mask(p.shape), p, 0.0)
        ds = (p * (dot(g, values, NT) - delta)).astype(BF16)
        dq_ref[0, 0] = (dot(ds, keys) * unit).astype(BF16)
        return dot(ds, q, TN) * unit, dot(p.astype(BF16), g, TN)

    @pl.when(full_ref[row] == 1)
    def _():
        dk, dv = gradients(k_ref[...].reshape(-1, HEAD), v_ref[...].reshape(-1, HEAD), None)
        dk_acc[...] += dk.reshape(dk_acc.shape)
        dv_acc[...] += dv.reshape(dv_acc.shape)

    @pl.when(full_ref[row] == 0)
    def _():
        gather_tiles(k_ref, kidx_ref, row, k_few, tile, count)
        gather_tiles(v_ref, kidx_ref, row, v_few, tile, count)

        def mask(shape):
            return lax.broadcasted_iota(jnp.int32, shape, 1) < kcnt_ref[row] * tile

        dk, dv = gradients(k_few[...], v_few[...], mask)
        for j in range(count):
            at = kidx_ref[row, j]
            dk_acc[at] += dk[j * tile:(j + 1) * tile]
            dv_acc[at] += dv[j * tile:(j + 1) * tile]

    @pl.when(row == last)
    def _():
        parts, _, chunks, rows, _ = dkv_ref.shape
        shape = (parts, chunks, rows, HEAD)
        dkv_ref[:, 0] = dk_acc[...].reshape(shape).astype(BF16)
        dkv_ref[:, 1] = dv_acc[...].reshape(shape).astype(BF16)


def whole_block(shape):
    return pl.BlockSpec(shape, lambda *_: (0,) * len(shape))


def tile_block(which, per_chunk, tile):
    return pl.BlockSpec(
        (1, 1, tile, HEAD), lambda r, *_: (r // per_chunk, which, r % per_chunk, 0)
    )


def shifts(t, s):
    return [(c, (c + s) % t) for c in range(t)]


def per_device(n, t, queries, key_vectors, value_vectors, out_weight, out_grad, block_segment):
    rows, width = queries.shape
    heads_here = width // HEAD
    heads = heads_here * t
    sub = rows // t
    tile = min(sub, BLK)
    per_chunk = sub // tile
    core = lax.axis_index("tp")
    chunks = [h * n // heads for h in range(heads)]

    def tp_order(stack):
        return [lax.dynamic_index_in_dim(stack, (core - p) % t, 0, False) for p in range(t)]

    def tp_split(pack):
        got = [lax.dynamic_index_in_dim(pack, core, 0, False)]
        for s in range(1, t):
            block = lax.dynamic_index_in_dim(pack, (core + s) % t, 0, False)
            got.append(lax.ppermute(block, "tp", shifts(t, s)))
        return tp_order(jnp.stack(got))

    def to_heads(arrays):
        pack = jnp.stack(
            [a.reshape(t, sub, heads_here, HEAD).transpose(0, 2, 1, 3) for a in arrays], axis=2
        )
        every = jnp.concatenate(tp_split(pack), axis=0)
        empty = jnp.zeros_like(every[0])
        sent = [empty] * n
        for h, chunk in enumerate(chunks):
            sent[chunk] = every[h]
        return lax.all_to_all(jnp.stack(sent), "ctx", 0, 0, tiled=True)

    def to_tokens(pack):
        got = lax.all_to_all(pack, "ctx", 0, 0, tiled=True)
        every = jnp.stack([got[chunk] for chunk in chunks])
        every = every.reshape((t, heads_here) + every.shape[1:])
        mine = jnp.stack(tp_split(every))
        return [
            mine[:, :, a].transpose(0, 2, 1, 3).reshape(rows, width) for a in range(pack.shape[1])
        ]

    chunk_row = jnp.arange(n)[:, None] * rows + jnp.arange(per_chunk)[None, :] * tile

    def tile_segments(part):
        return jnp.take(block_segment, ((chunk_row + part * sub) // BLK).reshape(-1))

    seg_parts = [tile_segments((core - s) % t) for s in range(t)]
    seg_q = seg_parts[0]
    seg_k = jnp.concatenate(seg_parts)
    full = (seg_q == 0) | (seg_q == TARGET)
    permitted = (seg_k[None] == 0) | (seg_k[None] == seg_q[:, None])
    total_blocks = block_segment.shape[0]
    count = (TXT_BLK + -(-(total_blocks - TXT_BLK) // RUNS)) * (BLK // tile)
    kcnt = jnp.sum(permitted.astype(jnp.int32), axis=1)
    tiles_k = seg_k.shape[0]
    ids = jnp.arange(tiles_k)
    place = jnp.sum((permitted[:, None, :] & (ids[None, None, :] < ids[None, :, None])).astype(jnp.int32), axis=2)
    hit = permitted[:, None, :] & (place[:, None, :] == jnp.arange(count)[None, :, None])
    kidx = jnp.sum(jnp.where(hit, ids[None, None, :], 0), axis=2).astype(jnp.int32)
    full = full.astype(jnp.int32)

    half = out_grad.shape[1]
    grads = [out_grad] + [lax.ppermute(out_grad, "tp", shifts(t, s)) for s in range(1, t)]
    full_grad = jnp.concatenate(tp_order(jnp.stack(grads)), axis=1)

    kv = to_heads([key_vectors, value_vectors])
    grad_attn = dot(full_grad, out_weight, NT).astype(BF16)
    qg = to_heads([queries, grad_attn])

    kv_parts = jnp.stack([kv] + [lax.ppermute(kv, "tp", shifts(t, s)) for s in range(1, t)])
    keys = kv_parts[:, :, 0].reshape(tiles_k, tile, HEAD)
    values = kv_parts[:, :, 1].reshape(tiles_k, tile, HEAD)

    tiles_q = n * per_chunk
    few = [pltpu.VMEM((count * tile, HEAD), BF16)] * 2
    params = pltpu.CompilerParams(vmem_limit_bytes=48 * 2**20)
    q_block = tile_block(0, per_chunk, tile)
    g_block = tile_block(1, per_chunk, tile)
    key_block = whole_block((tiles_k, tile, HEAD))
    lse_block = pl.BlockSpec((tile, HEAD), lambda r, *_: (r, 0))
    attn, lse = pl.pallas_call(
        functools.partial(forward_kernel, tile, count),
        grid_spec=pltpu.PrefetchScalarGridSpec(
            num_scalar_prefetch=3,
            grid=(tiles_q,),
            in_specs=[q_block, key_block, key_block],
            out_specs=[q_block, lse_block],
            scratch_shapes=few,
        ),
        out_shape=[
            jax.ShapeDtypeStruct((n, 1, sub, HEAD), BF16),
            jax.ShapeDtypeStruct((tiles_q * tile, HEAD), F32),
        ],
        compiler_params=params,
        cost_estimate=pl.CostEstimate(
            flops=tiles_q * tile * tiles_k * tile * HEAD * 2, bytes_accessed=5 * 2**20, transcendentals=2**22
        ),
        name="forward",
    )(full, kcnt, kidx, qg, keys, values)

    (attention,) = to_tokens(attn)
    projected = dot(attention, out_weight)
    own = lax.dynamic_slice_in_dim(projected, core * half, half, 1)
    for s in range(1, t):
        there = lax.dynamic_slice_in_dim(projected, (core + s) % t * half, half, 1)
        own = own + lax.ppermute(there.astype(BF16), "tp", shifts(t, s)).astype(F32)
    attention_out = own.astype(BF16)
    weight_term = dot(attention, full_grad, TN)
    grad_weight = lax.psum(weight_term.astype(BF16), "ctx").astype(F32)

    dq, dkv = pl.pallas_call(
        functools.partial(backward_kernel, tile, count),
        grid_spec=pltpu.PrefetchScalarGridSpec(
            num_scalar_prefetch=3,
            grid=(tiles_q,),
            in_specs=[q_block, g_block, q_block, lse_block, key_block, key_block],
            out_specs=[q_block, whole_block((t, 2, n, sub, HEAD))],
            scratch_shapes=few + [pltpu.VMEM((tiles_k, tile, HEAD), F32)] * 2,
        ),
        out_shape=[
            jax.ShapeDtypeStruct((n, 1, sub, HEAD), BF16),
            jax.ShapeDtypeStruct((t, 2, n, sub, HEAD), BF16),
        ],
        compiler_params=params,
        cost_estimate=pl.CostEstimate(
            flops=tiles_q * tile * tiles_k * tile * HEAD * 5, bytes_accessed=8 * 2**20, transcendentals=2**22
        ),
        name="backward",
    )(full, kcnt, kidx, qg, qg, attn, lse, keys, values)

    sums = dkv[0].astype(F32)
    for s in range(1, t):
        back = [(c, (c - s) % t) for c in range(t)]
        sums = sums + lax.ppermute(dkv[s], "tp", back).astype(F32)
    sums = sums.astype(BF16).transpose(1, 0, 2, 3)
    grad_queries, grad_keys, grad_values = to_tokens(jnp.concatenate([dq, sums], axis=1))
    return attention_out, grad_queries, grad_keys, grad_values, grad_weight


def solution(mesh):
    n, t = mesh.shape["ctx"], mesh.shape["tp"]
    in_specs = (P("ctx", "tp"), P("ctx", "tp"), P("ctx", "tp"), P("tp", None), P("ctx", "tp"), P())
    out_specs = (P("ctx", "tp"), P("ctx", "tp"), P("ctx", "tp"), P("ctx", "tp"), P("tp", None))
    return jax.shard_map(
        functools.partial(per_device, n, t), mesh=mesh, in_specs=in_specs, out_specs=out_specs, check_vma=False
    )
```

```python
import functools
import math

import jax
import jax.numpy as jnp
from jax import lax
from jax.experimental import pallas as pl
from jax.experimental.pallas import tpu as pltpu
from jax.sharding import PartitionSpec as P

HEAD = 128
BLK = 128
TXT_BLK = 4
RUNS = 5
TARGET = 5
PLANES = 4
LOG2E = math.log2(math.e)
NEG_BIG = -1e30

NT = (((1,), (1,)), ((), ()))
TN = (((0,), (0,)), ((), ()))
F32 = jnp.float32
BF16 = jnp.bfloat16


def dot(a, b, dims=(((1,), (0,)), ((), ()))):
    return lax.dot_general(a, b, dims, preferred_element_type=F32)


def gather_tiles(k_ref, kidx_ref, row, dst, tile, count):
    for j in range(count):
        dst[pl.ds(j * tile, tile), :] = k_ref[kidx_ref[row, j]]


def join_parts(parts, k_all, v_all):
    shape = (k_all.shape[0] // (len(parts) // 2),) + k_all.shape[1:]
    for s in range(len(parts) // 2):
        at = pl.ds(s * shape[0], shape[0])
        k_all[at] = parts[2 * s][...].reshape(shape)
        v_all[at] = parts[2 * s + 1][...].reshape(shape)


def forward_kernel(t, tile, count, full_ref, kcnt_ref, kidx_ref, q_ref, *refs):
    parts, (out_ref, lse_ref, k_few, v_few, k_ref, v_ref) = refs[:2 * t], refs[2 * t:]
    row = pl.program_id(0)
    q = q_ref[0, 0]

    @pl.when(row == 0)
    def _():
        join_parts(parts, k_ref, v_ref)

    def finish(s, v):
        top = jnp.max(s, axis=1, keepdims=True)
        p = jnp.exp2(s - top)
        mass = jnp.sum(p, axis=1, keepdims=True)
        out = dot(p.astype(BF16), v)
        out_ref[0, 0] = (out / mass).astype(BF16)
        lse_ref[...] = jnp.broadcast_to(top + jnp.log2(mass), lse_ref.shape)

    scale = HEAD ** -0.5 * LOG2E

    @pl.when(full_ref[row] == 1)
    def _():
        keys = k_ref[...].reshape(-1, HEAD)
        finish(dot(q, keys, NT) * scale, v_ref[...].reshape(-1, HEAD))

    @pl.when(full_ref[row] == 0)
    def _():
        gather_tiles(k_ref, kidx_ref, row, k_few, tile, count)
        gather_tiles(v_ref, kidx_ref, row, v_few, tile, count)
        s = dot(q, k_few[...], NT) * scale
        column = lax.broadcasted_iota(jnp.int32, s.shape, 1)
        s = jnp.where(column < kcnt_ref[row] * tile, s, NEG_BIG)
        finish(s, v_few[...])


def backward_kernel(t, tile, count, full_ref, kcnt_ref, kidx_ref, q_ref, g_ref, o_ref, lse_ref, *refs):
    parts, (dq_ref, dkv_ref, k_few, v_few, k_ref, v_ref, dk_acc, dv_acc) = refs[:2 * t], refs[2 * t:]
    row = pl.program_id(0)
    last = pl.num_programs(0) - 1

    @pl.when(row == 0)
    def _():
        join_parts(parts, k_ref, v_ref)
        dk_acc[...] = jnp.zeros_like(dk_acc)
        dv_acc[...] = jnp.zeros_like(dv_acc)

    q = q_ref[0, 0]
    g = g_ref[0, 0]
    delta = jnp.sum(g.astype(F32) * o_ref[0, 0].astype(F32), axis=1, keepdims=True)
    lse = lse_ref[:, :1]
    unit = HEAD ** -0.5
    scale = unit * LOG2E

    def gradients(keys, values, mask):
        s = dot(q, keys, NT)
        p = jnp.exp2(s * scale - lse)
        if mask is not None:
            p = jnp.where(mask(p.shape), p, 0.0)
        ds = (p * (dot(g, values, NT) - delta)).astype(BF16)
        dq_ref[0, 0] = (dot(ds, keys) * unit).astype(BF16)
        return dot(ds, q, TN) * unit, dot(p.astype(BF16), g, TN)

    @pl.when(full_ref[row] == 1)
    def _():
        dk, dv = gradients(k_ref[...].reshape(-1, HEAD), v_ref[...].reshape(-1, HEAD), None)
        dk_acc[...] += dk.reshape(dk_acc.shape)
        dv_acc[...] += dv.reshape(dv_acc.shape)

    @pl.when(full_ref[row] == 0)
    def _():
        gather_tiles(k_ref, kidx_ref, row, k_few, tile, count)
        gather_tiles(v_ref, kidx_ref, row, v_few, tile, count)

        def mask(shape):
            return lax.broadcasted_iota(jnp.int32, shape, 1) < kcnt_ref[row] * tile

        dk, dv = gradients(k_few[...], v_few[...], mask)
        for j in range(count):
            at = kidx_ref[row, j]
            dk_acc[at] += dk[j * tile:(j + 1) * tile]
            dv_acc[at] += dv[j * tile:(j + 1) * tile]

    @pl.when(row == last)
    def _():
        parts, _, chunks, rows, _ = dkv_ref.shape
        shape = (parts, chunks, rows, HEAD)
        dkv_ref[:, 0] = dk_acc[...].reshape(shape).astype(BF16)
        dkv_ref[:, 1] = dv_acc[...].reshape(shape).astype(BF16)


def whole_block(shape):
    return pl.BlockSpec(shape, lambda *_: (0,) * len(shape))


def one_array(which, n, sub):
    return pl.BlockSpec((n, 1, sub, HEAD), lambda *_: (0, which, 0, 0))


def tile_block(which, per_chunk, tile):
    return pl.BlockSpec(
        (1, 1, tile, HEAD), lambda r, *_: (r // per_chunk, which, r % per_chunk, 0)
    )


def shifts(t, s):
    return [(c, (c + s) % t) for c in range(t)]


def per_device(n, t, queries, key_vectors, value_vectors, out_weight, out_grad, block_segment):
    rows, width = queries.shape
    heads_here = width // HEAD
    heads = heads_here * t
    sub = rows // t
    tile = min(sub, BLK)
    per_chunk = sub // tile
    core = lax.axis_index("tp")
    chip = lax.axis_index("ctx")
    in_plane = n // PLANES
    heads_plane = heads // PLANES
    seat = chip % in_plane

    def tp_swap(pick):
        got = [pick(core)]
        for s in range(1, t):
            got.append(lax.ppermute(pick((core + s) % t), "tp", shifts(t, s)))
        return [lax.select_n((core - p) % t, *got) for p in range(t)]

    def tp_gather(x):
        return tp_swap(lambda _: x)

    def tp_split(pack):
        return tp_swap(lambda p: lax.dynamic_index_in_dim(pack, p, 0, False))

    def plane_swap(pick):
        got = [pick(seat)]
        for k in range(1, in_plane):
            got.append(lax.ppermute(pick(seat ^ k), "ctx", [(i, i ^ k) for i in range(n)]))
        return [lax.select_n(seat ^ b, *got) for b in range(in_plane)]

    def to_heads(arrays):
        pack = jnp.stack(
            [a.reshape(t, sub, heads_here, HEAD).transpose(0, 2, 1, 3) for a in arrays], axis=2
        )
        every = jnp.concatenate(tp_split(pack), axis=0)
        every = every.reshape((PLANES, heads_plane) + every.shape[1:])
        spare = in_plane - heads_plane
        sent = jnp.pad(every, ((0, 0), (0, spare), (0, 0), (0, 0), (0, 0)))
        return lax.all_to_all(sent.reshape((n,) + every.shape[2:]), "ctx", 0, 0, tiled=True)

    def to_tokens(pack):
        got = lax.all_to_all(pack, "ctx", 0, 0, tiled=True)
        every = got.reshape((PLANES, in_plane) + got.shape[1:])[:, :heads_plane]
        mine = jnp.stack(tp_split(every.reshape((t, heads_here) + got.shape[1:])))
        return [
            mine[:, :, a].transpose(0, 2, 1, 3).reshape(rows, width) for a in range(pack.shape[1])
        ]

    chunk_row = jnp.arange(n)[:, None] * rows + jnp.arange(per_chunk)[None, :] * tile

    def tile_segments(part):
        return jnp.take(block_segment, ((chunk_row + part * sub) // BLK).reshape(-1))

    seg_parts = [tile_segments((core - s) % t) for s in range(t)]
    seg_q = seg_parts[0]
    seg_k = jnp.concatenate(seg_parts)
    full = (seg_q == 0) | (seg_q == TARGET)
    permitted = (seg_k[None] == 0) | (seg_k[None] == seg_q[:, None])
    total_blocks = block_segment.shape[0]
    count = (TXT_BLK + -(-(total_blocks - TXT_BLK) // RUNS)) * (BLK // tile)
    kcnt = jnp.sum(permitted.astype(jnp.int32), axis=1)
    tiles_k = seg_k.shape[0]
    ids = jnp.arange(tiles_k)
    place = jnp.sum((permitted[:, None, :] & (ids[None, None, :] < ids[None, :, None])).astype(jnp.int32), axis=2)
    hit = permitted[:, None, :] & (place[:, None, :] == jnp.arange(count)[None, :, None])
    kidx = jnp.sum(jnp.where(hit, ids[None, None, :], 0), axis=2).astype(jnp.int32)
    full = full.astype(jnp.int32)

    qkv = to_heads([queries, key_vectors, value_vectors])

    half = out_grad.shape[1]
    model = half * t
    full_grad = jnp.concatenate(tp_gather(out_grad), axis=1)
    grad_attn = dot(full_grad, out_weight, NT).astype(BF16)
    g_heads = to_heads([grad_attn])

    cols = model // in_plane
    mine = lax.dynamic_slice_in_dim(full_grad, core * sub, sub, 0)
    plane_grad = jnp.stack(
        plane_swap(lambda b: lax.dynamic_slice_in_dim(mine, b * cols, cols, 1))
    )
    lines = [[a * in_plane + b for a in range(PLANES)] for b in range(in_plane)]
    slice_grad = lax.all_gather(plane_grad, "ctx", axis_index_groups=lines)
    slice_grad = slice_grad.reshape(n * sub, cols)

    others = [lax.ppermute(qkv, "tp", shifts(t, s)) for s in range(1, t)]

    tiles_q = n * per_chunk
    few = [pltpu.VMEM((count * tile, HEAD), BF16)] * 2 + [pltpu.VMEM((tiles_k, tile, HEAD), BF16)] * 2
    params = pltpu.CompilerParams(vmem_limit_bytes=48 * 2**20)
    q_block = tile_block(0, per_chunk, tile)
    part_blocks = [one_array(1, n, sub), one_array(2, n, sub)] * t
    part_arrays = [a for pack in [qkv] + others for a in (pack, pack)]
    lse_block = pl.BlockSpec((tile, HEAD), lambda r, *_: (r, 0))
    attn, lse = pl.pallas_call(
        functools.partial(forward_kernel, t, tile, count),
        grid_spec=pltpu.PrefetchScalarGridSpec(
            num_scalar_prefetch=3,
            grid=(tiles_q,),
            in_specs=[q_block] + part_blocks,
            out_specs=[q_block, lse_block],
            scratch_shapes=few,
        ),
        out_shape=[
            jax.ShapeDtypeStruct((n, 1, sub, HEAD), BF16),
            jax.ShapeDtypeStruct((tiles_q * tile, HEAD), F32),
        ],
        compiler_params=params,
        cost_estimate=pl.CostEstimate(
            flops=tiles_q * tile * tiles_k * tile * HEAD * 2, bytes_accessed=5 * 2**20, transcendentals=2**22
        ),
        name="forward",
    )(full, kcnt, kidx, qkv, *part_arrays)

    plane_attn = plane_swap(lambda _: attn)[:heads_plane]
    plane_attn = jnp.stack([a.reshape(n * sub, HEAD) for a in plane_attn])
    tile_term = jnp.einsum("hrd,rc->hdc", plane_attn, slice_grad, preferred_element_type=F32)
    tile_rows = heads_plane * HEAD
    piece = tile_rows // t
    tile_term = tile_term.reshape(t, piece, cols)
    tile_sum = lax.dynamic_index_in_dim(tile_term, core, 0, False)
    for s in range(1, t):
        there = lax.dynamic_index_in_dim(tile_term, (core + s) % t, 0, False)
        tile_sum = tile_sum + lax.ppermute(there.astype(BF16), "tp", shifts(t, s)).astype(F32)
    tiles = lax.all_gather(tile_sum.astype(BF16), "ctx")
    planes_here = PLANES // t
    tiles = jnp.stack(tp_split(tiles.reshape(t, planes_here, in_plane, piece, cols)))
    grad_weight = tiles.transpose(1, 0, 3, 2, 4).reshape(width, model).astype(F32)

    (attention,) = to_tokens(attn)
    projected = dot(attention, out_weight)
    own = lax.dynamic_slice_in_dim(projected, core * half, half, 1)
    for s in range(1, t):
        there = lax.dynamic_slice_in_dim(projected, (core + s) % t * half, half, 1)
        own = own + lax.ppermute(there.astype(BF16), "tp", shifts(t, s)).astype(F32)
    attention_out = own.astype(BF16)

    dq, dkv = pl.pallas_call(
        functools.partial(backward_kernel, t, tile, count),
        grid_spec=pltpu.PrefetchScalarGridSpec(
            num_scalar_prefetch=3,
            grid=(tiles_q,),
            in_specs=[q_block, q_block, q_block, lse_block] + part_blocks,
            out_specs=[q_block, whole_block((t, 2, n, sub, HEAD))],
            scratch_shapes=few + [pltpu.VMEM((tiles_k, tile, HEAD), F32)] * 2,
        ),
        out_shape=[
            jax.ShapeDtypeStruct((n, 1, sub, HEAD), BF16),
            jax.ShapeDtypeStruct((t, 2, n, sub, HEAD), BF16),
        ],
        compiler_params=params,
        cost_estimate=pl.CostEstimate(
            flops=tiles_q * tile * tiles_k * tile * HEAD * 5, bytes_accessed=8 * 2**20, transcendentals=2**22
        ),
        name="backward",
    )(full, kcnt, kidx, qkv, g_heads, attn, lse, *part_arrays)

    sums = dkv[0].astype(F32)
    for s in range(1, t):
        back = [(c, (c - s) % t) for c in range(t)]
        sums = sums + lax.ppermute(dkv[s], "tp", back).astype(F32)
    sums = sums.astype(BF16).transpose(1, 0, 2, 3)
    grad_queries, grad_keys, grad_values = to_tokens(jnp.concatenate([dq, sums], axis=1))
    return attention_out, grad_queries, grad_keys, grad_values, grad_weight


def solution(mesh):
    n, t = mesh.shape["ctx"], mesh.shape["tp"]
    in_specs = (P("ctx", "tp"), P("ctx", "tp"), P("ctx", "tp"), P("tp", None), P("ctx", "tp"), P())
    out_specs = (P("ctx", "tp"), P("ctx", "tp"), P("ctx", "tp"), P("ctx", "tp"), P("tp", None))
    return jax.shard_map(
        functools.partial(per_device, n, t), mesh=mesh, in_specs=in_specs, out_specs=out_specs, check_vma=False
    )
```

```python
import functools
import math

import jax
import jax.numpy as jnp
from jax import lax
from jax.experimental import pallas as pl
from jax.experimental.pallas import tpu as pltpu
from jax.sharding import PartitionSpec as P

HEAD = 128
BLK = 128
TXT_BLK = 4
RUNS = 5
TARGET = 5
PLANES = 4
LOG2E = math.log2(math.e)
NEG_BIG = -1e30

NT = (((1,), (1,)), ((), ()))
TN = (((0,), (0,)), ((), ()))
F32 = jnp.float32
BF16 = jnp.bfloat16


def dot(a, b, dims=(((1,), (0,)), ((), ()))):
    return lax.dot_general(a, b, dims, preferred_element_type=F32)


def gather_tiles(k_ref, kidx_ref, row, dst, tile, count):
    for j in range(count):
        dst[pl.ds(j * tile, tile), :] = k_ref[kidx_ref[row, j]]


def join_parts(parts, k_all, v_all):
    shape = (k_all.shape[0] // (len(parts) // 2),) + k_all.shape[1:]
    for s in range(len(parts) // 2):
        at = pl.ds(s * shape[0], shape[0])
        k_all[at] = parts[2 * s][...].reshape(shape)
        v_all[at] = parts[2 * s + 1][...].reshape(shape)


def forward_kernel(t, tile, count, full_ref, kcnt_ref, kidx_ref, q_ref, *refs):
    parts, (out_ref, lse_ref, k_few, v_few, k_ref, v_ref) = refs[:2 * t], refs[2 * t:]
    row = pl.program_id(0)
    q = q_ref[0, 0]

    @pl.when(row == 0)
    def _():
        join_parts(parts, k_ref, v_ref)

    def finish(s, v):
        top = jnp.max(s, axis=1, keepdims=True)
        p = jnp.exp2(s - top)
        mass = jnp.sum(p, axis=1, keepdims=True)
        out = dot(p.astype(BF16), v)
        out_ref[0, 0] = (out / mass).astype(BF16)
        lse_ref[...] = jnp.broadcast_to(top + jnp.log2(mass), lse_ref.shape)

    scale = HEAD ** -0.5 * LOG2E

    @pl.when(full_ref[row] == 1)
    def _():
        keys = k_ref[...].reshape(-1, HEAD)
        finish(dot(q, keys, NT) * scale, v_ref[...].reshape(-1, HEAD))

    @pl.when(full_ref[row] == 0)
    def _():
        gather_tiles(k_ref, kidx_ref, row, k_few, tile, count)
        gather_tiles(v_ref, kidx_ref, row, v_few, tile, count)
        s = dot(q, k_few[...], NT) * scale
        column = lax.broadcasted_iota(jnp.int32, s.shape, 1)
        s = jnp.where(column < kcnt_ref[row] * tile, s, NEG_BIG)
        finish(s, v_few[...])


def backward_kernel(t, tile, count, full_ref, kcnt_ref, kidx_ref, q_ref, g_ref, o_ref, lse_ref, *refs):
    parts, (dq_ref, dkv_ref, k_few, v_few, k_ref, v_ref, dk_acc, dv_acc) = refs[:2 * t], refs[2 * t:]
    row = pl.program_id(0)
    last = pl.num_programs(0) - 1

    @pl.when(row == 0)
    def _():
        join_parts(parts, k_ref, v_ref)
        dk_acc[...] = jnp.zeros_like(dk_acc)
        dv_acc[...] = jnp.zeros_like(dv_acc)

    q = q_ref[0, 0]
    g = g_ref[0, 0]
    delta = jnp.sum(g.astype(F32) * o_ref[0, 0].astype(F32), axis=1, keepdims=True)
    lse = lse_ref[:, :1]
    unit = HEAD ** -0.5
    scale = unit * LOG2E

    def gradients(keys, values, mask):
        s = dot(q, keys, NT)
        p = jnp.exp2(s * scale - lse)
        if mask is not None:
            p = jnp.where(mask(p.shape), p, 0.0)
        ds = (p * (dot(g, values, NT) - delta)).astype(BF16)
        dq_ref[0, 0] = (dot(ds, keys) * unit).astype(BF16)
        return dot(ds, q, TN) * unit, dot(p.astype(BF16), g, TN)

    @pl.when(full_ref[row] == 1)
    def _():
        dk, dv = gradients(k_ref[...].reshape(-1, HEAD), v_ref[...].reshape(-1, HEAD), None)
        dk_acc[...] += dk.reshape(dk_acc.shape)
        dv_acc[...] += dv.reshape(dv_acc.shape)

    @pl.when(full_ref[row] == 0)
    def _():
        gather_tiles(k_ref, kidx_ref, row, k_few, tile, count)
        gather_tiles(v_ref, kidx_ref, row, v_few, tile, count)

        def mask(shape):
            return lax.broadcasted_iota(jnp.int32, shape, 1) < kcnt_ref[row] * tile

        dk, dv = gradients(k_few[...], v_few[...], mask)
        for j in range(count):
            at = kidx_ref[row, j]
            dk_acc[at] += dk[j * tile:(j + 1) * tile]
            dv_acc[at] += dv[j * tile:(j + 1) * tile]

    @pl.when(row == last)
    def _():
        parts, _, chunks, rows, _ = dkv_ref.shape
        shape = (parts, chunks, rows, HEAD)
        dkv_ref[:, 0] = dk_acc[...].reshape(shape).astype(BF16)
        dkv_ref[:, 1] = dv_acc[...].reshape(shape).astype(BF16)


def whole_block(shape):
    return pl.BlockSpec(shape, lambda *_: (0,) * len(shape))


def one_array(which, n, sub):
    return pl.BlockSpec((n, 1, sub, HEAD), lambda *_: (0, which, 0, 0))


def tile_block(which, per_chunk, tile):
    return pl.BlockSpec(
        (1, 1, tile, HEAD), lambda r, *_: (r // per_chunk, which, r % per_chunk, 0)
    )


def shifts(t, s):
    return [(c, (c + s) % t) for c in range(t)]


def place_kernel(place_ref, *refs):
    sources, out_ref = refs[:-1], refs[-1]
    step = pl.program_id(0)
    for u in range(2):
        own, beside, above, upper, lower = sources[5 * u:5 * u + 5]
        for v, source in enumerate((own, beside, above)):
            @pl.when(step == 4 * u + v)
            def _(source=source):
                out_ref[...] = source[...].astype(F32)

        @pl.when(step == 4 * u + 3)
        def _(upper=upper, lower=lower):
            middle = upper.shape[0]
            out_ref[:middle] = upper[...].astype(F32)
            out_ref[middle:] = lower[...].astype(F32)


def gather_tiles_by_core(n, t, tile_sum, chip, core):
    in_plane = n // PLANES
    plane, seat = chip // in_plane, chip % in_plane
    tile_rows, cols = tile_sum.shape
    across = [
        (i * t + c, (i ^ 2 * in_plane) * t + c)
        for i in range(n) for c in range(t) if i // in_plane // 2 == c
    ]
    from_half = lax.ppermute(tile_sum, ("ctx", "tp"), across)

    def swap(x, k):
        return lax.ppermute(x, "ctx", [(i, i ^ k) for i in range(n)])

    first = jnp.where(plane // 2 == core, tile_sum, from_half)
    second = swap(first, in_plane)
    middle = tile_rows // 2
    sources = []
    for mine in (first, second):
        beside, above = swap(mine, 1), swap(mine, 2)
        sources += [mine, beside, above, swap(beside[:middle], 2), swap(above[middle:], 1)]
    place = jnp.stack([plane % 2, seat]).astype(jnp.int32)
    return pl.pallas_call(
        place_kernel,
        grid_spec=pltpu.PrefetchScalarGridSpec(
            num_scalar_prefetch=1,
            grid=(8,),
            in_specs=[whole_block(x.shape) for x in sources],
            out_specs=pl.BlockSpec(
                (tile_rows, cols), lambda s, place: (s // 4 ^ place[0], s % 4 ^ place[1])
            ),
        ),
        out_shape=jax.ShapeDtypeStruct((2 * tile_rows, in_plane * cols), F32),
        compiler_params=pltpu.CompilerParams(vmem_limit_bytes=48 * 2**20),
        name="place",
    )(place, *sources)


def per_device(n, t, queries, key_vectors, value_vectors, out_weight, out_grad, block_segment):
    rows, width = queries.shape
    heads_here = width // HEAD
    heads = heads_here * t
    sub = rows // t
    tile = min(sub, BLK)
    per_chunk = sub // tile
    core = lax.axis_index("tp")
    chip = lax.axis_index("ctx")
    in_plane = n // PLANES
    heads_plane = heads // PLANES
    seat = chip % in_plane

    def tp_swap(pick):
        got = [pick(core)]
        for s in range(1, t):
            got.append(lax.ppermute(pick((core + s) % t), "tp", shifts(t, s)))
        return [lax.select_n((core - p) % t, *got) for p in range(t)]

    def tp_gather(x):
        return tp_swap(lambda _: x)

    def tp_split(pack):
        return tp_swap(lambda p: lax.dynamic_index_in_dim(pack, p, 0, False))

    def plane_swap(pick):
        got = [pick(seat)]
        for k in range(1, in_plane):
            got.append(lax.ppermute(pick(seat ^ k), "ctx", [(i, i ^ k) for i in range(n)]))
        return [lax.select_n(seat ^ b, *got) for b in range(in_plane)]

    def to_heads(arrays):
        pack = jnp.stack(
            [a.reshape(t, sub, heads_here, HEAD).transpose(0, 2, 1, 3) for a in arrays], axis=2
        )
        every = jnp.concatenate(tp_split(pack), axis=0)
        every = every.reshape((PLANES, heads_plane) + every.shape[1:])
        spare = in_plane - heads_plane
        sent = jnp.pad(every, ((0, 0), (0, spare), (0, 0), (0, 0), (0, 0)))
        return lax.all_to_all(sent.reshape((n,) + every.shape[2:]), "ctx", 0, 0, tiled=True)

    def to_tokens(pack):
        got = lax.all_to_all(pack, "ctx", 0, 0, tiled=True)
        every = got.reshape((PLANES, in_plane) + got.shape[1:])[:, :heads_plane]
        mine = jnp.stack(tp_split(every.reshape((t, heads_here) + got.shape[1:])))
        return [
            mine[:, :, a].transpose(0, 2, 1, 3).reshape(rows, width) for a in range(pack.shape[1])
        ]

    chunk_row = jnp.arange(n)[:, None] * rows + jnp.arange(per_chunk)[None, :] * tile

    def tile_segments(part):
        return jnp.take(block_segment, ((chunk_row + part * sub) // BLK).reshape(-1))

    seg_parts = [tile_segments((core - s) % t) for s in range(t)]
    seg_q = seg_parts[0]
    seg_k = jnp.concatenate(seg_parts)
    full = (seg_q == 0) | (seg_q == TARGET)
    permitted = (seg_k[None] == 0) | (seg_k[None] == seg_q[:, None])
    total_blocks = block_segment.shape[0]
    count = (TXT_BLK + -(-(total_blocks - TXT_BLK) // RUNS)) * (BLK // tile)
    kcnt = jnp.sum(permitted.astype(jnp.int32), axis=1)
    tiles_k = seg_k.shape[0]
    ids = jnp.arange(tiles_k)
    place = jnp.sum((permitted[:, None, :] & (ids[None, None, :] < ids[None, :, None])).astype(jnp.int32), axis=2)
    hit = permitted[:, None, :] & (place[:, None, :] == jnp.arange(count)[None, :, None])
    kidx = jnp.sum(jnp.where(hit, ids[None, None, :], 0), axis=2).astype(jnp.int32)
    full = full.astype(jnp.int32)

    qkv = to_heads([queries, key_vectors, value_vectors])

    half = out_grad.shape[1]
    model = half * t
    full_grad = jnp.concatenate(tp_gather(out_grad), axis=1)
    grad_attn = dot(full_grad, out_weight, NT).astype(BF16)
    g_heads = to_heads([grad_attn])

    cols = model // in_plane
    mine = lax.dynamic_slice_in_dim(full_grad, core * sub, sub, 0)
    plane_grad = jnp.stack(
        plane_swap(lambda b: lax.dynamic_slice_in_dim(mine, b * cols, cols, 1))
    )
    lines = [[a * in_plane + b for a in range(PLANES)] for b in range(in_plane)]
    slice_grad = lax.all_gather(plane_grad, "ctx", axis_index_groups=lines)
    slice_grad = slice_grad.reshape(n * sub, cols)

    others = [lax.ppermute(qkv, "tp", shifts(t, s)) for s in range(1, t)]

    tiles_q = n * per_chunk
    few = [pltpu.VMEM((count * tile, HEAD), BF16)] * 2 + [pltpu.VMEM((tiles_k, tile, HEAD), BF16)] * 2
    params = pltpu.CompilerParams(vmem_limit_bytes=48 * 2**20)
    q_block = tile_block(0, per_chunk, tile)
    part_blocks = [one_array(1, n, sub), one_array(2, n, sub)] * t
    part_arrays = [a for pack in [qkv] + others for a in (pack, pack)]
    lse_block = pl.BlockSpec((tile, HEAD), lambda r, *_: (r, 0))
    attn, lse = pl.pallas_call(
        functools.partial(forward_kernel, t, tile, count),
        grid_spec=pltpu.PrefetchScalarGridSpec(
            num_scalar_prefetch=3,
            grid=(tiles_q,),
            in_specs=[q_block] + part_blocks,
            out_specs=[q_block, lse_block],
            scratch_shapes=few,
        ),
        out_shape=[
            jax.ShapeDtypeStruct((n, 1, sub, HEAD), BF16),
            jax.ShapeDtypeStruct((tiles_q * tile, HEAD), F32),
        ],
        compiler_params=params,
        cost_estimate=pl.CostEstimate(
            flops=16 * 10**9, bytes_accessed=5 * 2**20, transcendentals=2**22
        ),
        name="forward",
    )(full, kcnt, kidx, qkv, *part_arrays)

    got_attn = plane_swap(lambda _: attn)[:heads_plane]

    dq, dkv = pl.pallas_call(
        functools.partial(backward_kernel, t, tile, count),
        grid_spec=pltpu.PrefetchScalarGridSpec(
            num_scalar_prefetch=3,
            grid=(tiles_q,),
            in_specs=[q_block, q_block, q_block, lse_block] + part_blocks,
            out_specs=[q_block, whole_block((t, 2, n, sub, HEAD))],
            scratch_shapes=few + [pltpu.VMEM((tiles_k, tile, HEAD), F32)] * 2,
        ),
        out_shape=[
            jax.ShapeDtypeStruct((n, 1, sub, HEAD), BF16),
            jax.ShapeDtypeStruct((t, 2, n, sub, HEAD), BF16),
        ],
        compiler_params=params,
        cost_estimate=pl.CostEstimate(
            flops=20 * 10**9, bytes_accessed=8 * 2**20, transcendentals=2**22
        ),
        name="backward",
    )(full, kcnt, kidx, qkv, g_heads, attn, lse, *part_arrays)

    got_attn, dq, dkv = lax.optimization_barrier((got_attn, dq, dkv))

    plane_attn = jnp.stack([a.reshape(n * sub, HEAD) for a in got_attn])
    tile_term = jnp.einsum("hrd,rc->hdc", plane_attn, slice_grad, preferred_element_type=F32)
    tile_term = tile_term.reshape(heads_plane * HEAD, cols)
    tile_rows = heads_plane * HEAD
    planes_here = PLANES // t
    if in_plane == 4 and t == 2:
        tile_sum = tile_term
        for s in range(1, t):
            tile_sum = tile_sum + lax.ppermute(tile_term.astype(BF16), "tp", shifts(t, s)).astype(F32)
        grad_weight = gather_tiles_by_core(n, t, tile_sum.astype(BF16), chip, core)
    else:
        piece = tile_rows // t
        tile_term = tile_term.reshape(t, piece, cols)
        tile_sum = lax.dynamic_index_in_dim(tile_term, core, 0, False)
        for s in range(1, t):
            there = lax.dynamic_index_in_dim(tile_term, (core + s) % t, 0, False)
            tile_sum = tile_sum + lax.ppermute(there.astype(BF16), "tp", shifts(t, s)).astype(F32)
        tiles = lax.all_gather(tile_sum.astype(BF16), "ctx")
        tiles = jnp.stack(tp_split(tiles.reshape(t, planes_here, in_plane, piece, cols)))
        grad_weight = tiles.transpose(1, 0, 3, 2, 4).reshape(width, model).astype(F32)

    (attention,) = to_tokens(attn)
    projected = dot(attention, out_weight)
    own = lax.dynamic_slice_in_dim(projected, core * half, half, 1)
    for s in range(1, t):
        there = lax.dynamic_slice_in_dim(projected, (core + s) % t * half, half, 1)
        own = own + lax.ppermute(there.astype(BF16), "tp", shifts(t, s)).astype(F32)
    attention_out = own.astype(BF16)

    sums = dkv[0].astype(F32)
    for s in range(1, t):
        back = [(c, (c - s) % t) for c in range(t)]
        sums = sums + lax.ppermute(dkv[s], "tp", back).astype(F32)
    sums = sums.astype(BF16).transpose(1, 0, 2, 3)
    grad_queries, grad_keys, grad_values = to_tokens(jnp.concatenate([dq, sums], axis=1))
    return attention_out, grad_queries, grad_keys, grad_values, grad_weight


def solution(mesh):
    n, t = mesh.shape["ctx"], mesh.shape["tp"]
    in_specs = (P("ctx", "tp"), P("ctx", "tp"), P("ctx", "tp"), P("tp", None), P("ctx", "tp"), P())
    out_specs = (P("ctx", "tp"), P("ctx", "tp"), P("ctx", "tp"), P("ctx", "tp"), P("tp", None))
    return jax.shard_map(
        functools.partial(per_device, n, t), mesh=mesh, in_specs=in_specs, out_specs=out_specs, check_vma=False
    )
```

```python
import functools
import math

import jax
import jax.numpy as jnp
from jax import lax
from jax.experimental import pallas as pl
from jax.experimental.pallas import tpu as pltpu
from jax.sharding import PartitionSpec as P

HEAD = 128
BLK = 128
TXT_BLK = 4
RUNS = 5
TARGET = 5
PLANES = 4
LOG2E = math.log2(math.e)
NEG_BIG = -1e30

NT = (((1,), (1,)), ((), ()))
TN = (((0,), (0,)), ((), ()))
F32 = jnp.float32
BF16 = jnp.bfloat16


def dot(a, b, dims=(((1,), (0,)), ((), ()))):
    return lax.dot_general(a, b, dims, preferred_element_type=F32)


def gather_tiles(k_ref, kidx_ref, row, dst, tile, count):
    for j in range(count):
        dst[pl.ds(j * tile, tile), :] = k_ref[kidx_ref[row, j]]


def join_parts(parts, k_all, v_all):
    shape = (k_all.shape[0] // (len(parts) // 2),) + k_all.shape[1:]
    for s in range(len(parts) // 2):
        at = pl.ds(s * shape[0], shape[0])
        k_all[at] = parts[2 * s][...].reshape(shape)
        v_all[at] = parts[2 * s + 1][...].reshape(shape)


def head_of(chip, in_plane, heads_plane):
    place = (chip % in_plane + in_plane - chip // in_plane % in_plane) % in_plane
    return place < heads_plane, chip // in_plane * heads_plane + jnp.minimum(place, heads_plane - 1)


def pack_kernel(n, t, where_ref, *refs):
    arrays, got, outs, heads_all = refs[:4], refs[4:4 + 2 * (t - 1)], refs[4 + 2 * (t - 1):-1], refs[-1]
    chip, core = where_ref[0], where_ref[1]
    sub = heads_all.shape[2]
    heads_here = heads_all.shape[0] // t
    for a in range(4):
        for h in range(heads_here):
            column = pl.ds(h * HEAD, HEAD)
            heads_all[core * heads_here + h, a] = arrays[a][pl.ds(core * sub, sub), column]
            for s in range(1, t):
                first = (core + t - s) % t * heads_here
                source = got[2 * (s - 1)] if a < 3 else got[2 * (s - 1) + 1]
                heads_all[first + h, a] = source[a % 3, :, column]
    for k in range(n):
        _, head = head_of(chip ^ k, n // PLANES, heads_all.shape[0] // PLANES)
        outs[k][...] = heads_all[head]


def join_kernel(n, where_ref, *refs):
    chunks, (qg_ref, kv_ref) = refs[:n], refs[n:]
    chip = where_ref[0]
    for k in range(n):
        sub = chunks[k].shape[1]
        at = pl.ds(pl.multiple_of((chip ^ k) * sub, sub), sub)
        qg_ref[0, at] = chunks[k][0]
        kv_ref[0, at] = chunks[k][1]
        kv_ref[1, at] = chunks[k][2]
        qg_ref[1, at] = chunks[k][3]


def unjoin_kernel(n, t, where_ref, attn_ref, dq_ref, dkv_ref, *refs):
    got, outs = refs[:t - 1], refs[t - 1:]
    chip = where_ref[0]
    for k in range(n):
        sub = outs[k].shape[1]
        at = pl.ds(pl.multiple_of((chip ^ k) * sub, sub), sub)
        outs[k][0] = attn_ref[at]
        outs[k][1] = dq_ref[at]
        for a in range(2):
            total = dkv_ref[a, at].astype(F32)
            for other in got:
                total = total + other[a, at].astype(F32)
            outs[k][2 + a] = total.astype(BF16)


def by_core_kernel(n, t, where_ref, *refs):
    chunks, outs, heads_all = refs[:n], refs[n:n + t], refs[-1]
    chip, core = where_ref[0], where_ref[1]
    heads_here = heads_all.shape[0] // t
    for k in range(n):
        held, head = head_of(chip ^ k, n // PLANES, heads_all.shape[0] // PLANES)

        @pl.when(held)
        def _(k=k, head=head):
            heads_all[head] = chunks[k][...]
    for s in range(t):
        outs[s][...] = heads_all[pl.ds((core + s) % t * heads_here, heads_here)]


def unpack_kernel(t, where_ref, *refs):
    parts, outs = refs[:t], refs[t:]
    core = where_ref[1]
    heads_here, _, sub, _ = parts[0].shape
    for s in range(t):
        at = pl.ds(pl.multiple_of((core + t - s) % t * sub, sub), sub)
        for a in range(4):
            for h in range(heads_here):
                outs[a][at, pl.ds(h * HEAD, HEAD)] = parts[s][h, a]


def forward_kernel(t, tile, count, full_ref, kcnt_ref, kidx_ref, q_ref, *refs):
    parts, (out_ref, lse_ref, k_few, v_few, k_ref, v_ref) = refs[:2 * t], refs[2 * t:]
    row = pl.program_id(0)
    q = q_ref[0]

    @pl.when(row == 0)
    def _():
        join_parts(parts, k_ref, v_ref)

    def finish(s, v):
        top = jnp.max(s, axis=1, keepdims=True)
        p = jnp.exp2(s - top)
        mass = jnp.sum(p, axis=1, keepdims=True)
        out = dot(p.astype(BF16), v)
        out_ref[...] = (out / mass).astype(BF16)
        lse_ref[...] = jnp.broadcast_to(top + jnp.log2(mass), lse_ref.shape)

    scale = HEAD ** -0.5 * LOG2E

    @pl.when(full_ref[row] == 1)
    def _():
        keys = k_ref[...].reshape(-1, HEAD)
        finish(dot(q, keys, NT) * scale, v_ref[...].reshape(-1, HEAD))

    @pl.when(full_ref[row] == 0)
    def _():
        gather_tiles(k_ref, kidx_ref, row, k_few, tile, count)
        gather_tiles(v_ref, kidx_ref, row, v_few, tile, count)
        s = dot(q, k_few[...], NT) * scale
        column = lax.broadcasted_iota(jnp.int32, s.shape, 1)
        s = jnp.where(column < kcnt_ref[row] * tile, s, NEG_BIG)
        finish(s, v_few[...])


def backward_kernel(t, tile, count, full_ref, kcnt_ref, kidx_ref, q_ref, g_ref, o_ref, lse_ref, *refs):
    parts, dkv_refs = refs[:2 * t], refs[2 * t + 1:3 * t + 1]
    dq_ref = refs[2 * t]
    k_few, v_few, k_ref, v_ref, dk_acc, dv_acc = refs[3 * t + 1:]
    row = pl.program_id(0)
    last = pl.num_programs(0) - 1

    @pl.when(row == 0)
    def _():
        join_parts(parts, k_ref, v_ref)
        dk_acc[...] = jnp.zeros_like(dk_acc)
        dv_acc[...] = jnp.zeros_like(dv_acc)

    q = q_ref[0]
    g = g_ref[0]
    delta = jnp.sum(g.astype(F32) * o_ref[...].astype(F32), axis=1, keepdims=True)
    lse = lse_ref[:, :1]
    unit = HEAD ** -0.5
    scale = unit * LOG2E

    def gradients(keys, values, mask):
        s = dot(q, keys, NT)
        p = jnp.exp2(s * scale - lse)
        if mask is not None:
            p = jnp.where(mask(p.shape), p, 0.0)
        ds = (p * (dot(g, values, NT) - delta)).astype(BF16)
        dq_ref[...] = (dot(ds, keys) * unit).astype(BF16)
        return dot(ds, q, TN) * unit, dot(p.astype(BF16), g, TN)

    @pl.when(full_ref[row] == 1)
    def _():
        dk, dv = gradients(k_ref[...].reshape(-1, HEAD), v_ref[...].reshape(-1, HEAD), None)
        dk_acc[...] += dk.reshape(dk_acc.shape)
        dv_acc[...] += dv.reshape(dv_acc.shape)

    @pl.when(full_ref[row] == 0)
    def _():
        gather_tiles(k_ref, kidx_ref, row, k_few, tile, count)
        gather_tiles(v_ref, kidx_ref, row, v_few, tile, count)

        def mask(shape):
            return lax.broadcasted_iota(jnp.int32, shape, 1) < kcnt_ref[row] * tile

        dk, dv = gradients(k_few[...], v_few[...], mask)
        for j in range(count):
            at = kidx_ref[row, j]
            dk_acc[at] += dk[j * tile:(j + 1) * tile]
            dv_acc[at] += dv[j * tile:(j + 1) * tile]

    @pl.when(row == last)
    def _():
        tiles = dk_acc.shape[0] // t
        for s, dkv_ref in enumerate(dkv_refs):
            at = pl.ds(s * tiles, tiles)
            dkv_ref[0] = dk_acc[at].reshape(dkv_ref.shape[1:]).astype(BF16)
            dkv_ref[1] = dv_acc[at].reshape(dkv_ref.shape[1:]).astype(BF16)


def whole_block(shape):
    return pl.BlockSpec(shape, lambda *_: (0,) * len(shape))


def one_array(which, length):
    return pl.BlockSpec((1, length, HEAD), lambda *_: (which, 0, 0))


def tile_block(which, tile):
    return pl.BlockSpec((1, tile, HEAD), lambda r, *_: (which, r, 0))


def simple_call(kernel, name, scalars, inputs, outputs, scratch=()):
    size = sum(2 * math.prod(x.shape) for x in list(inputs) + list(outputs))
    return pl.pallas_call(
        kernel,
        grid_spec=pltpu.PrefetchScalarGridSpec(
            num_scalar_prefetch=1,
            grid=(1,),
            in_specs=[whole_block(x.shape) for x in inputs],
            out_specs=[whole_block(x.shape) for x in outputs],
            scratch_shapes=scratch,
        ),
        out_shape=outputs,
        compiler_params=pltpu.CompilerParams(vmem_limit_bytes=48 * 2**20),
        cost_estimate=pl.CostEstimate(flops=0, bytes_accessed=2 * size, transcendentals=0),
        name=name,
    )(scalars, *inputs)


def shifts(t, s):
    return [(c, (c + s) % t) for c in range(t)]


def place_kernel(place_ref, *refs):
    sources, out_ref = refs[:-1], refs[-1]
    step = pl.program_id(0)
    for u in range(2):
        own, beside, above, upper, lower = sources[5 * u:5 * u + 5]
        for v, source in enumerate((own, beside, above)):
            @pl.when(step == 4 * u + v)
            def _(source=source):
                out_ref[...] = source[...].astype(F32)

        @pl.when(step == 4 * u + 3)
        def _(upper=upper, lower=lower):
            middle = upper.shape[0]
            out_ref[:middle] = upper[...].astype(F32)
            out_ref[middle:] = lower[...].astype(F32)


def gather_tiles_by_core(n, t, tile_sum, chip, core):
    in_plane = n // PLANES
    plane, seat = chip // in_plane, chip % in_plane
    tile_rows, cols = tile_sum.shape
    across = [
        (i * t + c, (i ^ 2 * in_plane) * t + c)
        for i in range(n) for c in range(t) if i // in_plane // 2 == c
    ]
    from_half = lax.ppermute(tile_sum, ("ctx", "tp"), across)

    def swap(x, k):
        return lax.ppermute(x, "ctx", [(i, i ^ k) for i in range(n)])

    first = jnp.where(plane // 2 == core, tile_sum, from_half)
    second = swap(first, in_plane)
    middle = tile_rows // 2
    sources = []
    for mine in (first, second):
        beside, above = swap(mine, 1), swap(mine, 2)
        sources += [mine, beside, above, swap(beside[:middle], 2), swap(above[middle:], 1)]
    place = jnp.stack([plane % 2, seat]).astype(jnp.int32)
    return pl.pallas_call(
        place_kernel,
        grid_spec=pltpu.PrefetchScalarGridSpec(
            num_scalar_prefetch=1,
            grid=(8,),
            in_specs=[whole_block(x.shape) for x in sources],
            out_specs=pl.BlockSpec(
                (tile_rows, cols), lambda s, place: (s // 4 ^ place[0], s % 4 ^ place[1])
            ),
        ),
        out_shape=jax.ShapeDtypeStruct((2 * tile_rows, in_plane * cols), F32),
        compiler_params=pltpu.CompilerParams(vmem_limit_bytes=48 * 2**20),
        name="place",
    )(place, *sources)


def per_device(n, t, queries, key_vectors, value_vectors, out_weight, out_grad, block_segment):
    rows, width = queries.shape
    heads_here = width // HEAD
    heads = heads_here * t
    sub = rows // t
    tile = min(sub, BLK)
    per_chunk = sub // tile
    core = lax.axis_index("tp")
    chip = lax.axis_index("ctx")
    in_plane = n // PLANES
    heads_plane = heads // PLANES
    seat = chip % in_plane

    def tp_swap(pick):
        got = [pick(core)]
        for s in range(1, t):
            got.append(lax.ppermute(pick((core + s) % t), "tp", shifts(t, s)))
        return [lax.select_n((core - p) % t, *got) for p in range(t)]

    def tp_gather(x):
        return tp_swap(lambda _: x)

    def tp_split(pack):
        return tp_swap(lambda p: lax.dynamic_index_in_dim(pack, p, 0, False))

    def plane_swap(pick):
        got = [pick(seat)]
        for k in range(1, in_plane):
            got.append(lax.ppermute(pick(seat ^ k), "ctx", [(i, i ^ k) for i in range(n)]))
        return [lax.select_n(seat ^ b, *got) for b in range(in_plane)]

    def shape(*dims):
        return jax.ShapeDtypeStruct(dims, BF16)

    where = jnp.stack([chip, core]).astype(jnp.int32)
    held = [(i % in_plane - i // in_plane) % in_plane < heads_plane for i in range(n)]

    chunk_row = jnp.arange(n)[:, None] * rows + jnp.arange(per_chunk)[None, :] * tile

    def tile_segments(part):
        return jnp.take(block_segment, ((chunk_row + part * sub) // BLK).reshape(-1))

    seg_parts = [tile_segments((core - s) % t) for s in range(t)]
    seg_q = seg_parts[0]
    seg_k = jnp.concatenate(seg_parts)
    full = (seg_q == 0) | (seg_q == TARGET)
    permitted = (seg_k[None] == 0) | (seg_k[None] == seg_q[:, None])
    total_blocks = block_segment.shape[0]
    count = (TXT_BLK + -(-(total_blocks - TXT_BLK) // RUNS)) * (BLK // tile)
    kcnt = jnp.sum(permitted.astype(jnp.int32), axis=1)
    tiles_k = seg_k.shape[0]
    ids = jnp.arange(tiles_k)
    place = jnp.sum((permitted[:, None, :] & (ids[None, None, :] < ids[None, :, None])).astype(jnp.int32), axis=2)
    hit = permitted[:, None, :] & (place[:, None, :] == jnp.arange(count)[None, :, None])
    kidx = jnp.sum(jnp.where(hit, ids[None, None, :], 0), axis=2).astype(jnp.int32)
    full = full.astype(jnp.int32)

    def other_rows(*arrays):
        return [
            lax.ppermute(
                jnp.stack([
                    lax.dynamic_slice_in_dim(x, (core + s) % t * sub, sub, 0) for x in arrays
                ]),
                "tp", shifts(t, s),
            )
            for s in range(1, t)
        ]

    got_qkv = other_rows(queries, key_vectors, value_vectors)

    half = out_grad.shape[1]
    model = half * t
    full_grad = jnp.concatenate(tp_gather(out_grad), axis=1)
    grad_attn = dot(full_grad, out_weight, NT).astype(BF16)
    got_g = other_rows(grad_attn)

    cols = model // in_plane
    mine = lax.dynamic_slice_in_dim(full_grad, core * sub, sub, 0)
    plane_grad = jnp.stack(
        plane_swap(lambda b: lax.dynamic_slice_in_dim(mine, b * cols, cols, 1))
    )
    lines = [[a * in_plane + b for a in range(PLANES)] for b in range(in_plane)]
    slice_grad = lax.all_gather(plane_grad, "ctx", axis_index_groups=lines)
    slice_grad = slice_grad.reshape(n * sub, cols)

    got = [x for pair in zip(got_qkv, got_g) for x in pair]
    sent = simple_call(
        functools.partial(pack_kernel, n, t), "pack", where,
        [queries, key_vectors, value_vectors, grad_attn] + got,
        [shape(4, sub, HEAD)] * n,
        [pltpu.VMEM((heads, 4, sub, HEAD), BF16)],
    )
    chunks = [sent[0]] + [
        lax.ppermute(sent[k], "ctx", [(i, i ^ k) for i in range(n) if held[i ^ k]]) for k in range(1, n)
    ]
    length = n * sub
    qg, kv = simple_call(
        functools.partial(join_kernel, n), "join", where, chunks, [shape(2, length, HEAD)] * 2
    )
    kv_all = [kv] + [lax.ppermute(kv, "tp", shifts(t, s)) for s in range(1, t)]

    tiles_q = n * per_chunk
    few = [pltpu.VMEM((count * tile, HEAD), BF16)] * 2 + [pltpu.VMEM((tiles_k, tile, HEAD), BF16)] * 2
    params = pltpu.CompilerParams(vmem_limit_bytes=48 * 2**20)
    part_blocks = [one_array(0, length), one_array(1, length)] * t
    part_arrays = [a for pack in kv_all for a in (pack, pack)]
    row_block = pl.BlockSpec((tile, HEAD), lambda r, *_: (r, 0))
    attn, lse = pl.pallas_call(
        functools.partial(forward_kernel, t, tile, count),
        grid_spec=pltpu.PrefetchScalarGridSpec(
            num_scalar_prefetch=3,
            grid=(tiles_q,),
            in_specs=[tile_block(0, tile)] + part_blocks,
            out_specs=[row_block, row_block],
            scratch_shapes=few,
        ),
        out_shape=[shape(length, HEAD), jax.ShapeDtypeStruct((length, HEAD), F32)],
        compiler_params=params,
        cost_estimate=pl.CostEstimate(flops=16 * 10**9, bytes_accessed=5 * 2**20, transcendentals=2**22),
        name="forward",
    )(full, kcnt, kidx, qg, *part_arrays)

    plane = chip // in_plane
    travel = [attn] + [
        lax.ppermute(attn, "ctx", [(i, i ^ k) for i in range(n) if held[i]]) for k in range(1, in_plane)
    ]
    got_attn = [
        lax.select_n(seat ^ ((plane + j) % in_plane), *travel) for j in range(heads_plane)
    ]

    dq, *dkv = pl.pallas_call(
        functools.partial(backward_kernel, t, tile, count),
        grid_spec=pltpu.PrefetchScalarGridSpec(
            num_scalar_prefetch=3,
            grid=(tiles_q,),
            in_specs=[tile_block(0, tile), tile_block(1, tile), row_block, row_block] + part_blocks,
            out_specs=[row_block] + [whole_block((2, length, HEAD))] * t,
            scratch_shapes=few + [pltpu.VMEM((tiles_k, tile, HEAD), F32)] * 2,
        ),
        out_shape=[shape(length, HEAD)] + [shape(2, length, HEAD)] * t,
        compiler_params=params,
        cost_estimate=pl.CostEstimate(flops=20 * 10**9, bytes_accessed=8 * 2**20, transcendentals=2**22),
        name="backward",
    )(full, kcnt, kidx, qg, qg, attn, lse, *part_arrays)

    got_attn, dq = lax.optimization_barrier((got_attn, dq))

    plane_attn = jnp.stack([a.reshape(n * sub, HEAD) for a in got_attn])
    tile_term = jnp.einsum("hrd,rc->hdc", plane_attn, slice_grad, preferred_element_type=F32)
    tile_term = tile_term.reshape(heads_plane * HEAD, cols)
    tile_rows = heads_plane * HEAD
    planes_here = PLANES // t
    if in_plane == 4 and t == 2:
        tile_sum = tile_term
        for s in range(1, t):
            tile_sum = tile_sum + lax.ppermute(tile_term.astype(BF16), "tp", shifts(t, s)).astype(F32)
        grad_weight = gather_tiles_by_core(n, t, tile_sum.astype(BF16), chip, core)
    else:
        piece = tile_rows // t
        tile_term = tile_term.reshape(t, piece, cols)
        tile_sum = lax.dynamic_index_in_dim(tile_term, core, 0, False)
        for s in range(1, t):
            there = lax.dynamic_index_in_dim(tile_term, (core + s) % t, 0, False)
            tile_sum = tile_sum + lax.ppermute(there.astype(BF16), "tp", shifts(t, s)).astype(F32)
        tiles = lax.all_gather(tile_sum.astype(BF16), "ctx")
        tiles = jnp.stack(tp_split(tiles.reshape(t, planes_here, in_plane, piece, cols)))
        grad_weight = tiles.transpose(1, 0, 3, 2, 4).reshape(width, model).astype(F32)

    got_dkv = [
        lax.ppermute(dkv[s], "tp", [(c, (c - s) % t) for c in range(t)]) for s in range(1, t)
    ]
    sent = simple_call(
        functools.partial(unjoin_kernel, n, t), "unjoin", where,
        [attn, dq, dkv[0]] + got_dkv, [shape(4, sub, HEAD)] * n,
    )
    chunks = [sent[0]] + [
        lax.ppermute(sent[k], "ctx", [(i, i ^ k) for i in range(n) if held[i]]) for k in range(1, n)
    ]
    mine = simple_call(
        functools.partial(by_core_kernel, n, t), "by_core", where, chunks,
        [shape(heads_here, 4, sub, HEAD)] * t, [pltpu.VMEM((heads, 4, sub, HEAD), BF16)],
    )
    parts = [mine[0]] + [lax.ppermute(mine[s], "tp", shifts(t, s)) for s in range(1, t)]
    attention, grad_queries, grad_keys, grad_values = simple_call(
        functools.partial(unpack_kernel, t), "unpack", where, parts, [shape(rows, width)] * 4
    )
    projected = dot(attention, out_weight)
    own = lax.dynamic_slice_in_dim(projected, core * half, half, 1)
    for s in range(1, t):
        there = lax.dynamic_slice_in_dim(projected, (core + s) % t * half, half, 1)
        own = own + lax.ppermute(there.astype(BF16), "tp", shifts(t, s)).astype(F32)
    attention_out = own.astype(BF16)

    return attention_out, grad_queries, grad_keys, grad_values, grad_weight


def solution(mesh):
    n, t = mesh.shape["ctx"], mesh.shape["tp"]
    in_specs = (P("ctx", "tp"), P("ctx", "tp"), P("ctx", "tp"), P("tp", None), P("ctx", "tp"), P())
    out_specs = (P("ctx", "tp"), P("ctx", "tp"), P("ctx", "tp"), P("ctx", "tp"), P("tp", None))
    return jax.shard_map(
        functools.partial(per_device, n, t), mesh=mesh, in_specs=in_specs, out_specs=out_specs, check_vma=False
    )
```

```python
import functools
import math

import jax
import jax.numpy as jnp
from jax import lax
from jax.experimental import pallas as pl
from jax.experimental.pallas import tpu as pltpu
from jax.sharding import PartitionSpec as P

HEAD = 128
BLK = 128
TXT_BLK = 4
RUNS = 5
TARGET = 5
PLANES = 4
LOG2E = math.log2(math.e)
NEG_BIG = -1e30

NT = (((1,), (1,)), ((), ()))
TN = (((0,), (0,)), ((), ()))
F32 = jnp.float32
BF16 = jnp.bfloat16


def dot(a, b, dims=(((1,), (0,)), ((), ()))):
    return lax.dot_general(a, b, dims, preferred_element_type=F32)


def gather_tiles(k_ref, kidx_ref, row, dst, tile, count):
    for j in range(count):
        dst[pl.ds(j * tile, tile), :] = k_ref[kidx_ref[row, j]]


def join_parts(parts, k_all, v_all):
    shape = (k_all.shape[0] // (len(parts) // 2),) + k_all.shape[1:]
    for s in range(len(parts) // 2):
        at = pl.ds(s * shape[0], shape[0])
        k_all[at] = parts[2 * s][...].reshape(shape)
        v_all[at] = parts[2 * s + 1][...].reshape(shape)


def head_of(chip, in_plane, heads_plane):
    place = (chip % in_plane - chip // in_plane) % in_plane
    return place < heads_plane, chip // in_plane * heads_plane + min(place, heads_plane - 1)


def pack_kernel(n, t, where_ref, *refs):
    arrays, got, outs, heads_all = refs[:4], refs[4:4 + 2 * (t - 1)], refs[4 + 2 * (t - 1):-1], refs[-1]
    core = where_ref[1]
    sub = heads_all.shape[2]
    heads_here = heads_all.shape[0] // t
    for a in range(4):
        for h in range(heads_here):
            column = pl.ds(h * HEAD, HEAD)
            heads_all[core * heads_here + h, a] = arrays[a][pl.ds(core * sub, sub), column]
            for s in range(1, t):
                first = (core + t - s) % t * heads_here
                source = got[2 * (s - 1)] if a < 3 else got[2 * (s - 1) + 1]
                heads_all[first + h, a] = source[a % 3, :, column]
    out_ref = outs[0]
    for k in range(n):
        held, head = head_of(k, n // PLANES, heads_all.shape[0] // PLANES)
        out_ref[k] = heads_all[head] if held else jnp.zeros_like(heads_all[0])


def join_kernel(n, where_ref, chunks_ref, qg_ref, kv_ref):
    sub = chunks_ref.shape[2]
    for k in range(n):
        at = pl.ds(k * sub, sub)
        qg_ref[0, at] = chunks_ref[k, 0]
        kv_ref[0, at] = chunks_ref[k, 1]
        kv_ref[1, at] = chunks_ref[k, 2]
        qg_ref[1, at] = chunks_ref[k, 3]


def unjoin_kernel(n, t, where_ref, attn_ref, dq_ref, dkv_ref, *refs):
    got, out_ref = refs[:t - 1], refs[t - 1]
    sub = out_ref.shape[2]
    for k in range(n):
        at = pl.ds(k * sub, sub)
        out_ref[k, 0] = attn_ref[at]
        out_ref[k, 1] = dq_ref[at]
        for a in range(2):
            total = dkv_ref[a, at].astype(F32)
            for other in got:
                total = total + other[a, at].astype(F32)
            out_ref[k, 2 + a] = total.astype(BF16)


def by_core_kernel(n, t, where_ref, chunks_ref, *refs):
    outs, heads_all = refs[:t], refs[t]
    core = where_ref[1]
    heads_here = heads_all.shape[0] // t
    for k in range(n):
        held, head = head_of(k, n // PLANES, heads_all.shape[0] // PLANES)
        if held:
            heads_all[head] = chunks_ref[k]
    for s in range(t):
        outs[s][...] = heads_all[pl.ds((core + s) % t * heads_here, heads_here)]


def seats_kernel(in_plane, where_ref, *refs):
    got, out_ref = refs[:in_plane], refs[in_plane]
    seat = where_ref[0] % in_plane
    for k in range(in_plane):
        out_ref[seat ^ k] = got[k][...]


def tile_kernel(in_plane, heads_plane, t, where_ref, *refs):
    attns, (grad_ref, own_ref), sends = refs[:in_plane], refs[in_plane:in_plane + 2], refs[in_plane + 2:-2]
    seats, total = refs[-2:]
    chip, core = where_ref[0], where_ref[1]
    seat = chip % in_plane
    plane = chip // in_plane
    step = pl.program_id(0)
    for k in range(in_plane):
        seats[seat ^ k] = attns[k][...]

    @pl.when(step == 0)
    def _():
        total[...] = jnp.zeros_like(total)

    grad = grad_ref[...]
    for j in range(heads_plane):
        total[pl.ds(j * HEAD, HEAD)] += dot(seats[(plane + j) % in_plane], grad, TN)

    @pl.when(step == pl.num_programs(0) - 1)
    def _():
        piece = own_ref.shape[0]
        own_ref[...] = total[pl.ds(pl.multiple_of(core * piece, piece), piece)]
        for s in range(1, t):
            at = pl.ds(pl.multiple_of((core + s) % t * piece, piece), piece)
            sends[s - 1][...] = total[at].astype(BF16)


def place_kernel(t, where_ref, *refs):
    parts, out_ref = refs[:t], refs[t]
    core = where_ref[1]
    piece = parts[0].shape[1]
    for s in range(t):
        at = pl.ds(pl.multiple_of((core + t - s) % t * piece, piece), piece)
        out_ref[at] = parts[s][0].astype(F32)


def unpack_kernel(t, where_ref, *refs):
    parts, outs = refs[:t], refs[t:]
    core = where_ref[1]
    heads_here, _, sub, _ = parts[0].shape
    for s in range(t):
        at = pl.ds(pl.multiple_of((core + t - s) % t * sub, sub), sub)
        for a in range(4):
            for h in range(heads_here):
                outs[a][at, pl.ds(h * HEAD, HEAD)] = parts[s][h, a]


def forward_kernel(t, tile, count, full_ref, kcnt_ref, kidx_ref, q_ref, *refs):
    parts, (out_ref, lse_ref, k_few, v_few, k_ref, v_ref) = refs[:2 * t], refs[2 * t:]
    row = pl.program_id(0)
    q = q_ref[0]

    @pl.when(row == 0)
    def _():
        join_parts(parts, k_ref, v_ref)

    def finish(s, v):
        top = jnp.max(s, axis=1, keepdims=True)
        p = jnp.exp2(s - top)
        mass = jnp.sum(p, axis=1, keepdims=True)
        out = dot(p.astype(BF16), v)
        out_ref[...] = (out / mass).astype(BF16)
        lse_ref[...] = jnp.broadcast_to(top + jnp.log2(mass), lse_ref.shape)

    scale = HEAD ** -0.5 * LOG2E

    @pl.when(full_ref[row] == 1)
    def _():
        keys = k_ref[...].reshape(-1, HEAD)
        finish(dot(q, keys, NT) * scale, v_ref[...].reshape(-1, HEAD))

    @pl.when(full_ref[row] == 0)
    def _():
        gather_tiles(k_ref, kidx_ref, row, k_few, tile, count)
        gather_tiles(v_ref, kidx_ref, row, v_few, tile, count)
        s = dot(q, k_few[...], NT) * scale
        column = lax.broadcasted_iota(jnp.int32, s.shape, 1)
        s = jnp.where(column < kcnt_ref[row] * tile, s, NEG_BIG)
        finish(s, v_few[...])


def backward_kernel(t, tile, count, full_ref, kcnt_ref, kidx_ref, q_ref, g_ref, o_ref, lse_ref, *refs):
    parts, dkv_refs = refs[:2 * t], refs[2 * t + 1:3 * t + 1]
    dq_ref = refs[2 * t]
    k_few, v_few, k_ref, v_ref, dk_acc, dv_acc = refs[3 * t + 1:]
    row = pl.program_id(0)
    last = pl.num_programs(0) - 1

    @pl.when(row == 0)
    def _():
        join_parts(parts, k_ref, v_ref)
        dk_acc[...] = jnp.zeros_like(dk_acc)
        dv_acc[...] = jnp.zeros_like(dv_acc)

    q = q_ref[0]
    g = g_ref[0]
    delta = jnp.sum(g.astype(F32) * o_ref[...].astype(F32), axis=1, keepdims=True)
    lse = lse_ref[:, :1]
    unit = HEAD ** -0.5
    scale = unit * LOG2E

    def gradients(keys, values, mask):
        s = dot(q, keys, NT)
        p = jnp.exp2(s * scale - lse)
        if mask is not None:
            p = jnp.where(mask(p.shape), p, 0.0)
        ds = (p * (dot(g, values, NT) - delta)).astype(BF16)
        dq_ref[...] = (dot(ds, keys) * unit).astype(BF16)
        return dot(ds, q, TN) * unit, dot(p.astype(BF16), g, TN)

    @pl.when(full_ref[row] == 1)
    def _():
        dk, dv = gradients(k_ref[...].reshape(-1, HEAD), v_ref[...].reshape(-1, HEAD), None)
        dk_acc[...] += dk.reshape(dk_acc.shape)
        dv_acc[...] += dv.reshape(dv_acc.shape)

    @pl.when(full_ref[row] == 0)
    def _():
        gather_tiles(k_ref, kidx_ref, row, k_few, tile, count)
        gather_tiles(v_ref, kidx_ref, row, v_few, tile, count)

        def mask(shape):
            return lax.broadcasted_iota(jnp.int32, shape, 1) < kcnt_ref[row] * tile

        dk, dv = gradients(k_few[...], v_few[...], mask)
        for j in range(count):
            at = kidx_ref[row, j]
            dk_acc[at] += dk[j * tile:(j + 1) * tile]
            dv_acc[at] += dv[j * tile:(j + 1) * tile]

    @pl.when(row == last)
    def _():
        tiles = dk_acc.shape[0] // t
        for s, dkv_ref in enumerate(dkv_refs):
            at = pl.ds(s * tiles, tiles)
            dkv_ref[0] = dk_acc[at].reshape(dkv_ref.shape[1:]).astype(BF16)
            dkv_ref[1] = dv_acc[at].reshape(dkv_ref.shape[1:]).astype(BF16)


def whole_block(shape):
    return pl.BlockSpec(shape, lambda *_: (0,) * len(shape))


def one_array(which, length):
    return pl.BlockSpec((1, length, HEAD), lambda *_: (which, 0, 0))


def tile_block(which, tile):
    return pl.BlockSpec((1, tile, HEAD), lambda r, *_: (which, r, 0))


def simple_call(kernel, name, scalars, inputs, outputs, scratch=()):
    size = sum(2 * math.prod(x.shape) for x in list(inputs) + list(outputs))
    return pl.pallas_call(
        kernel,
        grid_spec=pltpu.PrefetchScalarGridSpec(
            num_scalar_prefetch=1,
            grid=(1,),
            in_specs=[whole_block(x.shape) for x in inputs],
            out_specs=[whole_block(x.shape) for x in outputs],
            scratch_shapes=scratch,
        ),
        out_shape=outputs,
        compiler_params=pltpu.CompilerParams(vmem_limit_bytes=48 * 2**20),
        cost_estimate=pl.CostEstimate(flops=0, bytes_accessed=2 * size, transcendentals=0),
        name=name,
    )(scalars, *inputs)


def shifts(t, s):
    return [(c, (c + s) % t) for c in range(t)]


def per_device(n, t, queries, key_vectors, value_vectors, out_weight, out_grad, block_segment):
    rows, width = queries.shape
    heads_here = width // HEAD
    heads = heads_here * t
    sub = rows // t
    tile = min(sub, BLK)
    per_chunk = sub // tile
    core = lax.axis_index("tp")
    chip = lax.axis_index("ctx")
    in_plane = n // PLANES
    heads_plane = heads // PLANES
    seat = chip % in_plane

    def tp_swap(pick):
        got = [pick(core)]
        for s in range(1, t):
            got.append(lax.ppermute(pick((core + s) % t), "tp", shifts(t, s)))
        return [lax.select_n((core - p) % t, *got) for p in range(t)]

    def tp_gather(x):
        return tp_swap(lambda _: x)

    def shape(*dims):
        return jax.ShapeDtypeStruct(dims, BF16)

    where = jnp.stack([chip, core]).astype(jnp.int32)
    held = [(i % in_plane - i // in_plane) % in_plane < heads_plane for i in range(n)]

    chunk_row = jnp.arange(n)[:, None] * rows + jnp.arange(per_chunk)[None, :] * tile

    def tile_segments(part):
        return jnp.take(block_segment, ((chunk_row + part * sub) // BLK).reshape(-1))

    seg_parts = [tile_segments((core - s) % t) for s in range(t)]
    seg_q = seg_parts[0]
    seg_k = jnp.concatenate(seg_parts)
    full = (seg_q == 0) | (seg_q == TARGET)
    permitted = (seg_k[None] == 0) | (seg_k[None] == seg_q[:, None])
    total_blocks = block_segment.shape[0]
    count = (TXT_BLK + -(-(total_blocks - TXT_BLK) // RUNS)) * (BLK // tile)
    kcnt = jnp.sum(permitted.astype(jnp.int32), axis=1)
    tiles_k = seg_k.shape[0]
    ids = jnp.arange(tiles_k)
    place = jnp.sum((permitted[:, None, :] & (ids[None, None, :] < ids[None, :, None])).astype(jnp.int32), axis=2)
    hit = permitted[:, None, :] & (place[:, None, :] == jnp.arange(count)[None, :, None])
    kidx = jnp.sum(jnp.where(hit, ids[None, None, :], 0), axis=2).astype(jnp.int32)
    full = full.astype(jnp.int32)

    def other_rows(*arrays):
        return [
            lax.ppermute(
                jnp.stack([
                    lax.dynamic_slice_in_dim(x, (core + s) % t * sub, sub, 0) for x in arrays
                ]),
                "tp", shifts(t, s),
            )
            for s in range(1, t)
        ]

    got_qkv = other_rows(queries, key_vectors, value_vectors)

    half = out_grad.shape[1]
    model = half * t
    full_grad = jnp.concatenate(tp_gather(out_grad), axis=1)
    grad_attn = dot(full_grad, out_weight, NT).astype(BF16)
    got_g = other_rows(grad_attn)

    cols = model // in_plane
    mine = lax.dynamic_slice_in_dim(full_grad, core * sub, sub, 0)
    plane_got = [lax.dynamic_slice_in_dim(mine, seat * cols, cols, 1)]
    for k in range(1, in_plane):
        there = lax.dynamic_slice_in_dim(mine, (seat ^ k) * cols, cols, 1)
        plane_got.append(lax.ppermute(there, "ctx", [(i, i ^ k) for i in range(n)]))
    (plane_grad,) = simple_call(
        functools.partial(seats_kernel, in_plane), "seats", where, plane_got, [shape(in_plane, sub, cols)]
    )
    got = [x for pair in zip(got_qkv, got_g) for x in pair]
    (sent,) = simple_call(
        functools.partial(pack_kernel, n, t), "pack", where,
        [queries, key_vectors, value_vectors, grad_attn] + got,
        [shape(n, 4, sub, HEAD)],
        [pltpu.VMEM((heads, 4, sub, HEAD), BF16)],
    )
    sent, plane_grad = lax.optimization_barrier((sent, plane_grad))
    lines = [[a * in_plane + b for a in range(PLANES)] for b in range(in_plane)]
    slice_grad = lax.all_gather(plane_grad, "ctx", axis_index_groups=lines)
    slice_grad = slice_grad.reshape(n * sub, cols)
    chunks = lax.all_to_all(sent, "ctx", 0, 0, tiled=True)
    length = n * sub
    qg, kv = simple_call(
        functools.partial(join_kernel, n), "join", where, [chunks], [shape(2, length, HEAD)] * 2
    )
    kv_all = [kv] + [lax.ppermute(kv, "tp", shifts(t, s)) for s in range(1, t)]

    tiles_q = n * per_chunk
    few = [pltpu.VMEM((count * tile, HEAD), BF16)] * 2 + [pltpu.VMEM((tiles_k, tile, HEAD), BF16)] * 2
    params = pltpu.CompilerParams(vmem_limit_bytes=48 * 2**20)
    part_blocks = [one_array(0, length), one_array(1, length)] * t
    part_arrays = [a for pack in kv_all for a in (pack, pack)]
    row_block = pl.BlockSpec((tile, HEAD), lambda r, *_: (r, 0))
    attn, lse = pl.pallas_call(
        functools.partial(forward_kernel, t, tile, count),
        grid_spec=pltpu.PrefetchScalarGridSpec(
            num_scalar_prefetch=3,
            grid=(tiles_q,),
            in_specs=[tile_block(0, tile)] + part_blocks,
            out_specs=[row_block, row_block],
            scratch_shapes=few,
        ),
        out_shape=[shape(length, HEAD), jax.ShapeDtypeStruct((length, HEAD), F32)],
        compiler_params=params,
        cost_estimate=pl.CostEstimate(flops=16 * 10**9, bytes_accessed=5 * 2**20, transcendentals=2**22),
        name="forward",
    )(full, kcnt, kidx, qg, *part_arrays)

    travel = [attn] + [
        lax.ppermute(attn, "ctx", [(i, i ^ k) for i in range(n) if held[i]]) for k in range(1, in_plane)
    ]
    dq, *dkv = pl.pallas_call(
        functools.partial(backward_kernel, t, tile, count),
        grid_spec=pltpu.PrefetchScalarGridSpec(
            num_scalar_prefetch=3,
            grid=(tiles_q,),
            in_specs=[tile_block(0, tile), tile_block(1, tile), row_block, row_block] + part_blocks,
            out_specs=[row_block] + [whole_block((2, length, HEAD))] * t,
            scratch_shapes=few + [pltpu.VMEM((tiles_k, tile, HEAD), F32)] * 2,
        ),
        out_shape=[shape(length, HEAD)] + [shape(2, length, HEAD)] * t,
        compiler_params=params,
        cost_estimate=pl.CostEstimate(flops=20 * 10**9, bytes_accessed=8 * 2**20, transcendentals=2**22),
        name="backward",
    )(full, kcnt, kidx, qg, qg, attn, lse, *part_arrays)

    *travel, dq = lax.optimization_barrier((*travel, dq))

    tile_rows = heads_plane * HEAD
    piece = tile_rows // t
    step_rows = length // 4
    tile_own, *tile_sends = pl.pallas_call(
        functools.partial(tile_kernel, in_plane, heads_plane, t),
        grid_spec=pltpu.PrefetchScalarGridSpec(
            num_scalar_prefetch=1,
            grid=(4,),
            in_specs=[pl.BlockSpec((step_rows, HEAD), lambda r, *_: (r, 0))] * in_plane
            + [pl.BlockSpec((step_rows, cols), lambda r, *_: (r, 0))],
            out_specs=[whole_block((piece, cols))] * t,
            scratch_shapes=[
                pltpu.VMEM((in_plane, step_rows, HEAD), BF16), pltpu.VMEM((tile_rows, cols), F32)
            ],
        ),
        out_shape=[jax.ShapeDtypeStruct((piece, cols), F32)] + [shape(piece, cols)] * (t - 1),
        compiler_params=params,
        cost_estimate=pl.CostEstimate(flops=5 * 10**9, bytes_accessed=2**22, transcendentals=0),
        name="tile",
    )(where, *travel, slice_grad)
    tile_sum = tile_own
    for s in range(1, t):
        tile_sum = tile_sum + lax.ppermute(tile_sends[s - 1], "tp", shifts(t, s)).astype(F32)
    tiles = lax.all_gather(tile_sum.astype(BF16), "ctx")
    here = n // t
    tiles_core = [tiles] + [
        lax.ppermute(
            lax.dynamic_slice_in_dim(tiles, (core + s) % t * here, here, 0), "tp", shifts(t, s)
        )
        for s in range(1, t)
    ]
    grad_weight = pl.pallas_call(
        functools.partial(place_kernel, t),
        grid_spec=pltpu.PrefetchScalarGridSpec(
            num_scalar_prefetch=1,
            grid=(here,),
            in_specs=[pl.BlockSpec((1, piece, cols), lambda r, where: (where[1] * here + r, 0, 0))]
            + [pl.BlockSpec((1, piece, cols), lambda r, *_: (r, 0, 0))] * (t - 1),
            out_specs=pl.BlockSpec((tile_rows, cols), lambda r, *_: (r // in_plane, r % in_plane)),
        ),
        out_shape=jax.ShapeDtypeStruct((width, model), F32),
        compiler_params=params,
        cost_estimate=pl.CostEstimate(flops=0, bytes_accessed=2**24, transcendentals=0),
        name="place",
    )(where, *tiles_core)

    got_dkv = [
        lax.ppermute(dkv[s], "tp", [(c, (c - s) % t) for c in range(t)]) for s in range(1, t)
    ]
    (sent,) = simple_call(
        functools.partial(unjoin_kernel, n, t), "unjoin", where,
        [attn, dq, dkv[0]] + got_dkv, [shape(n, 4, sub, HEAD)],
    )
    chunks = lax.all_to_all(sent, "ctx", 0, 0, tiled=True)
    mine = simple_call(
        functools.partial(by_core_kernel, n, t), "by_core", where, [chunks],
        [shape(heads_here, 4, sub, HEAD)] * t, [pltpu.VMEM((heads, 4, sub, HEAD), BF16)],
    )
    parts = [mine[0]] + [lax.ppermute(mine[s], "tp", shifts(t, s)) for s in range(1, t)]
    attention, grad_queries, grad_keys, grad_values = simple_call(
        functools.partial(unpack_kernel, t), "unpack", where, parts, [shape(rows, width)] * 4
    )
    projected = dot(attention, out_weight)
    own = lax.dynamic_slice_in_dim(projected, core * half, half, 1)
    for s in range(1, t):
        there = lax.dynamic_slice_in_dim(projected, (core + s) % t * half, half, 1)
        own = own + lax.ppermute(there.astype(BF16), "tp", shifts(t, s)).astype(F32)
    attention_out = own.astype(BF16)

    return attention_out, grad_queries, grad_keys, grad_values, grad_weight


def solution(mesh):
    n, t = mesh.shape["ctx"], mesh.shape["tp"]
    in_specs = (P("ctx", "tp"), P("ctx", "tp"), P("ctx", "tp"), P("tp", None), P("ctx", "tp"), P())
    out_specs = (P("ctx", "tp"), P("ctx", "tp"), P("ctx", "tp"), P("ctx", "tp"), P("tp", None))
    return jax.shard_map(
        functools.partial(per_device, n, t), mesh=mesh, in_specs=in_specs, out_specs=out_specs, check_vma=False
    )
```

```python
import functools
import math

import jax
import jax.numpy as jnp
from jax import lax
from jax.experimental import pallas as pl
from jax.experimental.pallas import tpu as pltpu
from jax.sharding import PartitionSpec as P

HEAD = 128
BLK = 128
TXT_BLK = 4
RUNS = 5
TARGET = 5
PLANES = 4
LOG2E = math.log2(math.e)
NEG_BIG = -1e30

NT = (((1,), (1,)), ((), ()))
TN = (((0,), (0,)), ((), ()))
F32 = jnp.float32
BF16 = jnp.bfloat16


def dot(a, b, dims=(((1,), (0,)), ((), ()))):
    return lax.dot_general(a, b, dims, preferred_element_type=F32)


def gather_tiles(k_ref, kidx_ref, row, dst, tile, count):
    for j in range(count):
        dst[pl.ds(j * tile, tile), :] = k_ref[kidx_ref[row, j]]


def join_parts(parts, k_all, v_all):
    shape = (k_all.shape[0] // (len(parts) // 2),) + k_all.shape[1:]
    for s in range(len(parts) // 2):
        at = pl.ds(s * shape[0], shape[0])
        k_all[at] = parts[2 * s][...].reshape(shape)
        v_all[at] = parts[2 * s + 1][...].reshape(shape)


def head_of(chip, in_plane, heads_plane):
    place = (chip % in_plane - chip // in_plane) % in_plane
    return place < heads_plane, chip // in_plane * heads_plane + min(place, heads_plane - 1)


def pack_kernel(n, t, count, where_ref, *refs):
    arrays, got, (out_ref, heads_all) = refs[:count], refs[count:count + t - 1], refs[count + t - 1:]
    core = where_ref[1]
    sub = heads_all.shape[2]
    heads_here = heads_all.shape[0] // t
    for a in range(count):
        for h in range(heads_here):
            column = pl.ds(h * HEAD, HEAD)
            heads_all[core * heads_here + h, a] = arrays[a][pl.ds(core * sub, sub), column]
            for s in range(1, t):
                first = (core + t - s) % t * heads_here
                heads_all[first + h, a] = got[s - 1][a, :, column]
    for k in range(n):
        held, head = head_of(k, n // PLANES, heads_all.shape[0] // PLANES)
        out_ref[k] = heads_all[head] if held else jnp.zeros_like(heads_all[0])


def join_kernel(n, where_ref, chunks_ref, q_ref, kv_ref):
    sub = chunks_ref.shape[2]
    for k in range(n):
        at = pl.ds(k * sub, sub)
        q_ref[at] = chunks_ref[k, 0]
        kv_ref[0, at] = chunks_ref[k, 1]
        kv_ref[1, at] = chunks_ref[k, 2]


def unjoin_kernel(n, t, where_ref, attn_ref, dq_ref, dkv_ref, *refs):
    got, out_ref = refs[:t - 1], refs[t - 1]
    sub = out_ref.shape[2]
    for k in range(n):
        at = pl.ds(k * sub, sub)
        out_ref[k, 0] = attn_ref[at]
        out_ref[k, 1] = dq_ref[at]
        for a in range(2):
            total = dkv_ref[a, at].astype(F32)
            for other in got:
                total = total + other[a, at].astype(F32)
            out_ref[k, 2 + a] = total.astype(BF16)


def by_core_kernel(n, t, where_ref, chunks_ref, *refs):
    outs, heads_all = refs[:t], refs[t]
    core = where_ref[1]
    heads_here = heads_all.shape[0] // t
    for k in range(n):
        held, head = head_of(k, n // PLANES, heads_all.shape[0] // PLANES)
        if held:
            heads_all[head] = chunks_ref[k]
    for s in range(t):
        outs[s][...] = heads_all[pl.ds((core + s) % t * heads_here, heads_here)]


def seats_kernel(in_plane, where_ref, *refs):
    got, out_ref = refs[:in_plane], refs[in_plane]
    seat = where_ref[0] % in_plane
    for k in range(in_plane):
        out_ref[seat ^ k] = got[k][...]


def tile_kernel(in_plane, heads_plane, t, where_ref, *refs):
    attns, (grad_ref, own_ref), sends = refs[:in_plane], refs[in_plane:in_plane + 2], refs[in_plane + 2:-2]
    seats, total = refs[-2:]
    chip, core = where_ref[0], where_ref[1]
    seat = chip % in_plane
    plane = chip // in_plane
    step = pl.program_id(0)
    for k in range(in_plane):
        seats[seat ^ k] = attns[k][...]

    @pl.when(step == 0)
    def _():
        total[...] = jnp.zeros_like(total)

    grad = grad_ref[...]
    for j in range(heads_plane):
        total[pl.ds(j * HEAD, HEAD)] += dot(seats[(plane + j) % in_plane], grad, TN)

    @pl.when(step == pl.num_programs(0) - 1)
    def _():
        piece = own_ref.shape[0]
        if piece == total.shape[0]:
            own_ref[...] = total[...]
            sends[0][...] = total[...].astype(BF16)
            return
        own_ref[...] = total[pl.ds(pl.multiple_of(core * piece, piece), piece)]
        for s in range(1, t):
            at = pl.ds(pl.multiple_of((core + s) % t * piece, piece), piece)
            sends[s - 1][...] = total[at].astype(BF16)


def place_kernel(t, where_ref, *refs):
    parts, out_ref = refs[:t], refs[t]
    core = where_ref[1]
    piece = parts[0].shape[1]
    for s in range(t):
        at = pl.ds(pl.multiple_of((core + t - s) % t * piece, piece), piece)
        out_ref[at] = parts[s][0].astype(F32)


def unpack_kernel(t, where_ref, *refs):
    parts, outs = refs[:t], refs[t:]
    core = where_ref[1]
    heads_here, _, sub, _ = parts[0].shape
    for s in range(t):
        at = pl.ds(pl.multiple_of((core + t - s) % t * sub, sub), sub)
        for a in range(4):
            for h in range(heads_here):
                outs[a][at, pl.ds(h * HEAD, HEAD)] = parts[s][h, a]


def forward_kernel(t, tile, count, full_ref, kcnt_ref, kidx_ref, q_ref, *refs):
    parts, (out_ref, lse_ref, k_few, v_few, k_ref, v_ref) = refs[:2 * t], refs[2 * t:]
    row = pl.program_id(0)
    q = q_ref[...]

    @pl.when(row == 0)
    def _():
        join_parts(parts, k_ref, v_ref)

    def finish(s, v):
        top = jnp.max(s, axis=1, keepdims=True)
        p = jnp.exp2(s - top)
        mass = jnp.sum(p, axis=1, keepdims=True)
        out = dot(p.astype(BF16), v)
        out_ref[...] = (out / mass).astype(BF16)
        lse_ref[...] = jnp.broadcast_to(top + jnp.log2(mass), lse_ref.shape)

    scale = HEAD ** -0.5 * LOG2E

    @pl.when(full_ref[row] == 1)
    def _():
        keys = k_ref[...].reshape(-1, HEAD)
        finish(dot(q, keys, NT) * scale, v_ref[...].reshape(-1, HEAD))

    @pl.when(full_ref[row] == 0)
    def _():
        gather_tiles(k_ref, kidx_ref, row, k_few, tile, count)
        gather_tiles(v_ref, kidx_ref, row, v_few, tile, count)
        s = dot(q, k_few[...], NT) * scale
        column = lax.broadcasted_iota(jnp.int32, s.shape, 1)
        s = jnp.where(column < kcnt_ref[row] * tile, s, NEG_BIG)
        finish(s, v_few[...])


def backward_kernel(t, tile, count, full_ref, kcnt_ref, kidx_ref, q_ref, g_ref, o_ref, lse_ref, *refs):
    parts, dkv_refs = refs[:2 * t], refs[2 * t + 1:3 * t + 1]
    dq_ref = refs[2 * t]
    k_few, v_few, k_ref, v_ref, dk_acc, dv_acc = refs[3 * t + 1:]
    row = pl.program_id(0)
    last = pl.num_programs(0) - 1

    @pl.when(row == 0)
    def _():
        join_parts(parts, k_ref, v_ref)
        dk_acc[...] = jnp.zeros_like(dk_acc)
        dv_acc[...] = jnp.zeros_like(dv_acc)

    q = q_ref[...]
    g = g_ref[...]
    delta = jnp.sum(g.astype(F32) * o_ref[...].astype(F32), axis=1, keepdims=True)
    lse = lse_ref[:, :1]
    unit = HEAD ** -0.5
    scale = unit * LOG2E

    def gradients(keys, values, mask):
        s = dot(q, keys, NT)
        p = jnp.exp2(s * scale - lse)
        if mask is not None:
            p = jnp.where(mask(p.shape), p, 0.0)
        ds = (p * (dot(g, values, NT) - delta)).astype(BF16)
        dq_ref[...] = (dot(ds, keys) * unit).astype(BF16)
        return dot(ds, q, TN) * unit, dot(p.astype(BF16), g, TN)

    @pl.when(full_ref[row] == 1)
    def _():
        dk, dv = gradients(k_ref[...].reshape(-1, HEAD), v_ref[...].reshape(-1, HEAD), None)
        dk_acc[...] += dk.reshape(dk_acc.shape)
        dv_acc[...] += dv.reshape(dv_acc.shape)

    @pl.when(full_ref[row] == 0)
    def _():
        gather_tiles(k_ref, kidx_ref, row, k_few, tile, count)
        gather_tiles(v_ref, kidx_ref, row, v_few, tile, count)

        def mask(shape):
            return lax.broadcasted_iota(jnp.int32, shape, 1) < kcnt_ref[row] * tile

        dk, dv = gradients(k_few[...], v_few[...], mask)
        for j in range(count):
            at = kidx_ref[row, j]
            dk_acc[at] += dk[j * tile:(j + 1) * tile]
            dv_acc[at] += dv[j * tile:(j + 1) * tile]

    @pl.when(row == last)
    def _():
        tiles = dk_acc.shape[0] // t
        for s, dkv_ref in enumerate(dkv_refs):
            at = pl.ds(s * tiles, tiles)
            dkv_ref[0] = dk_acc[at].reshape(dkv_ref.shape[1:]).astype(BF16)
            dkv_ref[1] = dv_acc[at].reshape(dkv_ref.shape[1:]).astype(BF16)


def whole_block(shape):
    return pl.BlockSpec(shape, lambda *_: (0,) * len(shape))


def one_array(which, length):
    return pl.BlockSpec((1, length, HEAD), lambda *_: (which, 0, 0))


def simple_call(kernel, name, scalars, inputs, outputs, scratch=()):
    size = sum(2 * math.prod(x.shape) for x in list(inputs) + list(outputs))
    return pl.pallas_call(
        kernel,
        grid_spec=pltpu.PrefetchScalarGridSpec(
            num_scalar_prefetch=1,
            grid=(1,),
            in_specs=[whole_block(x.shape) for x in inputs],
            out_specs=[whole_block(x.shape) for x in outputs],
            scratch_shapes=scratch,
        ),
        out_shape=outputs,
        compiler_params=pltpu.CompilerParams(vmem_limit_bytes=48 * 2**20),
        cost_estimate=pl.CostEstimate(flops=0, bytes_accessed=2 * size, transcendentals=0),
        name=name,
    )(scalars, *inputs)


def shifts(t, s):
    return [(c, (c + s) % t) for c in range(t)]


def place_xor_kernel(place_ref, *refs):
    sources, out_ref = refs[:-1], refs[-1]
    step = pl.program_id(0)
    for u in range(2):
        own, beside, above, upper, lower = sources[5 * u:5 * u + 5]
        for v, source in enumerate((own, beside, above)):
            @pl.when(step == 4 * u + v)
            def _(source=source):
                out_ref[...] = source[...].astype(F32)

        @pl.when(step == 4 * u + 3)
        def _(upper=upper, lower=lower):
            middle = upper.shape[0]
            out_ref[:middle] = upper[...].astype(F32)
            out_ref[middle:] = lower[...].astype(F32)


def gather_tiles_by_core(n, t, tile_sum, chip, core):
    in_plane = n // PLANES
    plane, seat = chip // in_plane, chip % in_plane
    tile_rows, cols = tile_sum.shape
    across = [
        (i * t + c, (i ^ 2 * in_plane) * t + c)
        for i in range(n) for c in range(t) if i // in_plane // 2 == c
    ]
    from_half = lax.ppermute(tile_sum, ("ctx", "tp"), across)

    def swap(x, k):
        return lax.ppermute(x, "ctx", [(i, i ^ k) for i in range(n)])

    first = jnp.where(plane // 2 == core, tile_sum, from_half)
    second = swap(first, in_plane)
    middle = tile_rows // 2
    sources = []
    for mine in (first, second):
        beside, above = swap(mine, 1), swap(mine, 2)
        sources += [mine, beside, above, swap(beside[:middle], 2), swap(above[middle:], 1)]
    place = jnp.stack([plane % 2, seat]).astype(jnp.int32)
    return pl.pallas_call(
        place_xor_kernel,
        grid_spec=pltpu.PrefetchScalarGridSpec(
            num_scalar_prefetch=1,
            grid=(8,),
            in_specs=[whole_block(x.shape) for x in sources],
            out_specs=pl.BlockSpec(
                (tile_rows, cols), lambda s, place: (s // 4 ^ place[0], s % 4 ^ place[1])
            ),
        ),
        out_shape=jax.ShapeDtypeStruct((2 * tile_rows, in_plane * cols), F32),
        compiler_params=pltpu.CompilerParams(vmem_limit_bytes=48 * 2**20),
        cost_estimate=pl.CostEstimate(flops=0, bytes_accessed=2**24, transcendentals=0),
        name="place",
    )(place, *sources)


def per_device(n, t, queries, key_vectors, value_vectors, out_weight, out_grad, block_segment):
    rows, width = queries.shape
    heads_here = width // HEAD
    heads = heads_here * t
    sub = rows // t
    tile = min(sub, BLK)
    per_chunk = sub // tile
    core = lax.axis_index("tp")
    chip = lax.axis_index("ctx")
    in_plane = n // PLANES
    heads_plane = heads // PLANES
    seat = chip % in_plane

    def tp_swap(pick):
        got = [pick(core)]
        for s in range(1, t):
            got.append(lax.ppermute(pick((core + s) % t), "tp", shifts(t, s)))
        return [lax.select_n((core - p) % t, *got) for p in range(t)]

    def tp_gather(x):
        return tp_swap(lambda _: x)

    def shape(*dims):
        return jax.ShapeDtypeStruct(dims, BF16)

    where = jnp.stack([chip, core]).astype(jnp.int32)
    held = [(i % in_plane - i // in_plane) % in_plane < heads_plane for i in range(n)]

    chunk_row = jnp.arange(n)[:, None] * rows + jnp.arange(per_chunk)[None, :] * tile

    def tile_segments(part):
        return jnp.take(block_segment, ((chunk_row + part * sub) // BLK).reshape(-1))

    seg_parts = [tile_segments((core - s) % t) for s in range(t)]
    seg_q = seg_parts[0]
    seg_k = jnp.concatenate(seg_parts)
    full = (seg_q == 0) | (seg_q == TARGET)
    permitted = (seg_k[None] == 0) | (seg_k[None] == seg_q[:, None])
    total_blocks = block_segment.shape[0]
    count = (TXT_BLK + -(-(total_blocks - TXT_BLK) // RUNS)) * (BLK // tile)
    kcnt = jnp.sum(permitted.astype(jnp.int32), axis=1)
    tiles_k = seg_k.shape[0]
    ids = jnp.arange(tiles_k)
    place = jnp.sum((permitted[:, None, :] & (ids[None, None, :] < ids[None, :, None])).astype(jnp.int32), axis=2)
    hit = permitted[:, None, :] & (place[:, None, :] == jnp.arange(count)[None, :, None])
    kidx = jnp.sum(jnp.where(hit, ids[None, None, :], 0), axis=2).astype(jnp.int32)
    full = full.astype(jnp.int32)

    def other_rows(*arrays):
        return [
            lax.ppermute(
                jnp.stack([
                    lax.dynamic_slice_in_dim(x, (core + s) % t * sub, sub, 0) for x in arrays
                ]),
                "tp", shifts(t, s),
            )
            for s in range(1, t)
        ]

    got_qkv = other_rows(queries, key_vectors, value_vectors)

    half = out_grad.shape[1]
    model = half * t
    full_grad = jnp.concatenate(tp_gather(out_grad), axis=1)
    grad_attn = dot(full_grad, out_weight, NT).astype(BF16)
    got_g = other_rows(grad_attn)

    cols = model // in_plane
    mine = lax.dynamic_slice_in_dim(full_grad, core * sub, sub, 0)
    plane_got = [lax.dynamic_slice_in_dim(mine, seat * cols, cols, 1)]
    for k in range(1, in_plane):
        there = lax.dynamic_slice_in_dim(mine, (seat ^ k) * cols, cols, 1)
        plane_got.append(lax.ppermute(there, "ctx", [(i, i ^ k) for i in range(n)]))
    (plane_grad,) = simple_call(
        functools.partial(seats_kernel, in_plane), "seats", where, plane_got, [shape(in_plane, sub, cols)]
    )
    def pack(arrays, got):
        (sent,) = simple_call(
            functools.partial(pack_kernel, n, t, len(arrays)), "pack", where,
            arrays + got, [shape(n, len(arrays), sub, HEAD)],
            [pltpu.VMEM((heads, len(arrays), sub, HEAD), BF16)],
        )
        return sent

    sent_qkv = pack([queries, key_vectors, value_vectors], got_qkv)
    sent_g = pack([grad_attn], got_g)
    chunks = lax.all_to_all(sent_qkv, "ctx", 0, 0, tiled=True)
    chunks, sent_g, plane_grad = lax.optimization_barrier((chunks, sent_g, plane_grad))
    lines = [[a * in_plane + b for a in range(PLANES)] for b in range(in_plane)]
    slice_grad = lax.all_gather(plane_grad, "ctx", axis_index_groups=lines)
    slice_grad = slice_grad.reshape(n * sub, cols)
    g_rows = lax.all_to_all(sent_g, "ctx", 0, 0, tiled=True).reshape(n * sub, HEAD)
    length = n * sub
    q_rows, kv = simple_call(
        functools.partial(join_kernel, n), "join", where, [chunks], [shape(length, HEAD), shape(2, length, HEAD)]
    )
    kv_all = [kv] + [lax.ppermute(kv, "tp", shifts(t, s)) for s in range(1, t)]

    tiles_q = n * per_chunk
    few = [pltpu.VMEM((count * tile, HEAD), BF16)] * 2 + [pltpu.VMEM((tiles_k, tile, HEAD), BF16)] * 2
    params = pltpu.CompilerParams(vmem_limit_bytes=48 * 2**20)
    part_blocks = [one_array(0, length), one_array(1, length)] * t
    part_arrays = [a for pack in kv_all for a in (pack, pack)]
    row_block = pl.BlockSpec((tile, HEAD), lambda r, *_: (r, 0))
    attn, lse = pl.pallas_call(
        functools.partial(forward_kernel, t, tile, count),
        grid_spec=pltpu.PrefetchScalarGridSpec(
            num_scalar_prefetch=3,
            grid=(tiles_q,),
            in_specs=[row_block] + part_blocks,
            out_specs=[row_block, row_block],
            scratch_shapes=few,
        ),
        out_shape=[shape(length, HEAD), jax.ShapeDtypeStruct((length, HEAD), F32)],
        compiler_params=params,
        cost_estimate=pl.CostEstimate(flops=16 * 10**9, bytes_accessed=5 * 2**20, transcendentals=2**22),
        name="forward",
    )(full, kcnt, kidx, q_rows, *part_arrays)

    travel = [attn] + [
        lax.ppermute(attn, "ctx", [(i, i ^ k) for i in range(n) if held[i]]) for k in range(1, in_plane)
    ]
    dq, *dkv = pl.pallas_call(
        functools.partial(backward_kernel, t, tile, count),
        grid_spec=pltpu.PrefetchScalarGridSpec(
            num_scalar_prefetch=3,
            grid=(tiles_q,),
            in_specs=[row_block] * 4 + part_blocks,
            out_specs=[row_block] + [whole_block((2, length, HEAD))] * t,
            scratch_shapes=few + [pltpu.VMEM((tiles_k, tile, HEAD), F32)] * 2,
        ),
        out_shape=[shape(length, HEAD)] + [shape(2, length, HEAD)] * t,
        compiler_params=params,
        cost_estimate=pl.CostEstimate(flops=20 * 10**9, bytes_accessed=8 * 2**20, transcendentals=2**22),
        name="backward",
    )(full, kcnt, kidx, q_rows, g_rows, attn, lse, *part_arrays)

    *travel, dq = lax.optimization_barrier((*travel, dq))

    tile_rows = heads_plane * HEAD
    by_core = in_plane == 4 and t == 2
    piece = tile_rows if by_core else tile_rows // t
    step_rows = length // 4
    tile_own, *tile_sends = pl.pallas_call(
        functools.partial(tile_kernel, in_plane, heads_plane, t),
        grid_spec=pltpu.PrefetchScalarGridSpec(
            num_scalar_prefetch=1,
            grid=(4,),
            in_specs=[pl.BlockSpec((step_rows, HEAD), lambda r, *_: (r, 0))] * in_plane
            + [pl.BlockSpec((step_rows, cols), lambda r, *_: (r, 0))],
            out_specs=[whole_block((piece, cols))] * t,
            scratch_shapes=[
                pltpu.VMEM((in_plane, step_rows, HEAD), BF16), pltpu.VMEM((tile_rows, cols), F32)
            ],
        ),
        out_shape=[jax.ShapeDtypeStruct((piece, cols), F32)] + [shape(piece, cols)] * (t - 1),
        compiler_params=params,
        cost_estimate=pl.CostEstimate(flops=5 * 10**9, bytes_accessed=2**22, transcendentals=0),
        name="tile",
    )(where, *travel, slice_grad)
    tile_sum = tile_own
    for s in range(1, t):
        tile_sum = tile_sum + lax.ppermute(tile_sends[s - 1], "tp", shifts(t, s)).astype(F32)
    if by_core:
        grad_weight = gather_tiles_by_core(n, t, tile_sum.astype(BF16), chip, core)
    else:
        tiles = lax.all_gather(tile_sum.astype(BF16), "ctx")
        here = n // t
        tiles_core = [tiles] + [
            lax.ppermute(
                lax.dynamic_slice_in_dim(tiles, (core + s) % t * here, here, 0), "tp", shifts(t, s)
            )
            for s in range(1, t)
        ]
        grad_weight = pl.pallas_call(
            functools.partial(place_kernel, t),
            grid_spec=pltpu.PrefetchScalarGridSpec(
                num_scalar_prefetch=1,
                grid=(here,),
                in_specs=[pl.BlockSpec((1, piece, cols), lambda r, where: (where[1] * here + r, 0, 0))]
                + [pl.BlockSpec((1, piece, cols), lambda r, *_: (r, 0, 0))] * (t - 1),
                out_specs=pl.BlockSpec((tile_rows, cols), lambda r, *_: (r // in_plane, r % in_plane)),
            ),
            out_shape=jax.ShapeDtypeStruct((width, model), F32),
            compiler_params=params,
            cost_estimate=pl.CostEstimate(flops=0, bytes_accessed=2**24, transcendentals=0),
            name="place",
        )(where, *tiles_core)

    got_dkv = [
        lax.ppermute(dkv[s], "tp", [(c, (c - s) % t) for c in range(t)]) for s in range(1, t)
    ]
    (sent,) = simple_call(
        functools.partial(unjoin_kernel, n, t), "unjoin", where,
        [attn, dq, dkv[0]] + got_dkv, [shape(n, 4, sub, HEAD)],
    )
    chunks = lax.all_to_all(sent, "ctx", 0, 0, tiled=True)
    mine = simple_call(
        functools.partial(by_core_kernel, n, t), "by_core", where, [chunks],
        [shape(heads_here, 4, sub, HEAD)] * t, [pltpu.VMEM((heads, 4, sub, HEAD), BF16)],
    )
    parts = [mine[0]] + [lax.ppermute(mine[s], "tp", shifts(t, s)) for s in range(1, t)]
    attention, grad_queries, grad_keys, grad_values = simple_call(
        functools.partial(unpack_kernel, t), "unpack", where, parts, [shape(rows, width)] * 4
    )
    projected = dot(attention, out_weight)
    own = lax.dynamic_slice_in_dim(projected, core * half, half, 1)
    for s in range(1, t):
        there = lax.dynamic_slice_in_dim(projected, (core + s) % t * half, half, 1)
        own = own + lax.ppermute(there.astype(BF16), "tp", shifts(t, s)).astype(F32)
    attention_out = own.astype(BF16)

    return attention_out, grad_queries, grad_keys, grad_values, grad_weight


def solution(mesh):
    n, t = mesh.shape["ctx"], mesh.shape["tp"]
    in_specs = (P("ctx", "tp"), P("ctx", "tp"), P("ctx", "tp"), P("tp", None), P("ctx", "tp"), P())
    out_specs = (P("ctx", "tp"), P("ctx", "tp"), P("ctx", "tp"), P("ctx", "tp"), P("tp", None))
    return jax.shard_map(
        functools.partial(per_device, n, t), mesh=mesh, in_specs=in_specs, out_specs=out_specs, check_vma=False
    )
```

```python
import functools
import math

import jax
import jax.numpy as jnp
from jax import lax
from jax.experimental import pallas as pl
from jax.experimental.pallas import tpu as pltpu
from jax.sharding import PartitionSpec as P

HEAD = 128
BLK = 128
TXT_BLK = 4
RUNS = 5
TARGET = 5
PLANES = 4
LOG2E = math.log2(math.e)
NEG_BIG = -1e30

NT = (((1,), (1,)), ((), ()))
TN = (((0,), (0,)), ((), ()))
F32 = jnp.float32
BF16 = jnp.bfloat16


def dot(a, b, dims=(((1,), (0,)), ((), ()))):
    return lax.dot_general(a, b, dims, preferred_element_type=F32)


def gather_tiles(k_ref, kidx_ref, row, dst, tile, count):
    for j in range(count):
        dst[pl.ds(j * tile, tile), :] = k_ref[kidx_ref[row, j]]


def join_parts(parts, k_all, v_all):
    shape = (k_all.shape[0] // (len(parts) // 2),) + k_all.shape[1:]
    for s in range(len(parts) // 2):
        at = pl.ds(s * shape[0], shape[0])
        k_all[at] = parts[2 * s][...].reshape(shape)
        v_all[at] = parts[2 * s + 1][...].reshape(shape)


def head_of(chip, in_plane, heads_plane):
    place = (chip % in_plane - chip // in_plane) % in_plane
    return place < heads_plane, chip // in_plane * heads_plane + min(place, heads_plane - 1)


def pack_kernel(n, t, count, where_ref, *refs):
    arrays, got, (out_ref, heads_all) = refs[:count], refs[count:count + t - 1], refs[count + t - 1:]
    core = where_ref[1]
    sub = heads_all.shape[2]
    heads_here = heads_all.shape[0] // t
    for a in range(count):
        for h in range(heads_here):
            column = pl.ds(h * HEAD, HEAD)
            heads_all[core * heads_here + h, a] = arrays[a][pl.ds(core * sub, sub), column]
            for s in range(1, t):
                first = (core + t - s) % t * heads_here
                heads_all[first + h, a] = got[s - 1][a, :, column]
    for k in range(n):
        held, head = head_of(k, n // PLANES, heads_all.shape[0] // PLANES)
        out_ref[k] = heads_all[head] if held else jnp.zeros_like(heads_all[0])


def join_kernel(n, where_ref, chunks_ref, q_ref, kv_ref):
    sub = chunks_ref.shape[2]
    for k in range(n):
        at = pl.ds(k * sub, sub)
        q_ref[at] = chunks_ref[k, 0]
        kv_ref[0, at] = chunks_ref[k, 1]
        kv_ref[1, at] = chunks_ref[k, 2]


def unjoin_kernel(n, t, where_ref, attn_ref, dq_ref, dkv_ref, *refs):
    got, out_ref = refs[:t - 1], refs[t - 1]
    sub = out_ref.shape[2]
    for k in range(n):
        at = pl.ds(k * sub, sub)
        out_ref[k, 0] = attn_ref[at]
        out_ref[k, 1] = dq_ref[at]
        for a in range(2):
            total = dkv_ref[a, at].astype(F32)
            for other in got:
                total = total + other[a, at].astype(F32)
            out_ref[k, 2 + a] = total.astype(BF16)


def by_core_kernel(n, t, where_ref, chunks_ref, *refs):
    outs, heads_all = refs[:t], refs[t]
    core = where_ref[1]
    heads_here = heads_all.shape[0] // t
    for k in range(n):
        held, head = head_of(k, n // PLANES, heads_all.shape[0] // PLANES)
        if held:
            heads_all[head] = chunks_ref[k]
    for s in range(t):
        outs[s][...] = heads_all[pl.ds((core + s) % t * heads_here, heads_here)]


def seats_kernel(in_plane, where_ref, *refs):
    got, out_ref = refs[:in_plane], refs[in_plane]
    seat = where_ref[0] % in_plane
    for k in range(in_plane):
        out_ref[seat ^ k] = got[k][...]


def tile_kernel(in_plane, heads_plane, t, where_ref, *refs):
    attns, (grad_ref, own_ref), sends = refs[:in_plane], refs[in_plane:in_plane + 2], refs[in_plane + 2:-2]
    seats, total = refs[-2:]
    chip, core = where_ref[0], where_ref[1]
    seat = chip % in_plane
    plane = chip // in_plane
    step = pl.program_id(0)
    for k in range(in_plane):
        seats[seat ^ k] = attns[k][...]

    @pl.when(step == 0)
    def _():
        total[...] = jnp.zeros_like(total)

    grad = grad_ref[...]
    for j in range(heads_plane):
        total[pl.ds(j * HEAD, HEAD)] += dot(seats[(plane + j) % in_plane], grad, TN)

    @pl.when(step == pl.num_programs(0) - 1)
    def _():
        piece = own_ref.shape[0]
        if piece == total.shape[0]:
            own_ref[...] = total[...]
            sends[0][...] = total[...].astype(BF16)
            return
        own_ref[...] = total[pl.ds(pl.multiple_of(core * piece, piece), piece)]
        for s in range(1, t):
            at = pl.ds(pl.multiple_of((core + s) % t * piece, piece), piece)
            sends[s - 1][...] = total[at].astype(BF16)


def place_kernel(t, where_ref, *refs):
    parts, out_ref = refs[:t], refs[t]
    core = where_ref[1]
    piece = parts[0].shape[1]
    for s in range(t):
        at = pl.ds(pl.multiple_of((core + t - s) % t * piece, piece), piece)
        out_ref[at] = parts[s][0].astype(F32)


def unpack_kernel(t, where_ref, *refs):
    parts, outs = refs[:t], refs[t:]
    core = where_ref[1]
    heads_here, _, sub, _ = parts[0].shape
    for s in range(t):
        at = pl.ds(pl.multiple_of((core + t - s) % t * sub, sub), sub)
        for a in range(4):
            for h in range(heads_here):
                outs[a][at, pl.ds(h * HEAD, HEAD)] = parts[s][h, a]


def forward_kernel(t, tile, count, full_ref, kcnt_ref, kidx_ref, q_ref, *refs):
    parts, (out_ref, lse_ref, k_few, v_few, k_ref, v_ref) = refs[:2 * t], refs[2 * t:]
    row = pl.program_id(0)
    q = q_ref[...]

    @pl.when(row == 0)
    def _():
        join_parts(parts, k_ref, v_ref)

    def finish(s, v):
        top = jnp.max(s, axis=1, keepdims=True)
        p = jnp.exp2(s - top)
        mass = jnp.sum(p, axis=1, keepdims=True)
        out = dot(p.astype(BF16), v)
        out_ref[...] = (out / mass).astype(BF16)
        lse_ref[...] = jnp.broadcast_to(top + jnp.log2(mass), lse_ref.shape)

    scale = HEAD ** -0.5 * LOG2E

    @pl.when(full_ref[row] == 1)
    def _():
        keys = k_ref[...].reshape(-1, HEAD)
        finish(dot(q, keys, NT) * scale, v_ref[...].reshape(-1, HEAD))

    @pl.when(full_ref[row] == 0)
    def _():
        gather_tiles(k_ref, kidx_ref, row, k_few, tile, count)
        gather_tiles(v_ref, kidx_ref, row, v_few, tile, count)
        s = dot(q, k_few[...], NT) * scale
        column = lax.broadcasted_iota(jnp.int32, s.shape, 1)
        s = jnp.where(column < kcnt_ref[row] * tile, s, NEG_BIG)
        finish(s, v_few[...])


def backward_kernel(t, tile, count, full_ref, kcnt_ref, kidx_ref, q_ref, g_ref, o_ref, lse_ref, *refs):
    parts, dkv_refs = refs[:2 * t], refs[2 * t + 1:3 * t + 1]
    dq_ref = refs[2 * t]
    k_few, v_few, k_ref, v_ref, dk_acc, dv_acc = refs[3 * t + 1:]
    row = pl.program_id(0)
    last = pl.num_programs(0) - 1

    @pl.when(row == 0)
    def _():
        join_parts(parts, k_ref, v_ref)
        dk_acc[...] = jnp.zeros_like(dk_acc)
        dv_acc[...] = jnp.zeros_like(dv_acc)

    q = q_ref[...]
    g = g_ref[...]
    delta = jnp.sum(g.astype(F32) * o_ref[...].astype(F32), axis=1, keepdims=True)
    lse = lse_ref[:, :1]
    unit = HEAD ** -0.5
    scale = unit * LOG2E

    def gradients(keys, values, mask):
        s = dot(q, keys, NT)
        p = jnp.exp2(s * scale - lse)
        if mask is not None:
            p = jnp.where(mask(p.shape), p, 0.0)
        ds = (p * (dot(g, values, NT) - delta)).astype(BF16)
        dq_ref[...] = (dot(ds, keys) * unit).astype(BF16)
        return dot(ds, q, TN) * unit, dot(p.astype(BF16), g, TN)

    @pl.when(full_ref[row] == 1)
    def _():
        dk, dv = gradients(k_ref[...].reshape(-1, HEAD), v_ref[...].reshape(-1, HEAD), None)
        dk_acc[...] += dk.reshape(dk_acc.shape)
        dv_acc[...] += dv.reshape(dv_acc.shape)

    @pl.when(full_ref[row] == 0)
    def _():
        gather_tiles(k_ref, kidx_ref, row, k_few, tile, count)
        gather_tiles(v_ref, kidx_ref, row, v_few, tile, count)

        def mask(shape):
            return lax.broadcasted_iota(jnp.int32, shape, 1) < kcnt_ref[row] * tile

        dk, dv = gradients(k_few[...], v_few[...], mask)
        for j in range(count):
            at = kidx_ref[row, j]
            dk_acc[at] += dk[j * tile:(j + 1) * tile]
            dv_acc[at] += dv[j * tile:(j + 1) * tile]

    @pl.when(row == last)
    def _():
        tiles = dk_acc.shape[0] // t
        for s, dkv_ref in enumerate(dkv_refs):
            at = pl.ds(s * tiles, tiles)
            dkv_ref[0] = dk_acc[at].reshape(dkv_ref.shape[1:]).astype(BF16)
            dkv_ref[1] = dv_acc[at].reshape(dkv_ref.shape[1:]).astype(BF16)


def whole_block(shape):
    return pl.BlockSpec(shape, lambda *_: (0,) * len(shape))


def one_array(which, length):
    return pl.BlockSpec((1, length, HEAD), lambda *_: (which, 0, 0))


def simple_call(kernel, name, scalars, inputs, outputs, scratch=()):
    size = sum(2 * math.prod(x.shape) for x in list(inputs) + list(outputs))
    return pl.pallas_call(
        kernel,
        grid_spec=pltpu.PrefetchScalarGridSpec(
            num_scalar_prefetch=1,
            grid=(1,),
            in_specs=[whole_block(x.shape) for x in inputs],
            out_specs=[whole_block(x.shape) for x in outputs],
            scratch_shapes=scratch,
        ),
        out_shape=outputs,
        compiler_params=pltpu.CompilerParams(vmem_limit_bytes=48 * 2**20),
        cost_estimate=pl.CostEstimate(flops=0, bytes_accessed=2 * size, transcendentals=0),
        name=name,
    )(scalars, *inputs)


def shifts(t, s):
    return [(c, (c + s) % t) for c in range(t)]


def place_xor_kernel(place_ref, *refs):
    sources, out_ref = refs[:-1], refs[-1]
    step = pl.program_id(0)
    for u in range(2):
        own, beside, above, upper, lower = sources[5 * u:5 * u + 5]
        for v, source in enumerate((own, beside, above)):
            @pl.when(step == 4 * u + v)
            def _(source=source):
                out_ref[...] = source[...].astype(F32)

        @pl.when(step == 4 * u + 3)
        def _(upper=upper, lower=lower):
            middle = upper.shape[0]
            out_ref[:middle] = upper[...].astype(F32)
            out_ref[middle:] = lower[...].astype(F32)


def gather_tiles_by_core(n, t, tile_sum, chip, core, beside_chunks):
    in_plane = n // PLANES
    plane, seat = chip // in_plane, chip % in_plane
    tile_rows, cols = tile_sum.shape
    across = [
        (i * t + c, (i ^ 2 * in_plane) * t + c)
        for i in range(n) for c in range(t) if i // in_plane // 2 == c
    ]
    from_half = lax.ppermute(tile_sum, ("ctx", "tp"), across)

    def swap(x, k):
        return lax.ppermute(x, "ctx", [(i, i ^ k) for i in range(n)])

    first = jnp.where(plane // 2 == core, tile_sum, from_half)
    second = swap(first, in_plane)
    beside, above = swap(first, 1), swap(first, 2)
    second, beside, above, beside_chunks = lax.optimization_barrier((second, beside, above, beside_chunks))
    middle = tile_rows // 2
    sources = [first, beside, above, swap(beside[:middle], 2), swap(above[middle:], 1)]
    beside, above = swap(second, 1), swap(second, 2)
    sources += [second, beside, above, swap(beside[:middle], 2), swap(above[middle:], 1)]
    place = jnp.stack([plane % 2, seat]).astype(jnp.int32)
    return pl.pallas_call(
        place_xor_kernel,
        grid_spec=pltpu.PrefetchScalarGridSpec(
            num_scalar_prefetch=1,
            grid=(8,),
            in_specs=[whole_block(x.shape) for x in sources],
            out_specs=pl.BlockSpec(
                (tile_rows, cols), lambda s, place: (s // 4 ^ place[0], s % 4 ^ place[1])
            ),
        ),
        out_shape=jax.ShapeDtypeStruct((2 * tile_rows, in_plane * cols), F32),
        compiler_params=pltpu.CompilerParams(vmem_limit_bytes=48 * 2**20),
        cost_estimate=pl.CostEstimate(flops=0, bytes_accessed=2**24, transcendentals=0),
        name="place",
    )(place, *sources), beside_chunks


def per_device(n, t, queries, key_vectors, value_vectors, out_weight, out_grad, block_segment):
    rows, width = queries.shape
    heads_here = width // HEAD
    heads = heads_here * t
    sub = rows // t
    tile = min(sub, BLK)
    per_chunk = sub // tile
    core = lax.axis_index("tp")
    chip = lax.axis_index("ctx")
    in_plane = n // PLANES
    heads_plane = heads // PLANES
    seat = chip % in_plane

    def tp_swap(pick):
        got = [pick(core)]
        for s in range(1, t):
            got.append(lax.ppermute(pick((core + s) % t), "tp", shifts(t, s)))
        return [lax.select_n((core - p) % t, *got) for p in range(t)]

    def tp_gather(x):
        return tp_swap(lambda _: x)

    def shape(*dims):
        return jax.ShapeDtypeStruct(dims, BF16)

    where = jnp.stack([chip, core]).astype(jnp.int32)
    held = [(i % in_plane - i // in_plane) % in_plane < heads_plane for i in range(n)]

    chunk_row = jnp.arange(n)[:, None] * rows + jnp.arange(per_chunk)[None, :] * tile

    def tile_segments(part):
        return jnp.take(block_segment, ((chunk_row + part * sub) // BLK).reshape(-1))

    seg_parts = [tile_segments((core - s) % t) for s in range(t)]
    seg_q = seg_parts[0]
    seg_k = jnp.concatenate(seg_parts)
    full = (seg_q == 0) | (seg_q == TARGET)
    permitted = (seg_k[None] == 0) | (seg_k[None] == seg_q[:, None])
    total_blocks = block_segment.shape[0]
    count = (TXT_BLK + -(-(total_blocks - TXT_BLK) // RUNS)) * (BLK // tile)
    kcnt = jnp.sum(permitted.astype(jnp.int32), axis=1)
    tiles_k = seg_k.shape[0]
    ids = jnp.arange(tiles_k)
    place = jnp.sum((permitted[:, None, :] & (ids[None, None, :] < ids[None, :, None])).astype(jnp.int32), axis=2)
    hit = permitted[:, None, :] & (place[:, None, :] == jnp.arange(count)[None, :, None])
    kidx = jnp.sum(jnp.where(hit, ids[None, None, :], 0), axis=2).astype(jnp.int32)
    full = full.astype(jnp.int32)

    def other_rows(*arrays):
        return [
            lax.ppermute(
                jnp.stack([
                    lax.dynamic_slice_in_dim(x, (core + s) % t * sub, sub, 0) for x in arrays
                ]),
                "tp", shifts(t, s),
            )
            for s in range(1, t)
        ]

    got_qkv = other_rows(queries, key_vectors, value_vectors)

    half = out_grad.shape[1]
    model = half * t
    full_grad = jnp.concatenate(tp_gather(out_grad), axis=1)
    grad_attn = dot(full_grad, out_weight, NT).astype(BF16)
    got_g = other_rows(grad_attn)

    cols = model // in_plane
    mine = lax.dynamic_slice_in_dim(full_grad, core * sub, sub, 0)
    plane_got = [lax.dynamic_slice_in_dim(mine, seat * cols, cols, 1)]
    for k in range(1, in_plane):
        there = lax.dynamic_slice_in_dim(mine, (seat ^ k) * cols, cols, 1)
        plane_got.append(lax.ppermute(there, "ctx", [(i, i ^ k) for i in range(n)]))
    (plane_grad,) = simple_call(
        functools.partial(seats_kernel, in_plane), "seats", where, plane_got, [shape(in_plane, sub, cols)]
    )
    def pack(arrays, got):
        (sent,) = simple_call(
            functools.partial(pack_kernel, n, t, len(arrays)), "pack", where,
            arrays + got, [shape(n, len(arrays), sub, HEAD)],
            [pltpu.VMEM((heads, len(arrays), sub, HEAD), BF16)],
        )
        return sent

    sent_qkv = pack([queries, key_vectors, value_vectors], got_qkv)
    sent_g = pack([grad_attn], got_g)
    chunks = lax.all_to_all(sent_qkv, "ctx", 0, 0, tiled=True)
    chunks, sent_g, plane_grad = lax.optimization_barrier((chunks, sent_g, plane_grad))
    lines = [[a * in_plane + b for a in range(PLANES)] for b in range(in_plane)]
    slice_grad = lax.all_gather(plane_grad, "ctx", axis_index_groups=lines)
    slice_grad = slice_grad.reshape(n * sub, cols)
    g_rows = lax.all_to_all(sent_g, "ctx", 0, 0, tiled=True).reshape(n * sub, HEAD)
    length = n * sub
    q_rows, kv = simple_call(
        functools.partial(join_kernel, n), "join", where, [chunks], [shape(length, HEAD), shape(2, length, HEAD)]
    )
    kv_all = [kv] + [lax.ppermute(kv, "tp", shifts(t, s)) for s in range(1, t)]

    tiles_q = n * per_chunk
    few = [pltpu.VMEM((count * tile, HEAD), BF16)] * 2 + [pltpu.VMEM((tiles_k, tile, HEAD), BF16)] * 2
    params = pltpu.CompilerParams(vmem_limit_bytes=48 * 2**20)
    part_blocks = [one_array(0, length), one_array(1, length)] * t
    part_arrays = [a for pack in kv_all for a in (pack, pack)]
    row_block = pl.BlockSpec((tile, HEAD), lambda r, *_: (r, 0))
    attn, lse = pl.pallas_call(
        functools.partial(forward_kernel, t, tile, count),
        grid_spec=pltpu.PrefetchScalarGridSpec(
            num_scalar_prefetch=3,
            grid=(tiles_q,),
            in_specs=[row_block] + part_blocks,
            out_specs=[row_block, row_block],
            scratch_shapes=few,
        ),
        out_shape=[shape(length, HEAD), jax.ShapeDtypeStruct((length, HEAD), F32)],
        compiler_params=params,
        cost_estimate=pl.CostEstimate(flops=16 * 10**9, bytes_accessed=5 * 2**20, transcendentals=2**22),
        name="forward",
    )(full, kcnt, kidx, q_rows, *part_arrays)

    travel = [attn] + [
        lax.ppermute(attn, "ctx", [(i, i ^ k) for i in range(n) if held[i]]) for k in range(1, in_plane)
    ]
    *travel, attn = lax.optimization_barrier((*travel, attn))

    dq, *dkv = pl.pallas_call(
        functools.partial(backward_kernel, t, tile, count),
        grid_spec=pltpu.PrefetchScalarGridSpec(
            num_scalar_prefetch=3,
            grid=(tiles_q,),
            in_specs=[row_block] * 4 + part_blocks,
            out_specs=[row_block] + [whole_block((2, length, HEAD))] * t,
            scratch_shapes=few + [pltpu.VMEM((tiles_k, tile, HEAD), F32)] * 2,
        ),
        out_shape=[shape(length, HEAD)] + [shape(2, length, HEAD)] * t,
        compiler_params=params,
        cost_estimate=pl.CostEstimate(flops=20 * 10**9, bytes_accessed=8 * 2**20, transcendentals=2**22),
        name="backward",
    )(full, kcnt, kidx, q_rows, g_rows, attn, lse, *part_arrays)

    got_dkv = [
        lax.ppermute(dkv[s], "tp", [(c, (c - s) % t) for c in range(t)]) for s in range(1, t)
    ]
    (sent,) = simple_call(
        functools.partial(unjoin_kernel, n, t), "unjoin", where,
        [attn, dq, dkv[0]] + got_dkv, [shape(n, 4, sub, HEAD)],
    )
    chunks = lax.all_to_all(sent, "ctx", 0, 0, tiled=True)

    tile_rows = heads_plane * HEAD
    by_core = in_plane == 4 and t == 2
    piece = tile_rows if by_core else tile_rows // t
    step_rows = length // 4
    tile_own, *tile_sends = pl.pallas_call(
        functools.partial(tile_kernel, in_plane, heads_plane, t),
        grid_spec=pltpu.PrefetchScalarGridSpec(
            num_scalar_prefetch=1,
            grid=(4,),
            in_specs=[pl.BlockSpec((step_rows, HEAD), lambda r, *_: (r, 0))] * in_plane
            + [pl.BlockSpec((step_rows, cols), lambda r, *_: (r, 0))],
            out_specs=[whole_block((piece, cols))] * t,
            scratch_shapes=[
                pltpu.VMEM((in_plane, step_rows, HEAD), BF16), pltpu.VMEM((tile_rows, cols), F32)
            ],
        ),
        out_shape=[jax.ShapeDtypeStruct((piece, cols), F32)] + [shape(piece, cols)] * (t - 1),
        compiler_params=params,
        cost_estimate=pl.CostEstimate(flops=5 * 10**9, bytes_accessed=2**22, transcendentals=0),
        name="tile",
    )(where, *travel, slice_grad)
    tile_sum = tile_own
    for s in range(1, t):
        tile_sum = tile_sum + lax.ppermute(tile_sends[s - 1], "tp", shifts(t, s)).astype(F32)
    if by_core:
        grad_weight, chunks = gather_tiles_by_core(n, t, tile_sum.astype(BF16), chip, core, chunks)
    else:
        tiles = lax.all_gather(tile_sum.astype(BF16), "ctx")
        here = n // t
        tiles_core = [tiles] + [
            lax.ppermute(
                lax.dynamic_slice_in_dim(tiles, (core + s) % t * here, here, 0), "tp", shifts(t, s)
            )
            for s in range(1, t)
        ]
        grad_weight = pl.pallas_call(
            functools.partial(place_kernel, t),
            grid_spec=pltpu.PrefetchScalarGridSpec(
                num_scalar_prefetch=1,
                grid=(here,),
                in_specs=[pl.BlockSpec((1, piece, cols), lambda r, where: (where[1] * here + r, 0, 0))]
                + [pl.BlockSpec((1, piece, cols), lambda r, *_: (r, 0, 0))] * (t - 1),
                out_specs=pl.BlockSpec((tile_rows, cols), lambda r, *_: (r // in_plane, r % in_plane)),
            ),
            out_shape=jax.ShapeDtypeStruct((width, model), F32),
            compiler_params=params,
            cost_estimate=pl.CostEstimate(flops=0, bytes_accessed=2**24, transcendentals=0),
            name="place",
        )(where, *tiles_core)

    mine = simple_call(
        functools.partial(by_core_kernel, n, t), "by_core", where, [chunks],
        [shape(heads_here, 4, sub, HEAD)] * t, [pltpu.VMEM((heads, 4, sub, HEAD), BF16)],
    )
    parts = [mine[0]] + [lax.ppermute(mine[s], "tp", shifts(t, s)) for s in range(1, t)]
    attention, grad_queries, grad_keys, grad_values = simple_call(
        functools.partial(unpack_kernel, t), "unpack", where, parts, [shape(rows, width)] * 4
    )
    projected = dot(attention, out_weight)
    own = lax.dynamic_slice_in_dim(projected, core * half, half, 1)
    for s in range(1, t):
        there = lax.dynamic_slice_in_dim(projected, (core + s) % t * half, half, 1)
        own = own + lax.ppermute(there.astype(BF16), "tp", shifts(t, s)).astype(F32)
    attention_out = own.astype(BF16)

    return attention_out, grad_queries, grad_keys, grad_values, grad_weight


def solution(mesh):
    n, t = mesh.shape["ctx"], mesh.shape["tp"]
    in_specs = (P("ctx", "tp"), P("ctx", "tp"), P("ctx", "tp"), P("tp", None), P("ctx", "tp"), P())
    out_specs = (P("ctx", "tp"), P("ctx", "tp"), P("ctx", "tp"), P("ctx", "tp"), P("tp", None))
    return jax.shard_map(
        functools.partial(per_device, n, t), mesh=mesh, in_specs=in_specs, out_specs=out_specs, check_vma=False
    )
```

```python
import functools
import math

import jax
import jax.numpy as jnp
from jax import lax
from jax.experimental import pallas as pl
from jax.experimental.pallas import tpu as pltpu
from jax.sharding import PartitionSpec as P

HEAD = 128
BLK = 128
TXT_BLK = 4
RUNS = 5
TARGET = 5
PLANES = 4
LOG2E = math.log2(math.e)
NEG_BIG = -1e30

NT = (((1,), (1,)), ((), ()))
TN = (((0,), (0,)), ((), ()))
F32 = jnp.float32
BF16 = jnp.bfloat16


def dot(a, b, dims=(((1,), (0,)), ((), ()))):
    return lax.dot_general(a, b, dims, preferred_element_type=F32)


def gather_tiles(k_ref, kidx_ref, row, dst, tile, count):
    for j in range(count):
        dst[pl.ds(j * tile, tile), :] = k_ref[kidx_ref[row, j]]


def join_parts(parts, k_all, v_all):
    shape = (k_all.shape[0] // (len(parts) // 2),) + k_all.shape[1:]
    for s in range(len(parts) // 2):
        at = pl.ds(s * shape[0], shape[0])
        k_all[at] = parts[2 * s][...].reshape(shape)
        v_all[at] = parts[2 * s + 1][...].reshape(shape)


def place_of(chip, seat, in_plane):
    return (seat + in_plane - chip // in_plane % in_plane) % in_plane


def pack_kernel(n, t, count, where_ref, *refs):
    arrays, got, outs, heads_all = refs[:count], refs[count:count + t - 1], refs[count + t - 1:-1], refs[-1]
    core = where_ref[1]
    sub = heads_all.shape[2]
    heads_here = heads_all.shape[0] // t
    for a in range(count):
        for h in range(heads_here):
            column = pl.ds(h * HEAD, HEAD)
            heads_all[core * heads_here + h, a] = arrays[a][pl.ds(core * sub, sub), column]
            for s in range(1, t):
                first = (core + t - s) % t * heads_here
                heads_all[first + h, a] = got[s - 1][a, :, column]
    plane = where_ref[0] // (n // PLANES)
    heads_plane = outs[0].shape[0]
    for k in range(PLANES):
        outs[k][...] = heads_all[pl.ds((plane ^ k) * heads_plane, heads_plane)]


def to_seats_kernel(n, where_ref, *refs):
    got, outs = refs[:PLANES], refs[PLANES:]
    chip = where_ref[0]
    in_plane = n // PLANES
    for m in range(in_plane):
        place = place_of(chip, chip % in_plane ^ m, in_plane)
        head = jnp.minimum(place, got[0].shape[0] - 1)
        for k in range(PLANES):
            outs[m][chip // in_plane ^ k] = got[k][head]


def join_kernel(n, where_ref, *refs):
    in_plane = n // PLANES
    chunks, outs = refs[:in_plane], refs[in_plane:]
    seat = where_ref[0] % in_plane
    sub = chunks[0].shape[2]
    for m in range(in_plane):
        for p in range(PLANES):
            at = pl.ds(pl.multiple_of((p * in_plane + (seat ^ m)) * sub, sub), sub)
            outs[0][at] = chunks[m][p, 0]
            if len(outs) > 1:
                outs[1][0, at] = chunks[m][p, 1]
                outs[1][1, at] = chunks[m][p, 2]


def unjoin_kernel(n, t, where_ref, attn_ref, dq_ref, dkv_ref, *refs):
    got, outs = refs[:t - 1], refs[t - 1:]
    in_plane = n // PLANES
    seat = where_ref[0] % in_plane
    sub = outs[0].shape[2]
    for m in range(in_plane):
        for p in range(PLANES):
            at = pl.ds(pl.multiple_of((p * in_plane + (seat ^ m)) * sub, sub), sub)
            outs[m][p, 0] = attn_ref[at]
            outs[m][p, 1] = dq_ref[at]
            for a in range(2):
                total = dkv_ref[a, at].astype(F32)
                for other in got:
                    total = total + other[a, at].astype(F32)
                outs[m][p, 2 + a] = total.astype(BF16)


def to_planes_kernel(n, where_ref, *refs):
    in_plane = n // PLANES
    got, outs = refs[:in_plane], refs[in_plane:]
    chip = where_ref[0]
    for m in range(in_plane):
        place = place_of(chip, chip % in_plane ^ m, in_plane)

        @pl.when(place < outs[0].shape[0])
        def _(m=m, place=place):
            for k in range(PLANES):
                outs[k][place] = got[m][chip // in_plane ^ k]


def by_core_kernel(n, t, where_ref, *refs):
    got, outs, heads_all = refs[:PLANES], refs[PLANES:PLANES + t], refs[-1]
    plane, core = where_ref[0] // (n // PLANES), where_ref[1]
    heads_here = heads_all.shape[0] // t
    heads_plane = got[0].shape[0]
    for k in range(PLANES):
        heads_all[pl.ds((plane ^ k) * heads_plane, heads_plane)] = got[k][...]
    for s in range(t):
        outs[s][...] = heads_all[pl.ds((core + s) % t * heads_here, heads_here)]


def seats_kernel(in_plane, where_ref, *refs):
    got, out_ref = refs[:in_plane], refs[in_plane]
    seat = where_ref[0] % in_plane
    for k in range(in_plane):
        out_ref[seat ^ k] = got[k][...]


def tile_kernel(in_plane, heads_plane, t, where_ref, *refs):
    attns, (grad_ref, own_ref), sends = refs[:in_plane], refs[in_plane:in_plane + 2], refs[in_plane + 2:-2]
    seats, total = refs[-2:]
    chip, core = where_ref[0], where_ref[1]
    seat = chip % in_plane
    plane = chip // in_plane
    step = pl.program_id(0)
    for k in range(in_plane):
        seats[seat ^ k] = attns[k][...]

    @pl.when(step == 0)
    def _():
        total[...] = jnp.zeros_like(total)

    grad = grad_ref[...]
    for j in range(heads_plane):
        total[pl.ds(j * HEAD, HEAD)] += dot(seats[(plane + j) % in_plane], grad, TN)

    @pl.when(step == pl.num_programs(0) - 1)
    def _():
        piece = own_ref.shape[0]
        if piece == total.shape[0]:
            own_ref[...] = total[...]
            sends[0][...] = total[...].astype(BF16)
            return
        own_ref[...] = total[pl.ds(pl.multiple_of(core * piece, piece), piece)]
        for s in range(1, t):
            at = pl.ds(pl.multiple_of((core + s) % t * piece, piece), piece)
            sends[s - 1][...] = total[at].astype(BF16)


def place_kernel(t, where_ref, *refs):
    parts, out_ref = refs[:t], refs[t]
    core = where_ref[1]
    piece = parts[0].shape[1]
    for s in range(t):
        at = pl.ds(pl.multiple_of((core + t - s) % t * piece, piece), piece)
        out_ref[at] = parts[s][0].astype(F32)


def unpack_kernel(t, where_ref, *refs):
    parts, outs = refs[:t], refs[t:]
    core = where_ref[1]
    heads_here, _, sub, _ = parts[0].shape
    for s in range(t):
        at = pl.ds(pl.multiple_of((core + t - s) % t * sub, sub), sub)
        for a in range(4):
            for h in range(heads_here):
                outs[a][at, pl.ds(h * HEAD, HEAD)] = parts[s][h, a]


def forward_kernel(t, tile, count, full_ref, kcnt_ref, kidx_ref, q_ref, *refs):
    parts, (out_ref, lse_ref, k_few, v_few, k_ref, v_ref) = refs[:2 * t], refs[2 * t:]
    row = pl.program_id(0)
    q = q_ref[...]

    @pl.when(row == 0)
    def _():
        join_parts(parts, k_ref, v_ref)

    def finish(s, v):
        top = jnp.max(s, axis=1, keepdims=True)
        p = jnp.exp2(s - top)
        mass = jnp.sum(p, axis=1, keepdims=True)
        out = dot(p.astype(BF16), v)
        out_ref[...] = (out / mass).astype(BF16)
        lse_ref[...] = jnp.broadcast_to(top + jnp.log2(mass), lse_ref.shape)

    scale = HEAD ** -0.5 * LOG2E

    @pl.when(full_ref[row] == 1)
    def _():
        keys = k_ref[...].reshape(-1, HEAD)
        finish(dot(q, keys, NT) * scale, v_ref[...].reshape(-1, HEAD))

    @pl.when(full_ref[row] == 0)
    def _():
        gather_tiles(k_ref, kidx_ref, row, k_few, tile, count)
        gather_tiles(v_ref, kidx_ref, row, v_few, tile, count)
        s = dot(q, k_few[...], NT) * scale
        column = lax.broadcasted_iota(jnp.int32, s.shape, 1)
        s = jnp.where(column < kcnt_ref[row] * tile, s, NEG_BIG)
        finish(s, v_few[...])


def backward_kernel(t, tile, count, full_ref, kcnt_ref, kidx_ref, q_ref, g_ref, o_ref, lse_ref, *refs):
    parts, dkv_refs = refs[:2 * t], refs[2 * t + 1:3 * t + 1]
    dq_ref = refs[2 * t]
    k_few, v_few, k_ref, v_ref, dk_acc, dv_acc = refs[3 * t + 1:]
    row = pl.program_id(0)
    last = pl.num_programs(0) - 1

    @pl.when(row == 0)
    def _():
        join_parts(parts, k_ref, v_ref)
        dk_acc[...] = jnp.zeros_like(dk_acc)
        dv_acc[...] = jnp.zeros_like(dv_acc)

    q = q_ref[...]
    g = g_ref[...]
    delta = jnp.sum(g.astype(F32) * o_ref[...].astype(F32), axis=1, keepdims=True)
    lse = lse_ref[:, :1]
    unit = HEAD ** -0.5
    scale = unit * LOG2E

    def gradients(keys, values, mask):
        s = dot(q, keys, NT)
        p = jnp.exp2(s * scale - lse)
        if mask is not None:
            p = jnp.where(mask(p.shape), p, 0.0)
        ds = (p * (dot(g, values, NT) - delta)).astype(BF16)
        dq_ref[...] = (dot(ds, keys) * unit).astype(BF16)
        return dot(ds, q, TN) * unit, dot(p.astype(BF16), g, TN)

    @pl.when(full_ref[row] == 1)
    def _():
        dk, dv = gradients(k_ref[...].reshape(-1, HEAD), v_ref[...].reshape(-1, HEAD), None)
        dk_acc[...] += dk.reshape(dk_acc.shape)
        dv_acc[...] += dv.reshape(dv_acc.shape)

    @pl.when(full_ref[row] == 0)
    def _():
        gather_tiles(k_ref, kidx_ref, row, k_few, tile, count)
        gather_tiles(v_ref, kidx_ref, row, v_few, tile, count)

        def mask(shape):
            return lax.broadcasted_iota(jnp.int32, shape, 1) < kcnt_ref[row] * tile

        dk, dv = gradients(k_few[...], v_few[...], mask)
        for j in range(count):
            at = kidx_ref[row, j]
            dk_acc[at] += dk[j * tile:(j + 1) * tile]
            dv_acc[at] += dv[j * tile:(j + 1) * tile]

    @pl.when(row == last)
    def _():
        tiles = dk_acc.shape[0] // t
        for s, dkv_ref in enumerate(dkv_refs):
            at = pl.ds(s * tiles, tiles)
            dkv_ref[0] = dk_acc[at].reshape(dkv_ref.shape[1:]).astype(BF16)
            dkv_ref[1] = dv_acc[at].reshape(dkv_ref.shape[1:]).astype(BF16)


def whole_block(shape):
    return pl.BlockSpec(shape, lambda *_: (0,) * len(shape))


def one_array(which, length):
    return pl.BlockSpec((1, length, HEAD), lambda *_: (which, 0, 0))


def simple_call(kernel, name, scalars, inputs, outputs, scratch=()):
    size = sum(2 * math.prod(x.shape) for x in list(inputs) + list(outputs))
    return pl.pallas_call(
        kernel,
        grid_spec=pltpu.PrefetchScalarGridSpec(
            num_scalar_prefetch=1,
            grid=(1,),
            in_specs=[whole_block(x.shape) for x in inputs],
            out_specs=[whole_block(x.shape) for x in outputs],
            scratch_shapes=scratch,
        ),
        out_shape=outputs,
        compiler_params=pltpu.CompilerParams(vmem_limit_bytes=48 * 2**20),
        cost_estimate=pl.CostEstimate(flops=0, bytes_accessed=2 * size, transcendentals=0),
        name=name,
    )(scalars, *inputs)


def shifts(t, s):
    return [(c, (c + s) % t) for c in range(t)]


def place_xor_kernel(place_ref, *refs):
    sources, out_ref = refs[:-1], refs[-1]
    step = pl.program_id(0)
    for u in range(2):
        own, beside, above, upper, lower = sources[5 * u:5 * u + 5]
        for v, source in enumerate((own, beside, above)):
            @pl.when(step == 4 * u + v)
            def _(source=source):
                out_ref[...] = source[...].astype(F32)

        @pl.when(step == 4 * u + 3)
        def _(upper=upper, lower=lower):
            middle = upper.shape[0]
            out_ref[:middle] = upper[...].astype(F32)
            out_ref[middle:] = lower[...].astype(F32)


def gather_tiles_by_core(n, t, tile_sum, chip, core):
    in_plane = n // PLANES
    plane, seat = chip // in_plane, chip % in_plane
    tile_rows, cols = tile_sum.shape
    across = [
        (i * t + c, (i ^ 2 * in_plane) * t + c)
        for i in range(n) for c in range(t) if i // in_plane // 2 == c
    ]
    from_half = lax.ppermute(tile_sum, ("ctx", "tp"), across)

    def swap(x, k):
        return lax.ppermute(x, "ctx", [(i, i ^ k) for i in range(n)])

    first = jnp.where(plane // 2 == core, tile_sum, from_half)
    second = swap(first, in_plane)
    beside, above = swap(first, 1), swap(first, 2)
    middle = tile_rows // 2
    sources = [first, beside, above, swap(beside[:middle], 2), swap(above[middle:], 1)]
    beside, above = swap(second, 1), swap(second, 2)
    sources += [second, beside, above, swap(beside[:middle], 2), swap(above[middle:], 1)]
    place = jnp.stack([plane % 2, seat]).astype(jnp.int32)
    return pl.pallas_call(
        place_xor_kernel,
        grid_spec=pltpu.PrefetchScalarGridSpec(
            num_scalar_prefetch=1,
            grid=(8,),
            in_specs=[whole_block(x.shape) for x in sources],
            out_specs=pl.BlockSpec(
                (tile_rows, cols), lambda s, place: (s // 4 ^ place[0], s % 4 ^ place[1])
            ),
        ),
        out_shape=jax.ShapeDtypeStruct((2 * tile_rows, in_plane * cols), F32),
        compiler_params=pltpu.CompilerParams(vmem_limit_bytes=48 * 2**20),
        cost_estimate=pl.CostEstimate(flops=0, bytes_accessed=2**24, transcendentals=0),
        name="place",
    )(place, *sources)


def per_device(n, t, queries, key_vectors, value_vectors, out_weight, out_grad, block_segment):
    rows, width = queries.shape
    heads_here = width // HEAD
    heads = heads_here * t
    sub = rows // t
    tile = min(sub, BLK)
    per_chunk = sub // tile
    core = lax.axis_index("tp")
    chip = lax.axis_index("ctx")
    in_plane = n // PLANES
    heads_plane = heads // PLANES
    seat = chip % in_plane

    def tp_swap(pick):
        got = [pick(core)]
        for s in range(1, t):
            got.append(lax.ppermute(pick((core + s) % t), "tp", shifts(t, s)))
        return [lax.select_n((core - p) % t, *got) for p in range(t)]

    def tp_gather(x):
        return tp_swap(lambda _: x)

    def shape(*dims):
        return jax.ShapeDtypeStruct(dims, BF16)

    where = jnp.stack([chip, core]).astype(jnp.int32)
    held = [(i % in_plane - i // in_plane) % in_plane < heads_plane for i in range(n)]

    chunk_row = jnp.arange(n)[:, None] * rows + jnp.arange(per_chunk)[None, :] * tile

    def tile_segments(part):
        return jnp.take(block_segment, ((chunk_row + part * sub) // BLK).reshape(-1))

    seg_parts = [tile_segments((core - s) % t) for s in range(t)]
    seg_q = seg_parts[0]
    seg_k = jnp.concatenate(seg_parts)
    full = (seg_q == 0) | (seg_q == TARGET)
    permitted = (seg_k[None] == 0) | (seg_k[None] == seg_q[:, None])
    total_blocks = block_segment.shape[0]
    count = (TXT_BLK + -(-(total_blocks - TXT_BLK) // RUNS)) * (BLK // tile)
    kcnt = jnp.sum(permitted.astype(jnp.int32), axis=1)
    tiles_k = seg_k.shape[0]
    ids = jnp.arange(tiles_k)
    place = jnp.sum((permitted[:, None, :] & (ids[None, None, :] < ids[None, :, None])).astype(jnp.int32), axis=2)
    hit = permitted[:, None, :] & (place[:, None, :] == jnp.arange(count)[None, :, None])
    kidx = jnp.sum(jnp.where(hit, ids[None, None, :], 0), axis=2).astype(jnp.int32)
    full = full.astype(jnp.int32)

    def other_rows(*arrays):
        return [
            lax.ppermute(
                jnp.stack([
                    lax.dynamic_slice_in_dim(x, (core + s) % t * sub, sub, 0) for x in arrays
                ]),
                "tp", shifts(t, s),
            )
            for s in range(1, t)
        ]

    got_qkv = other_rows(queries, key_vectors, value_vectors)

    half = out_grad.shape[1]
    model = half * t
    full_grad = jnp.concatenate(tp_gather(out_grad), axis=1)
    grad_attn = dot(full_grad, out_weight, NT).astype(BF16)
    got_g = other_rows(grad_attn)

    cols = model // in_plane
    mine = lax.dynamic_slice_in_dim(full_grad, core * sub, sub, 0)
    plane_got = [lax.dynamic_slice_in_dim(mine, seat * cols, cols, 1)]
    for k in range(1, in_plane):
        there = lax.dynamic_slice_in_dim(mine, (seat ^ k) * cols, cols, 1)
        plane_got.append(lax.ppermute(there, "ctx", [(i, i ^ k) for i in range(n)]))
    (plane_grad,) = simple_call(
        functools.partial(seats_kernel, in_plane), "seats", where, plane_got, [shape(in_plane, sub, cols)]
    )
    def along_z(packs):
        return [packs[0]] + [
            lax.ppermute(packs[k], "ctx", [(i, i ^ k * in_plane) for i in range(n)])
            for k in range(1, PLANES)
        ]

    def in_the_plane(packs, pairs):
        return [packs[0]] + [lax.ppermute(packs[m], "ctx", pairs(m)) for m in range(1, in_plane)]

    def to_held(m):
        return [(i, i ^ m) for i in range(n) if held[i ^ m]]

    def from_held(m):
        return [(i, i ^ m) for i in range(n) if held[i]]

    def pack(arrays, got):
        return simple_call(
            functools.partial(pack_kernel, n, t, len(arrays)), "pack", where,
            arrays + got, [shape(heads_plane, len(arrays), sub, HEAD)] * PLANES,
            [pltpu.VMEM((heads, len(arrays), sub, HEAD), BF16)],
        )

    def to_seats(packs):
        return simple_call(
            functools.partial(to_seats_kernel, n), "to_seats", where, packs,
            [shape(PLANES, packs[0].shape[1], sub, HEAD)] * in_plane,
        )

    length = n * sub
    seats_qkv = to_seats(along_z(pack([queries, key_vectors, value_vectors], got_qkv)))
    packs_g = pack([grad_attn], got_g)
    *seats_qkv, plane_grad, p0, p1, p2, p3 = lax.optimization_barrier((*seats_qkv, plane_grad, *packs_g))
    lines = [[a * in_plane + b for a in range(PLANES)] for b in range(in_plane)]
    slice_grad = lax.all_gather(plane_grad, "ctx", axis_index_groups=lines)
    slice_grad = slice_grad.reshape(length, cols)
    chunks = in_the_plane(seats_qkv, to_held)
    q_rows, kv = simple_call(
        functools.partial(join_kernel, n), "join", where, chunks, [shape(length, HEAD), shape(2, length, HEAD)]
    )
    seats_g = to_seats(along_z([p0, p1, p2, p3]))
    (g_rows,) = simple_call(
        functools.partial(join_kernel, n), "join_g", where, in_the_plane(seats_g, to_held), [shape(length, HEAD)]
    )
    kv_all = [kv] + [lax.ppermute(kv, "tp", shifts(t, s)) for s in range(1, t)]

    tiles_q = n * per_chunk
    few = [pltpu.VMEM((count * tile, HEAD), BF16)] * 2 + [pltpu.VMEM((tiles_k, tile, HEAD), BF16)] * 2
    params = pltpu.CompilerParams(vmem_limit_bytes=48 * 2**20)
    part_blocks = [one_array(0, length), one_array(1, length)] * t
    part_arrays = [a for pack in kv_all for a in (pack, pack)]
    row_block = pl.BlockSpec((tile, HEAD), lambda r, *_: (r, 0))
    attn, lse = pl.pallas_call(
        functools.partial(forward_kernel, t, tile, count),
        grid_spec=pltpu.PrefetchScalarGridSpec(
            num_scalar_prefetch=3,
            grid=(tiles_q,),
            in_specs=[row_block] + part_blocks,
            out_specs=[row_block, row_block],
            scratch_shapes=few,
        ),
        out_shape=[shape(length, HEAD), jax.ShapeDtypeStruct((length, HEAD), F32)],
        compiler_params=params,
        cost_estimate=pl.CostEstimate(flops=16 * 10**9, bytes_accessed=5 * 2**20, transcendentals=2**22),
        name="forward",
    )(full, kcnt, kidx, q_rows, *part_arrays)

    travel = [attn] + [
        lax.ppermute(attn, "ctx", [(i, i ^ k) for i in range(n) if held[i]]) for k in range(1, in_plane)
    ]
    *travel, attn = lax.optimization_barrier((*travel, attn))

    dq, *dkv = pl.pallas_call(
        functools.partial(backward_kernel, t, tile, count),
        grid_spec=pltpu.PrefetchScalarGridSpec(
            num_scalar_prefetch=3,
            grid=(tiles_q,),
            in_specs=[row_block] * 4 + part_blocks,
            out_specs=[row_block] + [whole_block((2, length, HEAD))] * t,
            scratch_shapes=few + [pltpu.VMEM((tiles_k, tile, HEAD), F32)] * 2,
        ),
        out_shape=[shape(length, HEAD)] + [shape(2, length, HEAD)] * t,
        compiler_params=params,
        cost_estimate=pl.CostEstimate(flops=20 * 10**9, bytes_accessed=8 * 2**20, transcendentals=2**22),
        name="backward",
    )(full, kcnt, kidx, q_rows, g_rows, attn, lse, *part_arrays)

    got_dkv = [
        lax.ppermute(dkv[s], "tp", [(c, (c - s) % t) for c in range(t)]) for s in range(1, t)
    ]
    back = simple_call(
        functools.partial(unjoin_kernel, n, t), "unjoin", where,
        [attn, dq, dkv[0]] + got_dkv, [shape(PLANES, 4, sub, HEAD)] * in_plane,
    )
    packs = simple_call(
        functools.partial(to_planes_kernel, n), "to_planes", where, in_the_plane(back, from_held),
        [shape(heads_plane, 4, sub, HEAD)] * PLANES,
    )

    tile_rows = heads_plane * HEAD
    by_core = in_plane == 4 and t == 2
    piece = tile_rows if by_core else tile_rows // t
    step_rows = length // 4
    tile_own, *tile_sends = pl.pallas_call(
        functools.partial(tile_kernel, in_plane, heads_plane, t),
        grid_spec=pltpu.PrefetchScalarGridSpec(
            num_scalar_prefetch=1,
            grid=(4,),
            in_specs=[pl.BlockSpec((step_rows, HEAD), lambda r, *_: (r, 0))] * in_plane
            + [pl.BlockSpec((step_rows, cols), lambda r, *_: (r, 0))],
            out_specs=[whole_block((piece, cols))] * t,
            scratch_shapes=[
                pltpu.VMEM((in_plane, step_rows, HEAD), BF16), pltpu.VMEM((tile_rows, cols), F32)
            ],
        ),
        out_shape=[jax.ShapeDtypeStruct((piece, cols), F32)] + [shape(piece, cols)] * (t - 1),
        compiler_params=params,
        cost_estimate=pl.CostEstimate(flops=5 * 10**9, bytes_accessed=2**22, transcendentals=0),
        name="tile",
    )(where, *travel, slice_grad)
    tile_sum = tile_own
    for s in range(1, t):
        tile_sum = tile_sum + lax.ppermute(tile_sends[s - 1], "tp", shifts(t, s)).astype(F32)
    if by_core:
        grad_weight = gather_tiles_by_core(n, t, tile_sum.astype(BF16), chip, core)
    else:
        tiles = lax.all_gather(tile_sum.astype(BF16), "ctx")
        here = n // t
        tiles_core = [tiles] + [
            lax.ppermute(
                lax.dynamic_slice_in_dim(tiles, (core + s) % t * here, here, 0), "tp", shifts(t, s)
            )
            for s in range(1, t)
        ]
        grad_weight = pl.pallas_call(
            functools.partial(place_kernel, t),
            grid_spec=pltpu.PrefetchScalarGridSpec(
                num_scalar_prefetch=1,
                grid=(here,),
                in_specs=[pl.BlockSpec((1, piece, cols), lambda r, where: (where[1] * here + r, 0, 0))]
                + [pl.BlockSpec((1, piece, cols), lambda r, *_: (r, 0, 0))] * (t - 1),
                out_specs=pl.BlockSpec((tile_rows, cols), lambda r, *_: (r // in_plane, r % in_plane)),
            ),
            out_shape=jax.ShapeDtypeStruct((width, model), F32),
            compiler_params=params,
            cost_estimate=pl.CostEstimate(flops=0, bytes_accessed=2**24, transcendentals=0),
            name="place",
        )(where, *tiles_core)

    mine = simple_call(
        functools.partial(by_core_kernel, n, t), "by_core", where, along_z(packs),
        [shape(heads_here, 4, sub, HEAD)] * t, [pltpu.VMEM((heads, 4, sub, HEAD), BF16)],
    )
    parts = [mine[0]] + [lax.ppermute(mine[s], "tp", shifts(t, s)) for s in range(1, t)]
    attention, grad_queries, grad_keys, grad_values = simple_call(
        functools.partial(unpack_kernel, t), "unpack", where, parts, [shape(rows, width)] * 4
    )
    projected = dot(attention, out_weight)
    own = lax.dynamic_slice_in_dim(projected, core * half, half, 1)
    for s in range(1, t):
        there = lax.dynamic_slice_in_dim(projected, (core + s) % t * half, half, 1)
        own = own + lax.ppermute(there.astype(BF16), "tp", shifts(t, s)).astype(F32)
    attention_out = own.astype(BF16)

    return attention_out, grad_queries, grad_keys, grad_values, grad_weight


def solution(mesh):
    n, t = mesh.shape["ctx"], mesh.shape["tp"]
    in_specs = (P("ctx", "tp"), P("ctx", "tp"), P("ctx", "tp"), P("tp", None), P("ctx", "tp"), P())
    out_specs = (P("ctx", "tp"), P("ctx", "tp"), P("ctx", "tp"), P("ctx", "tp"), P("tp", None))
    return jax.shard_map(
        functools.partial(per_device, n, t), mesh=mesh, in_specs=in_specs, out_specs=out_specs, check_vma=False
    )
```

```python
import functools
import math

import jax
import jax.numpy as jnp
from jax import lax
from jax.experimental import pallas as pl
from jax.experimental.pallas import tpu as pltpu
from jax.sharding import PartitionSpec as P

HEAD = 128
BLK = 128
TXT_BLK = 4
RUNS = 5
TARGET = 5
PLANES = 4
LOG2E = math.log2(math.e)
NEG_BIG = -1e30

NT = (((1,), (1,)), ((), ()))
TN = (((0,), (0,)), ((), ()))
F32 = jnp.float32
BF16 = jnp.bfloat16


def dot(a, b, dims=(((1,), (0,)), ((), ()))):
    return lax.dot_general(a, b, dims, preferred_element_type=F32)


def gather_tiles(k_ref, kidx_ref, row, dst, tile, count):
    for j in range(count):
        dst[pl.ds(j * tile, tile), :] = k_ref[kidx_ref[row, j]]


def join_parts(parts, k_all, v_all):
    shape = (k_all.shape[0] // (len(parts) // 2),) + k_all.shape[1:]
    for s in range(len(parts) // 2):
        at = pl.ds(s * shape[0], shape[0])
        k_all[at] = parts[2 * s][...].reshape(shape)
        v_all[at] = parts[2 * s + 1][...].reshape(shape)


def place_of(chip, seat, in_plane):
    return (seat + in_plane - chip // in_plane % in_plane) % in_plane


def pack_kernel(n, t, count, where_ref, *refs):
    arrays, got, outs, heads_all = refs[:count], refs[count:count + t - 1], refs[count + t - 1:-1], refs[-1]
    core = where_ref[1]
    sub = heads_all.shape[2]
    heads_here = heads_all.shape[0] // t
    for a in range(count):
        for h in range(heads_here):
            column = pl.ds(h * HEAD, HEAD)
            heads_all[core * heads_here + h, a] = arrays[a][pl.ds(core * sub, sub), column]
            for s in range(1, t):
                first = (core + t - s) % t * heads_here
                heads_all[first + h, a] = got[s - 1][a, :, column]
    plane = where_ref[0] // (n // PLANES)
    heads_plane = outs[0].shape[0]
    for k in range(PLANES):
        outs[k][...] = heads_all[pl.ds((plane ^ k) * heads_plane, heads_plane)]


def to_seats_kernel(n, where_ref, *refs):
    got, outs = refs[:PLANES], refs[PLANES:]
    chip = where_ref[0]
    in_plane = n // PLANES
    for m in range(in_plane):
        place = place_of(chip, chip % in_plane ^ m, in_plane)
        head = jnp.minimum(place, got[0].shape[0] - 1)
        for k in range(PLANES):
            outs[m][chip // in_plane ^ k] = got[k][head]


def join_kernel(n, where_ref, *refs):
    in_plane = n // PLANES
    chunks, outs = refs[:in_plane], refs[in_plane:]
    seat = where_ref[0] % in_plane
    sub = chunks[0].shape[2]
    for m in range(in_plane):
        for p in range(PLANES):
            at = pl.ds(pl.multiple_of((p * in_plane + (seat ^ m)) * sub, sub), sub)
            outs[0][at] = chunks[m][p, 0]
            if len(outs) > 1:
                outs[1][0, at] = chunks[m][p, 1]
                outs[1][1, at] = chunks[m][p, 2]


def unjoin_kernel(n, t, where_ref, attn_ref, dq_ref, dkv_ref, *refs):
    got, outs = refs[:t - 1], refs[t - 1:]
    in_plane = n // PLANES
    seat = where_ref[0] % in_plane
    sub = outs[0].shape[2]
    for m in range(in_plane):
        for p in range(PLANES):
            at = pl.ds(pl.multiple_of((p * in_plane + (seat ^ m)) * sub, sub), sub)
            outs[m][p, 0] = attn_ref[at]
            outs[m][p, 1] = dq_ref[at]
            for a in range(2):
                total = dkv_ref[a, at].astype(F32)
                for other in got:
                    total = total + other[a, at].astype(F32)
                outs[m][p, 2 + a] = total.astype(BF16)


def to_planes_kernel(n, where_ref, *refs):
    in_plane = n // PLANES
    got, outs = refs[:in_plane], refs[in_plane:]
    chip = where_ref[0]
    for m in range(in_plane):
        place = place_of(chip, chip % in_plane ^ m, in_plane)

        @pl.when(place < outs[0].shape[0])
        def _(m=m, place=place):
            for k in range(PLANES):
                outs[k][place] = got[m][chip // in_plane ^ k]


def by_core_kernel(n, t, where_ref, *refs):
    got, outs, heads_all = refs[:PLANES], refs[PLANES:PLANES + t], refs[-1]
    plane, core = where_ref[0] // (n // PLANES), where_ref[1]
    heads_here = heads_all.shape[0] // t
    heads_plane = got[0].shape[0]
    for k in range(PLANES):
        heads_all[pl.ds((plane ^ k) * heads_plane, heads_plane)] = got[k][...]
    for s in range(t):
        outs[s][...] = heads_all[pl.ds((core + s) % t * heads_here, heads_here)]


def seats_kernel(in_plane, where_ref, *refs):
    got, out_ref = refs[:in_plane], refs[in_plane]
    seat = where_ref[0] % in_plane
    for k in range(in_plane):
        out_ref[seat ^ k] = got[k][...]


def tile_kernel(in_plane, heads_plane, t, where_ref, *refs):
    attns, (grad_ref, own_ref), sends = refs[:in_plane], refs[in_plane:in_plane + 2], refs[in_plane + 2:-2]
    seats, total = refs[-2:]
    chip, core = where_ref[0], where_ref[1]
    seat = chip % in_plane
    plane = chip // in_plane
    step = pl.program_id(0)
    for k in range(in_plane):
        seats[seat ^ k] = attns[k][...]

    @pl.when(step == 0)
    def _():
        total[...] = jnp.zeros_like(total)

    grad = grad_ref[...]
    for j in range(heads_plane):
        total[pl.ds(j * HEAD, HEAD)] += dot(seats[(plane + j) % in_plane], grad, TN)

    @pl.when(step == pl.num_programs(0) - 1)
    def _():
        piece = own_ref.shape[0]
        if piece == total.shape[0]:
            own_ref[...] = total[...]
            sends[0][...] = total[...].astype(BF16)
            return
        own_ref[...] = total[pl.ds(pl.multiple_of(core * piece, piece), piece)]
        for s in range(1, t):
            at = pl.ds(pl.multiple_of((core + s) % t * piece, piece), piece)
            sends[s - 1][...] = total[at].astype(BF16)


def place_kernel(t, where_ref, *refs):
    parts, out_ref = refs[:t], refs[t]
    core = where_ref[1]
    piece = parts[0].shape[1]
    for s in range(t):
        at = pl.ds(pl.multiple_of((core + t - s) % t * piece, piece), piece)
        out_ref[at] = parts[s][0].astype(F32)


def unpack_kernel(t, where_ref, *refs):
    parts, outs = refs[:t], refs[t:]
    core = where_ref[1]
    heads_here, _, sub, _ = parts[0].shape
    for s in range(t):
        at = pl.ds(pl.multiple_of((core + t - s) % t * sub, sub), sub)
        for a in range(4):
            for h in range(heads_here):
                outs[a][at, pl.ds(h * HEAD, HEAD)] = parts[s][h, a]


def forward_kernel(t, tile, count, full_ref, kcnt_ref, kidx_ref, q_ref, *refs):
    parts, (out_ref, lse_ref, k_few, v_few, k_ref, v_ref) = refs[:2 * t], refs[2 * t:]
    row = pl.program_id(0)
    q = q_ref[...]

    @pl.when(row == 0)
    def _():
        join_parts(parts, k_ref, v_ref)

    def finish(s, v):
        top = jnp.max(s, axis=1, keepdims=True)
        p = jnp.exp2(s - top)
        mass = jnp.sum(p, axis=1, keepdims=True)
        out = dot(p.astype(BF16), v)
        out_ref[...] = (out / mass).astype(BF16)
        lse_ref[...] = jnp.broadcast_to(top + jnp.log2(mass), lse_ref.shape)

    scale = HEAD ** -0.5 * LOG2E

    @pl.when(full_ref[row] == 1)
    def _():
        keys = k_ref[...].reshape(-1, HEAD)
        finish(dot(q, keys, NT) * scale, v_ref[...].reshape(-1, HEAD))

    @pl.when(full_ref[row] == 0)
    def _():
        gather_tiles(k_ref, kidx_ref, row, k_few, tile, count)
        gather_tiles(v_ref, kidx_ref, row, v_few, tile, count)
        s = dot(q, k_few[...], NT) * scale
        column = lax.broadcasted_iota(jnp.int32, s.shape, 1)
        s = jnp.where(column < kcnt_ref[row] * tile, s, NEG_BIG)
        finish(s, v_few[...])


def backward_kernel(t, tile, count, full_ref, kcnt_ref, kidx_ref, q_ref, g_ref, o_ref, lse_ref, *refs):
    parts, dkv_refs = refs[:2 * t], refs[2 * t + 1:3 * t + 1]
    dq_ref = refs[2 * t]
    k_few, v_few, k_ref, v_ref, dk_acc, dv_acc = refs[3 * t + 1:]
    row = pl.program_id(0)
    last = pl.num_programs(0) - 1

    @pl.when(row == 0)
    def _():
        join_parts(parts, k_ref, v_ref)
        dk_acc[...] = jnp.zeros_like(dk_acc)
        dv_acc[...] = jnp.zeros_like(dv_acc)

    q = q_ref[...]
    g = g_ref[...]
    delta = jnp.sum(g.astype(F32) * o_ref[...].astype(F32), axis=1, keepdims=True)
    lse = lse_ref[:, :1]
    unit = HEAD ** -0.5
    scale = unit * LOG2E

    def gradients(keys, values, mask):
        s = dot(q, keys, NT)
        p = jnp.exp2(s * scale - lse)
        if mask is not None:
            p = jnp.where(mask(p.shape), p, 0.0)
        ds = (p * (dot(g, values, NT) - delta)).astype(BF16)
        dq_ref[...] = (dot(ds, keys) * unit).astype(BF16)
        return dot(ds, q, TN) * unit, dot(p.astype(BF16), g, TN)

    @pl.when(full_ref[row] == 1)
    def _():
        dk, dv = gradients(k_ref[...].reshape(-1, HEAD), v_ref[...].reshape(-1, HEAD), None)
        dk_acc[...] += dk.reshape(dk_acc.shape)
        dv_acc[...] += dv.reshape(dv_acc.shape)

    @pl.when(full_ref[row] == 0)
    def _():
        gather_tiles(k_ref, kidx_ref, row, k_few, tile, count)
        gather_tiles(v_ref, kidx_ref, row, v_few, tile, count)

        def mask(shape):
            return lax.broadcasted_iota(jnp.int32, shape, 1) < kcnt_ref[row] * tile

        dk, dv = gradients(k_few[...], v_few[...], mask)
        for j in range(count):
            at = kidx_ref[row, j]
            dk_acc[at] += dk[j * tile:(j + 1) * tile]
            dv_acc[at] += dv[j * tile:(j + 1) * tile]

    @pl.when(row == last)
    def _():
        tiles = dk_acc.shape[0] // t
        for s, dkv_ref in enumerate(dkv_refs):
            at = pl.ds(s * tiles, tiles)
            dkv_ref[0] = dk_acc[at].reshape(dkv_ref.shape[1:]).astype(BF16)
            dkv_ref[1] = dv_acc[at].reshape(dkv_ref.shape[1:]).astype(BF16)


def whole_block(shape):
    return pl.BlockSpec(shape, lambda *_: (0,) * len(shape))


def one_array(which, length):
    return pl.BlockSpec((1, length, HEAD), lambda *_: (which, 0, 0))


def simple_call(kernel, name, scalars, inputs, outputs, scratch=()):
    size = sum(2 * math.prod(x.shape) for x in list(inputs) + list(outputs))
    return pl.pallas_call(
        kernel,
        grid_spec=pltpu.PrefetchScalarGridSpec(
            num_scalar_prefetch=1,
            grid=(1,),
            in_specs=[whole_block(x.shape) for x in inputs],
            out_specs=[whole_block(x.shape) for x in outputs],
            scratch_shapes=scratch,
        ),
        out_shape=outputs,
        compiler_params=pltpu.CompilerParams(vmem_limit_bytes=48 * 2**20),
        cost_estimate=pl.CostEstimate(flops=0, bytes_accessed=2 * size, transcendentals=0),
        name=name,
    )(scalars, *inputs)


def shifts(t, s):
    return [(c, (c + s) % t) for c in range(t)]


def place_xor_kernel(place_ref, *refs):
    sources, out_ref = refs[:-1], refs[-1]
    step = pl.program_id(0)
    for u in range(2):
        own, beside, above, upper, lower = sources[5 * u:5 * u + 5]
        for v, source in enumerate((own, beside, above)):
            @pl.when(step == 4 * u + v)
            def _(source=source):
                out_ref[...] = source[...].astype(F32)

        @pl.when(step == 4 * u + 3)
        def _(upper=upper, lower=lower):
            middle = upper.shape[0]
            out_ref[:middle] = upper[...].astype(F32)
            out_ref[middle:] = lower[...].astype(F32)


def gather_tiles_by_core(n, t, tile_sum, chip, core, packs, along_z):
    in_plane = n // PLANES
    plane, seat = chip // in_plane, chip % in_plane
    tile_rows, cols = tile_sum.shape
    across = [
        (i * t + c, (i ^ 2 * in_plane) * t + c)
        for i in range(n) for c in range(t) if i // in_plane // 2 == c
    ]
    from_half = lax.ppermute(tile_sum, ("ctx", "tp"), across)

    def swap(x, k):
        return lax.ppermute(x, "ctx", [(i, i ^ k) for i in range(n)])

    first = jnp.where(plane // 2 == core, tile_sum, from_half)
    first, *packs = lax.optimization_barrier((first, *packs))
    second = swap(first, in_plane)
    beside, above = swap(first, 1), swap(first, 2)
    second, beside, above, *packs = lax.optimization_barrier((second, beside, above, *along_z(packs)))
    middle = tile_rows // 2
    sources = [first, beside, above, swap(beside[:middle], 2), swap(above[middle:], 1)]
    beside, above = swap(second, 1), swap(second, 2)
    sources += [second, beside, above, swap(beside[:middle], 2), swap(above[middle:], 1)]
    place = jnp.stack([plane % 2, seat]).astype(jnp.int32)
    return pl.pallas_call(
        place_xor_kernel,
        grid_spec=pltpu.PrefetchScalarGridSpec(
            num_scalar_prefetch=1,
            grid=(8,),
            in_specs=[whole_block(x.shape) for x in sources],
            out_specs=pl.BlockSpec(
                (tile_rows, cols), lambda s, place: (s // 4 ^ place[0], s % 4 ^ place[1])
            ),
        ),
        out_shape=jax.ShapeDtypeStruct((2 * tile_rows, in_plane * cols), F32),
        compiler_params=pltpu.CompilerParams(vmem_limit_bytes=48 * 2**20),
        cost_estimate=pl.CostEstimate(flops=0, bytes_accessed=2**24, transcendentals=0),
        name="place",
    )(place, *sources), packs


def per_device(n, t, queries, key_vectors, value_vectors, out_weight, out_grad, block_segment):
    rows, width = queries.shape
    heads_here = width // HEAD
    heads = heads_here * t
    sub = rows // t
    tile = min(sub, BLK)
    per_chunk = sub // tile
    core = lax.axis_index("tp")
    chip = lax.axis_index("ctx")
    in_plane = n // PLANES
    heads_plane = heads // PLANES
    seat = chip % in_plane

    def tp_swap(pick):
        got = [pick(core)]
        for s in range(1, t):
            got.append(lax.ppermute(pick((core + s) % t), "tp", shifts(t, s)))
        return [lax.select_n((core - p) % t, *got) for p in range(t)]

    def tp_gather(x):
        return tp_swap(lambda _: x)

    def shape(*dims):
        return jax.ShapeDtypeStruct(dims, BF16)

    where = jnp.stack([chip, core]).astype(jnp.int32)
    held = [(i % in_plane - i // in_plane) % in_plane < heads_plane for i in range(n)]

    chunk_row = jnp.arange(n)[:, None] * rows + jnp.arange(per_chunk)[None, :] * tile

    def tile_segments(part):
        return jnp.take(block_segment, ((chunk_row + part * sub) // BLK).reshape(-1))

    seg_parts = [tile_segments((core - s) % t) for s in range(t)]
    seg_q = seg_parts[0]
    seg_k = jnp.concatenate(seg_parts)
    full = (seg_q == 0) | (seg_q == TARGET)
    permitted = (seg_k[None] == 0) | (seg_k[None] == seg_q[:, None])
    total_blocks = block_segment.shape[0]
    count = (TXT_BLK + -(-(total_blocks - TXT_BLK) // RUNS)) * (BLK // tile)
    kcnt = jnp.sum(permitted.astype(jnp.int32), axis=1)
    tiles_k = seg_k.shape[0]
    ids = jnp.arange(tiles_k)
    place = jnp.sum((permitted[:, None, :] & (ids[None, None, :] < ids[None, :, None])).astype(jnp.int32), axis=2)
    hit = permitted[:, None, :] & (place[:, None, :] == jnp.arange(count)[None, :, None])
    kidx = jnp.sum(jnp.where(hit, ids[None, None, :], 0), axis=2).astype(jnp.int32)
    full = full.astype(jnp.int32)

    def other_rows(*arrays):
        return [
            lax.ppermute(
                jnp.stack([
                    lax.dynamic_slice_in_dim(x, (core + s) % t * sub, sub, 0) for x in arrays
                ]),
                "tp", shifts(t, s),
            )
            for s in range(1, t)
        ]

    got_qkv = other_rows(queries, key_vectors, value_vectors)

    half = out_grad.shape[1]
    model = half * t
    full_grad = jnp.concatenate(tp_gather(out_grad), axis=1)
    grad_attn = dot(full_grad, out_weight, NT).astype(BF16)
    got_g = other_rows(grad_attn)

    cols = model // in_plane
    mine = lax.dynamic_slice_in_dim(full_grad, core * sub, sub, 0)
    plane_got = [lax.dynamic_slice_in_dim(mine, seat * cols, cols, 1)]
    for k in range(1, in_plane):
        there = lax.dynamic_slice_in_dim(mine, (seat ^ k) * cols, cols, 1)
        plane_got.append(lax.ppermute(there, "ctx", [(i, i ^ k) for i in range(n)]))
    (plane_grad,) = simple_call(
        functools.partial(seats_kernel, in_plane), "seats", where, plane_got, [shape(in_plane, sub, cols)]
    )
    def along_z(packs):
        return [packs[0]] + [
            lax.ppermute(packs[k], "ctx", [(i, i ^ k * in_plane) for i in range(n)])
            for k in range(1, PLANES)
        ]

    def in_the_plane(packs, pairs):
        return [packs[0]] + [lax.ppermute(packs[m], "ctx", pairs(m)) for m in range(1, in_plane)]

    def to_held(m):
        return [(i, i ^ m) for i in range(n) if held[i ^ m]]

    def from_held(m):
        return [(i, i ^ m) for i in range(n) if held[i]]

    def pack(arrays, got):
        return simple_call(
            functools.partial(pack_kernel, n, t, len(arrays)), "pack", where,
            arrays + got, [shape(heads_plane, len(arrays), sub, HEAD)] * PLANES,
            [pltpu.VMEM((heads, len(arrays), sub, HEAD), BF16)],
        )

    def to_seats(packs):
        return simple_call(
            functools.partial(to_seats_kernel, n), "to_seats", where, packs,
            [shape(PLANES, packs[0].shape[1], sub, HEAD)] * in_plane,
        )

    length = n * sub
    seats_qkv = to_seats(along_z(pack([queries, key_vectors, value_vectors], got_qkv)))
    packs_g = pack([grad_attn], got_g)
    *seats_qkv, plane_grad, p0, p1, p2, p3 = lax.optimization_barrier((*seats_qkv, plane_grad, *packs_g))
    lines = [[a * in_plane + b for a in range(PLANES)] for b in range(in_plane)]
    slice_grad = lax.all_gather(plane_grad, "ctx", axis_index_groups=lines)
    slice_grad = slice_grad.reshape(length, cols)
    chunks = in_the_plane(seats_qkv, to_held)
    seats_g = to_seats(along_z([p0, p1, p2, p3]))
    tied = lax.optimization_barrier((*chunks, *seats_g))
    chunks, seats_g = list(tied[:in_plane]), list(tied[in_plane:])
    q_rows, kv = simple_call(
        functools.partial(join_kernel, n), "join", where, chunks, [shape(length, HEAD), shape(2, length, HEAD)]
    )
    (g_rows,) = simple_call(
        functools.partial(join_kernel, n), "join_g", where, in_the_plane(seats_g, to_held), [shape(length, HEAD)]
    )
    q_rows, g_rows = lax.optimization_barrier((q_rows, g_rows))
    kv_all = [kv] + [lax.ppermute(kv, "tp", shifts(t, s)) for s in range(1, t)]

    tiles_q = n * per_chunk
    few = [pltpu.VMEM((count * tile, HEAD), BF16)] * 2 + [pltpu.VMEM((tiles_k, tile, HEAD), BF16)] * 2
    params = pltpu.CompilerParams(vmem_limit_bytes=48 * 2**20)
    part_blocks = [one_array(0, length), one_array(1, length)] * t
    part_arrays = [a for pack in kv_all for a in (pack, pack)]
    row_block = pl.BlockSpec((tile, HEAD), lambda r, *_: (r, 0))
    attn, lse = pl.pallas_call(
        functools.partial(forward_kernel, t, tile, count),
        grid_spec=pltpu.PrefetchScalarGridSpec(
            num_scalar_prefetch=3,
            grid=(tiles_q,),
            in_specs=[row_block] + part_blocks,
            out_specs=[row_block, row_block],
            scratch_shapes=few,
        ),
        out_shape=[shape(length, HEAD), jax.ShapeDtypeStruct((length, HEAD), F32)],
        compiler_params=params,
        cost_estimate=pl.CostEstimate(flops=16 * 10**9, bytes_accessed=5 * 2**20, transcendentals=2**22),
        name="forward",
    )(full, kcnt, kidx, q_rows, *part_arrays)

    travel = [attn] + [
        lax.ppermute(attn, "ctx", [(i, i ^ k) for i in range(n) if held[i]]) for k in range(1, in_plane)
    ]
    *travel, attn = lax.optimization_barrier((*travel, attn))

    dq, *dkv = pl.pallas_call(
        functools.partial(backward_kernel, t, tile, count),
        grid_spec=pltpu.PrefetchScalarGridSpec(
            num_scalar_prefetch=3,
            grid=(tiles_q,),
            in_specs=[row_block] * 4 + part_blocks,
            out_specs=[row_block] + [whole_block((2, length, HEAD))] * t,
            scratch_shapes=few + [pltpu.VMEM((tiles_k, tile, HEAD), F32)] * 2,
        ),
        out_shape=[shape(length, HEAD)] + [shape(2, length, HEAD)] * t,
        compiler_params=params,
        cost_estimate=pl.CostEstimate(flops=20 * 10**9, bytes_accessed=8 * 2**20, transcendentals=2**22),
        name="backward",
    )(full, kcnt, kidx, q_rows, g_rows, attn, lse, *part_arrays)

    got_dkv = [
        lax.ppermute(dkv[s], "tp", [(c, (c - s) % t) for c in range(t)]) for s in range(1, t)
    ]
    back = simple_call(
        functools.partial(unjoin_kernel, n, t), "unjoin", where,
        [attn, dq, dkv[0]] + got_dkv, [shape(PLANES, 4, sub, HEAD)] * in_plane,
    )
    packs = simple_call(
        functools.partial(to_planes_kernel, n), "to_planes", where, in_the_plane(back, from_held),
        [shape(heads_plane, 4, sub, HEAD)] * PLANES,
    )

    tile_rows = heads_plane * HEAD
    by_core = in_plane == 4 and t == 2
    piece = tile_rows if by_core else tile_rows // t
    step_rows = length // 4
    tile_own, *tile_sends = pl.pallas_call(
        functools.partial(tile_kernel, in_plane, heads_plane, t),
        grid_spec=pltpu.PrefetchScalarGridSpec(
            num_scalar_prefetch=1,
            grid=(4,),
            in_specs=[pl.BlockSpec((step_rows, HEAD), lambda r, *_: (r, 0))] * in_plane
            + [pl.BlockSpec((step_rows, cols), lambda r, *_: (r, 0))],
            out_specs=[whole_block((piece, cols))] * t,
            scratch_shapes=[
                pltpu.VMEM((in_plane, step_rows, HEAD), BF16), pltpu.VMEM((tile_rows, cols), F32)
            ],
        ),
        out_shape=[jax.ShapeDtypeStruct((piece, cols), F32)] + [shape(piece, cols)] * (t - 1),
        compiler_params=params,
        cost_estimate=pl.CostEstimate(flops=5 * 10**9, bytes_accessed=2**22, transcendentals=0),
        name="tile",
    )(where, *travel, slice_grad)
    tile_sum = tile_own
    for s in range(1, t):
        tile_sum = tile_sum + lax.ppermute(tile_sends[s - 1], "tp", shifts(t, s)).astype(F32)
    if by_core:
        grad_weight, back = gather_tiles_by_core(
            n, t, tile_sum.astype(BF16), chip, core, packs, along_z
        )
    else:
        back = along_z(packs)
        tiles = lax.all_gather(tile_sum.astype(BF16), "ctx")
        here = n // t
        tiles_core = [tiles] + [
            lax.ppermute(
                lax.dynamic_slice_in_dim(tiles, (core + s) % t * here, here, 0), "tp", shifts(t, s)
            )
            for s in range(1, t)
        ]
        grad_weight = pl.pallas_call(
            functools.partial(place_kernel, t),
            grid_spec=pltpu.PrefetchScalarGridSpec(
                num_scalar_prefetch=1,
                grid=(here,),
                in_specs=[pl.BlockSpec((1, piece, cols), lambda r, where: (where[1] * here + r, 0, 0))]
                + [pl.BlockSpec((1, piece, cols), lambda r, *_: (r, 0, 0))] * (t - 1),
                out_specs=pl.BlockSpec((tile_rows, cols), lambda r, *_: (r // in_plane, r % in_plane)),
            ),
            out_shape=jax.ShapeDtypeStruct((width, model), F32),
            compiler_params=params,
            cost_estimate=pl.CostEstimate(flops=0, bytes_accessed=2**24, transcendentals=0),
            name="place",
        )(where, *tiles_core)

    mine = simple_call(
        functools.partial(by_core_kernel, n, t), "by_core", where, back,
        [shape(heads_here, 4, sub, HEAD)] * t, [pltpu.VMEM((heads, 4, sub, HEAD), BF16)],
    )
    parts = [mine[0]] + [lax.ppermute(mine[s], "tp", shifts(t, s)) for s in range(1, t)]
    attention, grad_queries, grad_keys, grad_values = simple_call(
        functools.partial(unpack_kernel, t), "unpack", where, parts, [shape(rows, width)] * 4
    )
    projected = dot(attention, out_weight)
    own = lax.dynamic_slice_in_dim(projected, core * half, half, 1)
    for s in range(1, t):
        there = lax.dynamic_slice_in_dim(projected, (core + s) % t * half, half, 1)
        own = own + lax.ppermute(there.astype(BF16), "tp", shifts(t, s)).astype(F32)
    attention_out = own.astype(BF16)

    return attention_out, grad_queries, grad_keys, grad_values, grad_weight


def solution(mesh):
    n, t = mesh.shape["ctx"], mesh.shape["tp"]
    in_specs = (P("ctx", "tp"), P("ctx", "tp"), P("ctx", "tp"), P("tp", None), P("ctx", "tp"), P())
    out_specs = (P("ctx", "tp"), P("ctx", "tp"), P("ctx", "tp"), P("ctx", "tp"), P("tp", None))
    return jax.shard_map(
        functools.partial(per_device, n, t), mesh=mesh, in_specs=in_specs, out_specs=out_specs, check_vma=False
    )
```

```python
import functools
import math

import jax
import jax.numpy as jnp
from jax import lax
from jax.experimental import pallas as pl
from jax.experimental.pallas import tpu as pltpu
from jax.sharding import PartitionSpec as P

HEAD = 128
BLK = 128
TXT_BLK = 4
RUNS = 5
TARGET = 5
PLANES = 4
LOG2E = math.log2(math.e)
NEG_BIG = -1e30

NT = (((1,), (1,)), ((), ()))
TN = (((0,), (0,)), ((), ()))
F32 = jnp.float32
BF16 = jnp.bfloat16


def dot(a, b, dims=(((1,), (0,)), ((), ()))):
    return lax.dot_general(a, b, dims, preferred_element_type=F32)


def gather_tiles(k_ref, kidx_ref, row, dst, tile, count):
    for j in range(count):
        dst[pl.ds(j * tile, tile), :] = k_ref[kidx_ref[row, j]]


def join_parts(parts, k_all, v_all):
    shape = (k_all.shape[0] // (len(parts) // 2),) + k_all.shape[1:]
    for s in range(len(parts) // 2):
        at = pl.ds(s * shape[0], shape[0])
        k_all[at] = parts[2 * s][...].reshape(shape)
        v_all[at] = parts[2 * s + 1][...].reshape(shape)


def place_of(chip, seat, in_plane):
    return (seat + in_plane - chip // in_plane % in_plane) % in_plane


def pack_kernel(n, t, count, where_ref, *refs):
    arrays, got, outs, heads_all = refs[:count], refs[count:count + t - 1], refs[count + t - 1:-1], refs[-1]
    core = where_ref[1]
    sub = heads_all.shape[2]
    heads_here = heads_all.shape[0] // t
    for a in range(count):
        for h in range(heads_here):
            column = pl.ds(h * HEAD, HEAD)
            heads_all[core * heads_here + h, a] = arrays[a][pl.ds(core * sub, sub), column]
            for s in range(1, t):
                first = (core + t - s) % t * heads_here
                heads_all[first + h, a] = got[s - 1][a, :, column]
    plane = where_ref[0] // (n // PLANES)
    heads_plane = outs[0].shape[0]
    for k in range(PLANES):
        outs[k][...] = heads_all[pl.ds((plane ^ k) * heads_plane, heads_plane)]


def to_seats_kernel(n, where_ref, *refs):
    got, outs = refs[:PLANES], refs[PLANES:]
    chip = where_ref[0]
    in_plane = n // PLANES
    for m in range(in_plane):
        place = place_of(chip, chip % in_plane ^ m, in_plane)
        head = jnp.minimum(place, got[0].shape[0] - 1)
        for k in range(PLANES):
            outs[m][chip // in_plane ^ k] = got[k][head]


def join_kernel(n, where_ref, *refs):
    in_plane = n // PLANES
    chunks, outs = refs[:in_plane], refs[in_plane:]
    seat = where_ref[0] % in_plane
    sub = chunks[0].shape[2]
    for m in range(in_plane):
        for p in range(PLANES):
            at = pl.ds(pl.multiple_of((p * in_plane + (seat ^ m)) * sub, sub), sub)
            outs[0][at] = chunks[m][p, 0]
            if len(outs) > 1:
                outs[1][0, at] = chunks[m][p, 1]
                outs[1][1, at] = chunks[m][p, 2]


def unjoin_kernel(n, t, where_ref, attn_ref, dq_ref, dkv_ref, *refs):
    got, outs = refs[:t - 1], refs[t - 1:]
    in_plane = n // PLANES
    seat = where_ref[0] % in_plane
    sub = outs[0].shape[2]
    for m in range(in_plane):
        for p in range(PLANES):
            at = pl.ds(pl.multiple_of((p * in_plane + (seat ^ m)) * sub, sub), sub)
            outs[m][p, 0] = attn_ref[at]
            outs[m][p, 1] = dq_ref[at]
            for a in range(2):
                total = dkv_ref[a, at].astype(F32)
                for other in got:
                    total = total + other[a, at].astype(F32)
                outs[m][p, 2 + a] = total.astype(BF16)


def to_planes_kernel(n, where_ref, *refs):
    in_plane = n // PLANES
    got, outs = refs[:in_plane], refs[in_plane:]
    chip = where_ref[0]
    for m in range(in_plane):
        place = place_of(chip, chip % in_plane ^ m, in_plane)

        @pl.when(place < outs[0].shape[0])
        def _(m=m, place=place):
            for k in range(PLANES):
                outs[k][place] = got[m][chip // in_plane ^ k]


def by_core_kernel(n, t, where_ref, *refs):
    got, outs, heads_all = refs[:PLANES], refs[PLANES:PLANES + t], refs[-1]
    plane, core = where_ref[0] // (n // PLANES), where_ref[1]
    heads_here = heads_all.shape[0] // t
    heads_plane = got[0].shape[0]
    for k in range(PLANES):
        heads_all[pl.ds((plane ^ k) * heads_plane, heads_plane)] = got[k][...]
    for s in range(t):
        outs[s][...] = heads_all[pl.ds((core + s) % t * heads_here, heads_here)]


def seats_kernel(in_plane, where_ref, *refs):
    got, out_ref = refs[:in_plane], refs[in_plane]
    seat = where_ref[0] % in_plane
    for k in range(in_plane):
        out_ref[seat ^ k] = got[k][...]


def tile_kernel(in_plane, heads_plane, t, where_ref, *refs):
    attns, (grad_ref, own_ref), sends = refs[:in_plane], refs[in_plane:in_plane + 2], refs[in_plane + 2:-2]
    seats, total = refs[-2:]
    chip, core = where_ref[0], where_ref[1]
    seat = chip % in_plane
    plane = chip // in_plane
    step = pl.program_id(0)
    for k in range(in_plane):
        seats[seat ^ k] = attns[k][...]

    @pl.when(step == 0)
    def _():
        total[...] = jnp.zeros_like(total)

    grad = grad_ref[...]
    for j in range(heads_plane):
        total[pl.ds(j * HEAD, HEAD)] += dot(seats[(plane + j) % in_plane], grad, TN)

    @pl.when(step == pl.num_programs(0) - 1)
    def _():
        piece = own_ref.shape[0]
        if piece == total.shape[0]:
            own_ref[...] = total[...]
            sends[0][...] = total[...].astype(BF16)
            return
        own_ref[...] = total[pl.ds(pl.multiple_of(core * piece, piece), piece)]
        for s in range(1, t):
            at = pl.ds(pl.multiple_of((core + s) % t * piece, piece), piece)
            sends[s - 1][...] = total[at].astype(BF16)


def place_kernel(t, where_ref, *refs):
    parts, out_ref = refs[:t], refs[t]
    core = where_ref[1]
    piece = parts[0].shape[1]
    for s in range(t):
        at = pl.ds(pl.multiple_of((core + t - s) % t * piece, piece), piece)
        out_ref[at] = parts[s][0].astype(F32)


def unpack_kernel(t, where_ref, *refs):
    parts, outs = refs[:t], refs[t:]
    core = where_ref[1]
    heads_here, _, sub, _ = parts[0].shape
    for s in range(t):
        at = pl.ds(pl.multiple_of((core + t - s) % t * sub, sub), sub)
        for a in range(4):
            for h in range(heads_here):
                outs[a][at, pl.ds(h * HEAD, HEAD)] = parts[s][h, a]


def forward_kernel(t, tile, count, full_ref, kcnt_ref, kidx_ref, q_ref, *refs):
    parts, (out_ref, lse_ref, k_few, v_few, k_ref, v_ref) = refs[:2 * t], refs[2 * t:]
    row = pl.program_id(0)
    q = q_ref[...]

    @pl.when(row == 0)
    def _():
        join_parts(parts, k_ref, v_ref)

    def finish(s, v):
        top = jnp.max(s, axis=1, keepdims=True)
        p = jnp.exp2(s - top)
        mass = jnp.sum(p, axis=1, keepdims=True)
        out = dot(p.astype(BF16), v)
        out_ref[...] = (out / mass).astype(BF16)
        lse_ref[...] = jnp.broadcast_to(top + jnp.log2(mass), lse_ref.shape)

    scale = HEAD ** -0.5 * LOG2E

    @pl.when(full_ref[row] == 1)
    def _():
        keys = k_ref[...].reshape(-1, HEAD)
        finish(dot(q, keys, NT) * scale, v_ref[...].reshape(-1, HEAD))

    @pl.when(full_ref[row] == 0)
    def _():
        gather_tiles(k_ref, kidx_ref, row, k_few, tile, count)
        gather_tiles(v_ref, kidx_ref, row, v_few, tile, count)
        s = dot(q, k_few[...], NT) * scale
        column = lax.broadcasted_iota(jnp.int32, s.shape, 1)
        s = jnp.where(column < kcnt_ref[row] * tile, s, NEG_BIG)
        finish(s, v_few[...])


def backward_kernel(t, tile, count, full_ref, kcnt_ref, kidx_ref, q_ref, g_ref, o_ref, lse_ref, *refs):
    parts, dkv_refs = refs[:2 * t], refs[2 * t + 1:3 * t + 1]
    dq_ref = refs[2 * t]
    k_few, v_few, k_ref, v_ref, dk_acc, dv_acc = refs[3 * t + 1:]
    row = pl.program_id(0)
    last = pl.num_programs(0) - 1

    @pl.when(row == 0)
    def _():
        join_parts(parts, k_ref, v_ref)
        dk_acc[...] = jnp.zeros_like(dk_acc)
        dv_acc[...] = jnp.zeros_like(dv_acc)

    q = q_ref[...]
    g = g_ref[...]
    delta = jnp.sum(g.astype(F32) * o_ref[...].astype(F32), axis=1, keepdims=True)
    lse = lse_ref[:, :1]
    unit = HEAD ** -0.5
    scale = unit * LOG2E

    def gradients(keys, values, mask):
        s = dot(q, keys, NT)
        p = jnp.exp2(s * scale - lse)
        if mask is not None:
            p = jnp.where(mask(p.shape), p, 0.0)
        ds = (p * (dot(g, values, NT) - delta)).astype(BF16)
        dq_ref[...] = (dot(ds, keys) * unit).astype(BF16)
        return dot(ds, q, TN) * unit, dot(p.astype(BF16), g, TN)

    @pl.when(full_ref[row] == 1)
    def _():
        dk, dv = gradients(k_ref[...].reshape(-1, HEAD), v_ref[...].reshape(-1, HEAD), None)
        dk_acc[...] += dk.reshape(dk_acc.shape)
        dv_acc[...] += dv.reshape(dv_acc.shape)

    @pl.when(full_ref[row] == 0)
    def _():
        gather_tiles(k_ref, kidx_ref, row, k_few, tile, count)
        gather_tiles(v_ref, kidx_ref, row, v_few, tile, count)

        def mask(shape):
            return lax.broadcasted_iota(jnp.int32, shape, 1) < kcnt_ref[row] * tile

        dk, dv = gradients(k_few[...], v_few[...], mask)
        for j in range(count):
            at = kidx_ref[row, j]
            dk_acc[at] += dk[j * tile:(j + 1) * tile]
            dv_acc[at] += dv[j * tile:(j + 1) * tile]

    @pl.when(row == last)
    def _():
        tiles = dk_acc.shape[0] // t
        for s, dkv_ref in enumerate(dkv_refs):
            at = pl.ds(s * tiles, tiles)
            dkv_ref[0] = dk_acc[at].reshape(dkv_ref.shape[1:]).astype(BF16)
            dkv_ref[1] = dv_acc[at].reshape(dkv_ref.shape[1:]).astype(BF16)


def whole_block(shape):
    return pl.BlockSpec(shape, lambda *_: (0,) * len(shape))


def one_array(which, length):
    return pl.BlockSpec((1, length, HEAD), lambda *_: (which, 0, 0))


def simple_call(kernel, name, scalars, inputs, outputs, scratch=()):
    size = sum(2 * math.prod(x.shape) for x in list(inputs) + list(outputs))
    return pl.pallas_call(
        kernel,
        grid_spec=pltpu.PrefetchScalarGridSpec(
            num_scalar_prefetch=1,
            grid=(1,),
            in_specs=[whole_block(x.shape) for x in inputs],
            out_specs=[whole_block(x.shape) for x in outputs],
            scratch_shapes=scratch,
        ),
        out_shape=outputs,
        compiler_params=pltpu.CompilerParams(vmem_limit_bytes=48 * 2**20),
        cost_estimate=pl.CostEstimate(flops=0, bytes_accessed=2 * size, transcendentals=0),
        name=name,
    )(scalars, *inputs)


def shifts(t, s):
    return [(c, (c + s) % t) for c in range(t)]


def place_xor_kernel(place_ref, *refs):
    sources, out_ref = refs[:-1], refs[-1]
    step = pl.program_id(0)
    for u in range(2):
        own, beside, above, upper, lower = sources[5 * u:5 * u + 5]
        for v, source in enumerate((own, beside, above)):
            @pl.when(step == 4 * u + v)
            def _(source=source):
                out_ref[...] = source[...].astype(F32)

        @pl.when(step == 4 * u + 3)
        def _(upper=upper, lower=lower):
            middle = upper.shape[0]
            out_ref[:middle] = upper[...].astype(F32)
            out_ref[middle:] = lower[...].astype(F32)


def gather_tiles_by_core(n, t, tile_sum, chip, core, packs, along_z):
    in_plane = n // PLANES
    plane, seat = chip // in_plane, chip % in_plane
    tile_rows, cols = tile_sum.shape
    across = [
        (i * t + c, (i ^ 2 * in_plane) * t + c)
        for i in range(n) for c in range(t) if i // in_plane // 2 == c
    ]
    from_half = lax.ppermute(tile_sum, ("ctx", "tp"), across)

    def swap(x, k):
        return lax.ppermute(x, "ctx", [(i, i ^ k) for i in range(n)])

    first = jnp.where(plane // 2 == core, tile_sum, from_half)
    second = swap(first, in_plane)
    beside, above = swap(first, 1), swap(first, 2)
    second, beside, above, *packs = lax.optimization_barrier((second, beside, above, *packs))
    packs = along_z(packs)
    middle = tile_rows // 2
    sources = [first, beside, above, swap(beside[:middle], 2), swap(above[middle:], 1)]
    beside, above = swap(second, 1), swap(second, 2)
    sources += [second, beside, above, swap(beside[:middle], 2), swap(above[middle:], 1)]
    place = jnp.stack([plane % 2, seat]).astype(jnp.int32)
    return pl.pallas_call(
        place_xor_kernel,
        grid_spec=pltpu.PrefetchScalarGridSpec(
            num_scalar_prefetch=1,
            grid=(8,),
            in_specs=[whole_block(x.shape) for x in sources],
            out_specs=pl.BlockSpec(
                (tile_rows, cols), lambda s, place: (s // 4 ^ place[0], s % 4 ^ place[1])
            ),
        ),
        out_shape=jax.ShapeDtypeStruct((2 * tile_rows, in_plane * cols), F32),
        compiler_params=pltpu.CompilerParams(vmem_limit_bytes=48 * 2**20),
        cost_estimate=pl.CostEstimate(flops=0, bytes_accessed=2**24, transcendentals=0),
        name="place",
    )(place, *sources), packs


def per_device(n, t, queries, key_vectors, value_vectors, out_weight, out_grad, block_segment):
    rows, width = queries.shape
    heads_here = width // HEAD
    heads = heads_here * t
    sub = rows // t
    tile = min(sub, BLK)
    per_chunk = sub // tile
    core = lax.axis_index("tp")
    chip = lax.axis_index("ctx")
    in_plane = n // PLANES
    heads_plane = heads // PLANES
    seat = chip % in_plane

    def tp_swap(pick):
        got = [pick(core)]
        for s in range(1, t):
            got.append(lax.ppermute(pick((core + s) % t), "tp", shifts(t, s)))
        return [lax.select_n((core - p) % t, *got) for p in range(t)]

    def tp_gather(x):
        return tp_swap(lambda _: x)

    def shape(*dims):
        return jax.ShapeDtypeStruct(dims, BF16)

    where = jnp.stack([chip, core]).astype(jnp.int32)
    held = [(i % in_plane - i // in_plane) % in_plane < heads_plane for i in range(n)]

    chunk_row = jnp.arange(n)[:, None] * rows + jnp.arange(per_chunk)[None, :] * tile

    def tile_segments(part):
        return jnp.take(block_segment, ((chunk_row + part * sub) // BLK).reshape(-1))

    seg_parts = [tile_segments((core - s) % t) for s in range(t)]
    seg_q = seg_parts[0]
    seg_k = jnp.concatenate(seg_parts)
    full = (seg_q == 0) | (seg_q == TARGET)
    permitted = (seg_k[None] == 0) | (seg_k[None] == seg_q[:, None])
    total_blocks = block_segment.shape[0]
    count = (TXT_BLK + -(-(total_blocks - TXT_BLK) // RUNS)) * (BLK // tile)
    kcnt = jnp.sum(permitted.astype(jnp.int32), axis=1)
    tiles_k = seg_k.shape[0]
    ids = jnp.arange(tiles_k)
    place = jnp.sum((permitted[:, None, :] & (ids[None, None, :] < ids[None, :, None])).astype(jnp.int32), axis=2)
    hit = permitted[:, None, :] & (place[:, None, :] == jnp.arange(count)[None, :, None])
    kidx = jnp.sum(jnp.where(hit, ids[None, None, :], 0), axis=2).astype(jnp.int32)
    full = full.astype(jnp.int32)

    def other_rows(*arrays):
        return [
            lax.ppermute(
                jnp.stack([
                    lax.dynamic_slice_in_dim(x, (core + s) % t * sub, sub, 0) for x in arrays
                ]),
                "tp", shifts(t, s),
            )
            for s in range(1, t)
        ]

    got_qkv = other_rows(queries, key_vectors, value_vectors)

    half = out_grad.shape[1]
    model = half * t
    full_grad = jnp.concatenate(tp_gather(out_grad), axis=1)
    grad_attn = dot(full_grad, out_weight, NT).astype(BF16)
    got_g = other_rows(grad_attn)

    cols = model // in_plane
    mine = lax.dynamic_slice_in_dim(full_grad, core * sub, sub, 0)
    plane_got = [lax.dynamic_slice_in_dim(mine, seat * cols, cols, 1)]
    for k in range(1, in_plane):
        there = lax.dynamic_slice_in_dim(mine, (seat ^ k) * cols, cols, 1)
        plane_got.append(lax.ppermute(there, "ctx", [(i, i ^ k) for i in range(n)]))
    (plane_grad,) = simple_call(
        functools.partial(seats_kernel, in_plane), "seats", where, plane_got, [shape(in_plane, sub, cols)]
    )
    def along_z(packs):
        return [packs[0]] + [
            lax.ppermute(packs[k], "ctx", [(i, i ^ k * in_plane) for i in range(n)])
            for k in range(1, PLANES)
        ]

    def in_the_plane(packs, pairs):
        return [packs[0]] + [lax.ppermute(packs[m], "ctx", pairs(m)) for m in range(1, in_plane)]

    def to_held(m):
        return [(i, i ^ m) for i in range(n) if held[i ^ m]]

    def from_held(m):
        return [(i, i ^ m) for i in range(n) if held[i]]

    def pack(arrays, got):
        return simple_call(
            functools.partial(pack_kernel, n, t, len(arrays)), "pack", where,
            arrays + got, [shape(heads_plane, len(arrays), sub, HEAD)] * PLANES,
            [pltpu.VMEM((heads, len(arrays), sub, HEAD), BF16)],
        )

    def to_seats(packs):
        return simple_call(
            functools.partial(to_seats_kernel, n), "to_seats", where, packs,
            [shape(PLANES, packs[0].shape[1], sub, HEAD)] * in_plane,
        )

    length = n * sub
    seats_qkv = to_seats(along_z(pack([queries, key_vectors, value_vectors], got_qkv)))
    packs_g = pack([grad_attn], got_g)
    *seats_qkv, plane_grad, p0, p1, p2, p3 = lax.optimization_barrier((*seats_qkv, plane_grad, *packs_g))
    lines = [[a * in_plane + b for a in range(PLANES)] for b in range(in_plane)]
    slice_grad = lax.all_gather(plane_grad, "ctx", axis_index_groups=lines)
    slice_grad = slice_grad.reshape(length, cols)
    chunks = in_the_plane(seats_qkv, to_held)
    seats_g = to_seats(along_z([p0, p1, p2, p3]))
    tied = lax.optimization_barrier((*chunks, *seats_g))
    chunks, seats_g = list(tied[:in_plane]), list(tied[in_plane:])
    q_rows, kv = simple_call(
        functools.partial(join_kernel, n), "join", where, chunks, [shape(length, HEAD), shape(2, length, HEAD)]
    )
    (g_rows,) = simple_call(
        functools.partial(join_kernel, n), "join_g", where, in_the_plane(seats_g, to_held), [shape(length, HEAD)]
    )
    q_rows, g_rows = lax.optimization_barrier((q_rows, g_rows))
    kv_all = [kv] + [lax.ppermute(kv, "tp", shifts(t, s)) for s in range(1, t)]

    tiles_q = n * per_chunk
    few = [pltpu.VMEM((count * tile, HEAD), BF16)] * 2 + [pltpu.VMEM((tiles_k, tile, HEAD), BF16)] * 2
    params = pltpu.CompilerParams(vmem_limit_bytes=48 * 2**20)
    part_blocks = [one_array(0, length), one_array(1, length)] * t
    part_arrays = [a for pack in kv_all for a in (pack, pack)]
    row_block = pl.BlockSpec((tile, HEAD), lambda r, *_: (r, 0))
    attn, lse = pl.pallas_call(
        functools.partial(forward_kernel, t, tile, count),
        grid_spec=pltpu.PrefetchScalarGridSpec(
            num_scalar_prefetch=3,
            grid=(tiles_q,),
            in_specs=[row_block] + part_blocks,
            out_specs=[row_block, row_block],
            scratch_shapes=few,
        ),
        out_shape=[shape(length, HEAD), jax.ShapeDtypeStruct((length, HEAD), F32)],
        compiler_params=params,
        cost_estimate=pl.CostEstimate(flops=16 * 10**9, bytes_accessed=5 * 2**20, transcendentals=2**22),
        name="forward",
    )(full, kcnt, kidx, q_rows, *part_arrays)

    travel = [attn] + [
        lax.ppermute(attn, "ctx", [(i, i ^ k) for i in range(n) if held[i]]) for k in range(1, in_plane)
    ]
    dq, *dkv = pl.pallas_call(
        functools.partial(backward_kernel, t, tile, count),
        grid_spec=pltpu.PrefetchScalarGridSpec(
            num_scalar_prefetch=3,
            grid=(tiles_q,),
            in_specs=[row_block] * 4 + part_blocks,
            out_specs=[row_block] + [whole_block((2, length, HEAD))] * t,
            scratch_shapes=few + [pltpu.VMEM((tiles_k, tile, HEAD), F32)] * 2,
        ),
        out_shape=[shape(length, HEAD)] + [shape(2, length, HEAD)] * t,
        compiler_params=params,
        cost_estimate=pl.CostEstimate(flops=20 * 10**9, bytes_accessed=8 * 2**20, transcendentals=2**22),
        name="backward",
    )(full, kcnt, kidx, q_rows, g_rows, attn, lse, *part_arrays)

    got_dkv = [
        lax.ppermute(dkv[s], "tp", [(c, (c - s) % t) for c in range(t)]) for s in range(1, t)
    ]
    back = simple_call(
        functools.partial(unjoin_kernel, n, t), "unjoin", where,
        [attn, dq, dkv[0]] + got_dkv, [shape(PLANES, 4, sub, HEAD)] * in_plane,
    )
    tied = lax.optimization_barrier((*travel, *back))
    travel, back = list(tied[:in_plane]), list(tied[in_plane:])
    packs = simple_call(
        functools.partial(to_planes_kernel, n), "to_planes", where, in_the_plane(back, from_held),
        [shape(heads_plane, 4, sub, HEAD)] * PLANES,
    )

    tile_rows = heads_plane * HEAD
    by_core = in_plane == 4 and t == 2
    piece = tile_rows if by_core else tile_rows // t
    step_rows = length // 4
    tile_own, *tile_sends = pl.pallas_call(
        functools.partial(tile_kernel, in_plane, heads_plane, t),
        grid_spec=pltpu.PrefetchScalarGridSpec(
            num_scalar_prefetch=1,
            grid=(4,),
            in_specs=[pl.BlockSpec((step_rows, HEAD), lambda r, *_: (r, 0))] * in_plane
            + [pl.BlockSpec((step_rows, cols), lambda r, *_: (r, 0))],
            out_specs=[whole_block((piece, cols))] * t,
            scratch_shapes=[
                pltpu.VMEM((in_plane, step_rows, HEAD), BF16), pltpu.VMEM((tile_rows, cols), F32)
            ],
        ),
        out_shape=[jax.ShapeDtypeStruct((piece, cols), F32)] + [shape(piece, cols)] * (t - 1),
        compiler_params=params,
        cost_estimate=pl.CostEstimate(flops=5 * 10**9, bytes_accessed=2**22, transcendentals=0),
        name="tile",
    )(where, *travel, slice_grad)
    tile_sum = tile_own
    for s in range(1, t):
        tile_sum = tile_sum + lax.ppermute(tile_sends[s - 1], "tp", shifts(t, s)).astype(F32)
    if by_core:
        grad_weight, back = gather_tiles_by_core(
            n, t, tile_sum.astype(BF16), chip, core, packs, along_z
        )
    else:
        back = along_z(packs)
        tiles = lax.all_gather(tile_sum.astype(BF16), "ctx")
        here = n // t
        tiles_core = [tiles] + [
            lax.ppermute(
                lax.dynamic_slice_in_dim(tiles, (core + s) % t * here, here, 0), "tp", shifts(t, s)
            )
            for s in range(1, t)
        ]
        grad_weight = pl.pallas_call(
            functools.partial(place_kernel, t),
            grid_spec=pltpu.PrefetchScalarGridSpec(
                num_scalar_prefetch=1,
                grid=(here,),
                in_specs=[pl.BlockSpec((1, piece, cols), lambda r, where: (where[1] * here + r, 0, 0))]
                + [pl.BlockSpec((1, piece, cols), lambda r, *_: (r, 0, 0))] * (t - 1),
                out_specs=pl.BlockSpec((tile_rows, cols), lambda r, *_: (r // in_plane, r % in_plane)),
            ),
            out_shape=jax.ShapeDtypeStruct((width, model), F32),
            compiler_params=params,
            cost_estimate=pl.CostEstimate(flops=0, bytes_accessed=2**24, transcendentals=0),
            name="place",
        )(where, *tiles_core)

    mine = simple_call(
        functools.partial(by_core_kernel, n, t), "by_core", where, back,
        [shape(heads_here, 4, sub, HEAD)] * t, [pltpu.VMEM((heads, 4, sub, HEAD), BF16)],
    )
    parts = [mine[0]] + [lax.ppermute(mine[s], "tp", shifts(t, s)) for s in range(1, t)]
    attention, grad_queries, grad_keys, grad_values = simple_call(
        functools.partial(unpack_kernel, t), "unpack", where, parts, [shape(rows, width)] * 4
    )
    projected = dot(attention, out_weight)
    own = lax.dynamic_slice_in_dim(projected, core * half, half, 1)
    for s in range(1, t):
        there = lax.dynamic_slice_in_dim(projected, (core + s) % t * half, half, 1)
        own = own + lax.ppermute(there.astype(BF16), "tp", shifts(t, s)).astype(F32)
    attention_out = own.astype(BF16)

    return attention_out, grad_queries, grad_keys, grad_values, grad_weight


def solution(mesh):
    n, t = mesh.shape["ctx"], mesh.shape["tp"]
    in_specs = (P("ctx", "tp"), P("ctx", "tp"), P("ctx", "tp"), P("tp", None), P("ctx", "tp"), P())
    out_specs = (P("ctx", "tp"), P("ctx", "tp"), P("ctx", "tp"), P("ctx", "tp"), P("tp", None))
    return jax.shard_map(
        functools.partial(per_device, n, t), mesh=mesh, in_specs=in_specs, out_specs=out_specs, check_vma=False
    )
```

```python
import functools
import math

import jax
import jax.numpy as jnp
from jax import lax
from jax.experimental import pallas as pl
from jax.experimental.pallas import tpu as pltpu
from jax.sharding import PartitionSpec as P

HEAD = 128
BLK = 128
TXT_BLK = 4
RUNS = 5
TARGET = 5
PLANES = 4
LOG2E = math.log2(math.e)
NEG_BIG = -1e30

NT = (((1,), (1,)), ((), ()))
TN = (((0,), (0,)), ((), ()))
F32 = jnp.float32
BF16 = jnp.bfloat16


def dot(a, b, dims=(((1,), (0,)), ((), ()))):
    return lax.dot_general(a, b, dims, preferred_element_type=F32)


def gather_tiles(k_ref, kidx_ref, row, dst, tile, count):
    for j in range(count):
        dst[pl.ds(j * tile, tile), :] = k_ref[kidx_ref[row, j]]


def join_parts(parts, k_all, v_all):
    shape = (k_all.shape[0] // (len(parts) // 2),) + k_all.shape[1:]
    for s in range(len(parts) // 2):
        at = pl.ds(s * shape[0], shape[0])
        k_all[at] = parts[2 * s][...].reshape(shape)
        v_all[at] = parts[2 * s + 1][...].reshape(shape)


def head_of(chip, in_plane, heads_plane):
    place = (chip % in_plane - chip // in_plane) % in_plane
    return place < heads_plane, chip // in_plane * heads_plane + min(place, heads_plane - 1)


def pack_kernel(n, t, count, where_ref, *refs):
    arrays, got, (out_ref, heads_all) = refs[:count], refs[count:count + t - 1], refs[count + t - 1:]
    core = where_ref[1]
    sub = heads_all.shape[2]
    heads_here = heads_all.shape[0] // t
    for a in range(count):
        for h in range(heads_here):
            column = pl.ds(h * HEAD, HEAD)
            heads_all[core * heads_here + h, a] = arrays[a][pl.ds(core * sub, sub), column]
            for s in range(1, t):
                first = (core + t - s) % t * heads_here
                heads_all[first + h, a] = got[s - 1][a, :, column]
    for k in range(n):
        held, head = head_of(k, n // PLANES, heads_all.shape[0] // PLANES)
        out_ref[k] = heads_all[head] if held else jnp.zeros_like(heads_all[0])


def join_kernel(n, where_ref, chunks_ref, q_ref, kv_ref):
    sub = chunks_ref.shape[2]
    for k in range(n):
        at = pl.ds(k * sub, sub)
        q_ref[at] = chunks_ref[k, 0]
        kv_ref[0, at] = chunks_ref[k, 1]
        kv_ref[1, at] = chunks_ref[k, 2]


def unjoin_kernel(n, t, where_ref, attn_ref, dq_ref, dkv_ref, *refs):
    got, out_ref = refs[:t - 1], refs[t - 1]
    sub = out_ref.shape[2]
    for k in range(n):
        at = pl.ds(k * sub, sub)
        out_ref[k, 0] = attn_ref[at]
        out_ref[k, 1] = dq_ref[at]
        for a in range(2):
            total = dkv_ref[a, at].astype(F32)
            for other in got:
                total = total + other[a, at].astype(F32)
            out_ref[k, 2 + a] = total.astype(BF16)


def by_core_kernel(n, t, where_ref, chunks_ref, *refs):
    outs, heads_all = refs[:t], refs[t]
    core = where_ref[1]
    heads_here = heads_all.shape[0] // t
    for k in range(n):
        held, head = head_of(k, n // PLANES, heads_all.shape[0] // PLANES)
        if held:
            heads_all[head] = chunks_ref[k]
    for s in range(t):
        outs[s][...] = heads_all[pl.ds((core + s) % t * heads_here, heads_here)]


def seats_kernel(in_plane, where_ref, *refs):
    got, out_ref = refs[:in_plane], refs[in_plane]
    seat = where_ref[0] % in_plane
    for k in range(in_plane):
        out_ref[seat ^ k] = got[k][...]


def tile_kernel(in_plane, heads_plane, t, where_ref, *refs):
    attns, (grad_ref, own_ref), sends = refs[:in_plane], refs[in_plane:in_plane + 2], refs[in_plane + 2:-2]
    seats, total = refs[-2:]
    chip, core = where_ref[0], where_ref[1]
    seat = chip % in_plane
    plane = chip // in_plane
    step = pl.program_id(0)
    for k in range(in_plane):
        seats[seat ^ k] = attns[k][...]

    @pl.when(step == 0)
    def _():
        total[...] = jnp.zeros_like(total)

    grad = grad_ref[...]
    for j in range(heads_plane):
        total[pl.ds(j * HEAD, HEAD)] += dot(seats[(plane + j) % in_plane], grad, TN)

    @pl.when(step == pl.num_programs(0) - 1)
    def _():
        piece = own_ref.shape[0]
        if piece == total.shape[0]:
            own_ref[...] = total[...]
            sends[0][...] = total[...].astype(BF16)
            return
        own_ref[...] = total[pl.ds(pl.multiple_of(core * piece, piece), piece)]
        for s in range(1, t):
            at = pl.ds(pl.multiple_of((core + s) % t * piece, piece), piece)
            sends[s - 1][...] = total[at].astype(BF16)


def place_kernel(t, where_ref, *refs):
    parts, out_ref = refs[:t], refs[t]
    core = where_ref[1]
    piece = parts[0].shape[1]
    for s in range(t):
        at = pl.ds(pl.multiple_of((core + t - s) % t * piece, piece), piece)
        out_ref[at] = parts[s][0].astype(F32)


def unpack_kernel(t, where_ref, *refs):
    parts, outs = refs[:t], refs[t:]
    core = where_ref[1]
    heads_here, _, sub, _ = parts[0].shape
    for s in range(t):
        at = pl.ds(pl.multiple_of((core + t - s) % t * sub, sub), sub)
        for a in range(4):
            for h in range(heads_here):
                outs[a][at, pl.ds(h * HEAD, HEAD)] = parts[s][h, a]


def forward_kernel(t, tile, count, full_ref, kcnt_ref, kidx_ref, q_ref, *refs):
    parts, (out_ref, lse_ref, k_few, v_few, k_ref, v_ref) = refs[:2 * t], refs[2 * t:]
    row = pl.program_id(0)
    q = q_ref[...]

    @pl.when(row == 0)
    def _():
        join_parts(parts, k_ref, v_ref)

    def finish(s, v):
        top = jnp.max(s, axis=1, keepdims=True)
        p = jnp.exp2(s - top)
        mass = jnp.sum(p, axis=1, keepdims=True)
        out = dot(p.astype(BF16), v)
        out_ref[...] = (out / mass).astype(BF16)
        lse_ref[...] = jnp.broadcast_to(top + jnp.log2(mass), lse_ref.shape)

    scale = HEAD ** -0.5 * LOG2E

    @pl.when(full_ref[row] == 1)
    def _():
        keys = k_ref[...].reshape(-1, HEAD)
        finish(dot(q, keys, NT) * scale, v_ref[...].reshape(-1, HEAD))

    @pl.when(full_ref[row] == 0)
    def _():
        gather_tiles(k_ref, kidx_ref, row, k_few, tile, count)
        gather_tiles(v_ref, kidx_ref, row, v_few, tile, count)
        s = dot(q, k_few[...], NT) * scale
        column = lax.broadcasted_iota(jnp.int32, s.shape, 1)
        s = jnp.where(column < kcnt_ref[row] * tile, s, NEG_BIG)
        finish(s, v_few[...])


def backward_kernel(t, tile, count, full_ref, kcnt_ref, kidx_ref, q_ref, g_ref, o_ref, lse_ref, *refs):
    parts, dkv_refs = refs[:2 * t], refs[2 * t + 1:3 * t + 1]
    dq_ref = refs[2 * t]
    k_few, v_few, k_ref, v_ref, dk_acc, dv_acc = refs[3 * t + 1:]
    row = pl.program_id(0)
    last = pl.num_programs(0) - 1

    @pl.when(row == 0)
    def _():
        join_parts(parts, k_ref, v_ref)
        dk_acc[...] = jnp.zeros_like(dk_acc)
        dv_acc[...] = jnp.zeros_like(dv_acc)

    q = q_ref[...]
    g = g_ref[...]
    delta = jnp.sum(g.astype(F32) * o_ref[...].astype(F32), axis=1, keepdims=True)
    lse = lse_ref[:, :1]
    unit = HEAD ** -0.5
    scale = unit * LOG2E

    def gradients(keys, values, mask):
        s = dot(q, keys, NT)
        p = jnp.exp2(s * scale - lse)
        if mask is not None:
            p = jnp.where(mask(p.shape), p, 0.0)
        ds = (p * (dot(g, values, NT) - delta)).astype(BF16)
        dq_ref[...] = (dot(ds, keys) * unit).astype(BF16)
        return dot(ds, q, TN) * unit, dot(p.astype(BF16), g, TN)

    @pl.when(full_ref[row] == 1)
    def _():
        dk, dv = gradients(k_ref[...].reshape(-1, HEAD), v_ref[...].reshape(-1, HEAD), None)
        dk_acc[...] += dk.reshape(dk_acc.shape)
        dv_acc[...] += dv.reshape(dv_acc.shape)

    @pl.when(full_ref[row] == 0)
    def _():
        gather_tiles(k_ref, kidx_ref, row, k_few, tile, count)
        gather_tiles(v_ref, kidx_ref, row, v_few, tile, count)

        def mask(shape):
            return lax.broadcasted_iota(jnp.int32, shape, 1) < kcnt_ref[row] * tile

        dk, dv = gradients(k_few[...], v_few[...], mask)
        for j in range(count):
            at = kidx_ref[row, j]
            dk_acc[at] += dk[j * tile:(j + 1) * tile]
            dv_acc[at] += dv[j * tile:(j + 1) * tile]

    @pl.when(row == last)
    def _():
        tiles = dk_acc.shape[0] // t
        for s, dkv_ref in enumerate(dkv_refs):
            at = pl.ds(s * tiles, tiles)
            dkv_ref[0] = dk_acc[at].reshape(dkv_ref.shape[1:]).astype(BF16)
            dkv_ref[1] = dv_acc[at].reshape(dkv_ref.shape[1:]).astype(BF16)


def whole_block(shape):
    return pl.BlockSpec(shape, lambda *_: (0,) * len(shape))


def one_array(which, length):
    return pl.BlockSpec((1, length, HEAD), lambda *_: (which, 0, 0))


def simple_call(kernel, name, scalars, inputs, outputs, scratch=()):
    size = sum(2 * math.prod(x.shape) for x in list(inputs) + list(outputs))
    return pl.pallas_call(
        kernel,
        grid_spec=pltpu.PrefetchScalarGridSpec(
            num_scalar_prefetch=1,
            grid=(1,),
            in_specs=[whole_block(x.shape) for x in inputs],
            out_specs=[whole_block(x.shape) for x in outputs],
            scratch_shapes=scratch,
        ),
        out_shape=outputs,
        compiler_params=pltpu.CompilerParams(vmem_limit_bytes=48 * 2**20),
        cost_estimate=pl.CostEstimate(flops=0, bytes_accessed=2 * size, transcendentals=0),
        name=name,
    )(scalars, *inputs)


def shifts(t, s):
    return [(c, (c + s) % t) for c in range(t)]


def place_xor_kernel(place_ref, *refs):
    sources, out_ref = refs[:-1], refs[-1]
    step = pl.program_id(0)
    for u in range(2):
        own, beside, above, upper, lower = sources[5 * u:5 * u + 5]
        for v, source in enumerate((own, beside, above)):
            @pl.when(step == 4 * u + v)
            def _(source=source):
                out_ref[...] = source[...].astype(F32)

        @pl.when(step == 4 * u + 3)
        def _(upper=upper, lower=lower):
            middle = upper.shape[0]
            out_ref[:middle] = upper[...].astype(F32)
            out_ref[middle:] = lower[...].astype(F32)


def gather_tiles_by_core(n, t, tile_sum, chip, core, beside_chunks):
    in_plane = n // PLANES
    plane, seat = chip // in_plane, chip % in_plane
    tile_rows, cols = tile_sum.shape
    across = [
        (i * t + c, (i ^ 2 * in_plane) * t + c)
        for i in range(n) for c in range(t) if i // in_plane // 2 == c
    ]
    from_half = lax.ppermute(tile_sum, ("ctx", "tp"), across)

    def swap(x, k):
        return lax.ppermute(x, "ctx", [(i, i ^ k) for i in range(n)])

    first = jnp.where(plane // 2 == core, tile_sum, from_half)
    second = swap(first, in_plane)
    beside, above = swap(first, 1), swap(first, 2)
    second, beside, above, beside_chunks = lax.optimization_barrier((second, beside, above, beside_chunks))
    middle = tile_rows // 2
    sources = [first, beside, above, swap(beside[:middle], 2), swap(above[middle:], 1)]
    beside, above = swap(second, 1), swap(second, 2)
    sources += [second, beside, above, swap(beside[:middle], 2), swap(above[middle:], 1)]
    place = jnp.stack([plane % 2, seat]).astype(jnp.int32)
    return pl.pallas_call(
        place_xor_kernel,
        grid_spec=pltpu.PrefetchScalarGridSpec(
            num_scalar_prefetch=1,
            grid=(8,),
            in_specs=[whole_block(x.shape) for x in sources],
            out_specs=pl.BlockSpec(
                (tile_rows, cols), lambda s, place: (s // 4 ^ place[0], s % 4 ^ place[1])
            ),
        ),
        out_shape=jax.ShapeDtypeStruct((2 * tile_rows, in_plane * cols), F32),
        compiler_params=pltpu.CompilerParams(vmem_limit_bytes=48 * 2**20),
        cost_estimate=pl.CostEstimate(flops=0, bytes_accessed=2**24, transcendentals=0),
        name="place",
    )(place, *sources), beside_chunks


def per_device(n, t, queries, key_vectors, value_vectors, out_weight, out_grad, block_segment):
    rows, width = queries.shape
    heads_here = width // HEAD
    heads = heads_here * t
    sub = rows // t
    tile = min(sub, BLK)
    per_chunk = sub // tile
    core = lax.axis_index("tp")
    chip = lax.axis_index("ctx")
    in_plane = n // PLANES
    heads_plane = heads // PLANES
    seat = chip % in_plane

    def tp_swap(pick):
        got = [pick(core)]
        for s in range(1, t):
            got.append(lax.ppermute(pick((core + s) % t), "tp", shifts(t, s)))
        return [lax.select_n((core - p) % t, *got) for p in range(t)]

    def tp_gather(x):
        return tp_swap(lambda _: x)

    def shape(*dims):
        return jax.ShapeDtypeStruct(dims, BF16)

    where = jnp.stack([chip, core]).astype(jnp.int32)
    held = [(i % in_plane - i // in_plane) % in_plane < heads_plane for i in range(n)]

    chunk_row = jnp.arange(n)[:, None] * rows + jnp.arange(per_chunk)[None, :] * tile

    def tile_segments(part):
        return jnp.take(block_segment, ((chunk_row + part * sub) // BLK).reshape(-1))

    seg_parts = [tile_segments((core - s) % t) for s in range(t)]
    seg_q = seg_parts[0]
    seg_k = jnp.concatenate(seg_parts)
    full = (seg_q == 0) | (seg_q == TARGET)
    permitted = (seg_k[None] == 0) | (seg_k[None] == seg_q[:, None])
    total_blocks = block_segment.shape[0]
    count = (TXT_BLK + -(-(total_blocks - TXT_BLK) // RUNS)) * (BLK // tile)
    kcnt = jnp.sum(permitted.astype(jnp.int32), axis=1)
    tiles_k = seg_k.shape[0]
    ids = jnp.arange(tiles_k)
    place = jnp.sum((permitted[:, None, :] & (ids[None, None, :] < ids[None, :, None])).astype(jnp.int32), axis=2)
    hit = permitted[:, None, :] & (place[:, None, :] == jnp.arange(count)[None, :, None])
    kidx = jnp.sum(jnp.where(hit, ids[None, None, :], 0), axis=2).astype(jnp.int32)
    full = full.astype(jnp.int32)

    def other_rows(*arrays):
        return [
            lax.ppermute(
                jnp.stack([
                    lax.dynamic_slice_in_dim(x, (core + s) % t * sub, sub, 0) for x in arrays
                ]),
                "tp", shifts(t, s),
            )
            for s in range(1, t)
        ]

    got_qkv = other_rows(queries, key_vectors, value_vectors)

    half = out_grad.shape[1]
    model = half * t
    full_grad = jnp.concatenate(tp_gather(out_grad), axis=1)
    grad_attn = dot(full_grad, out_weight, NT).astype(BF16)
    got_g = other_rows(grad_attn)

    cols = model // in_plane
    mine = lax.dynamic_slice_in_dim(full_grad, core * sub, sub, 0)
    plane_got = [lax.dynamic_slice_in_dim(mine, seat * cols, cols, 1)]
    for k in range(1, in_plane):
        there = lax.dynamic_slice_in_dim(mine, (seat ^ k) * cols, cols, 1)
        plane_got.append(lax.ppermute(there, "ctx", [(i, i ^ k) for i in range(n)]))
    (plane_grad,) = simple_call(
        functools.partial(seats_kernel, in_plane), "seats", where, plane_got, [shape(in_plane, sub, cols)]
    )
    def pack(arrays, got):
        (sent,) = simple_call(
            functools.partial(pack_kernel, n, t, len(arrays)), "pack", where,
            arrays + got, [shape(n, len(arrays), sub, HEAD)],
            [pltpu.VMEM((heads, len(arrays), sub, HEAD), BF16)],
        )
        return sent

    sent_qkv = pack([queries, key_vectors, value_vectors], got_qkv)
    sent_g = pack([grad_attn], got_g)
    chunks = lax.all_to_all(sent_qkv, "ctx", 0, 0, tiled=True)
    chunks, sent_g, plane_grad = lax.optimization_barrier((chunks, sent_g, plane_grad))
    lines = [[a * in_plane + b for a in range(PLANES)] for b in range(in_plane)]
    slice_grad = lax.all_gather(plane_grad, "ctx", axis_index_groups=lines)
    slice_grad = slice_grad.reshape(n * sub, cols)
    g_rows = lax.all_to_all(sent_g, "ctx", 0, 0, tiled=True).reshape(n * sub, HEAD)
    length = n * sub
    q_rows, kv = simple_call(
        functools.partial(join_kernel, n), "join", where, [chunks], [shape(length, HEAD), shape(2, length, HEAD)]
    )
    kv_all = [kv] + [lax.ppermute(kv, "tp", shifts(t, s)) for s in range(1, t)]

    tiles_q = n * per_chunk
    few = [pltpu.VMEM((count * tile, HEAD), BF16)] * 2 + [pltpu.VMEM((tiles_k, tile, HEAD), BF16)] * 2
    params = pltpu.CompilerParams(vmem_limit_bytes=48 * 2**20)
    part_blocks = [one_array(0, length), one_array(1, length)] * t
    part_arrays = [a for pack in kv_all for a in (pack, pack)]
    row_block = pl.BlockSpec((tile, HEAD), lambda r, *_: (r, 0))
    attn, lse = pl.pallas_call(
        functools.partial(forward_kernel, t, tile, count),
        grid_spec=pltpu.PrefetchScalarGridSpec(
            num_scalar_prefetch=3,
            grid=(tiles_q,),
            in_specs=[row_block] + part_blocks,
            out_specs=[row_block, row_block],
            scratch_shapes=few,
        ),
        out_shape=[shape(length, HEAD), jax.ShapeDtypeStruct((length, HEAD), F32)],
        compiler_params=params,
        cost_estimate=pl.CostEstimate(flops=16 * 10**9, bytes_accessed=5 * 2**20, transcendentals=2**22),
        name="forward",
    )(full, kcnt, kidx, q_rows, *part_arrays)

    dq, *dkv = pl.pallas_call(
        functools.partial(backward_kernel, t, tile, count),
        grid_spec=pltpu.PrefetchScalarGridSpec(
            num_scalar_prefetch=3,
            grid=(tiles_q,),
            in_specs=[row_block] * 4 + part_blocks,
            out_specs=[row_block] + [whole_block((2, length, HEAD))] * t,
            scratch_shapes=few + [pltpu.VMEM((tiles_k, tile, HEAD), F32)] * 2,
        ),
        out_shape=[shape(length, HEAD)] + [shape(2, length, HEAD)] * t,
        compiler_params=params,
        cost_estimate=pl.CostEstimate(flops=20 * 10**9, bytes_accessed=8 * 2**20, transcendentals=2**22),
        name="backward",
    )(full, kcnt, kidx, q_rows, g_rows, attn, lse, *part_arrays)

    got_dkv = [
        lax.ppermute(dkv[s], "tp", [(c, (c - s) % t) for c in range(t)]) for s in range(1, t)
    ]
    (sent,) = simple_call(
        functools.partial(unjoin_kernel, n, t), "unjoin", where,
        [attn, dq, dkv[0]] + got_dkv, [shape(n, 4, sub, HEAD)],
    )
    sent, attn = lax.optimization_barrier((sent, attn))
    chunks = lax.all_to_all(sent, "ctx", 0, 0, tiled=True)
    travel = [attn] + [
        lax.ppermute(attn, "ctx", [(i, i ^ k) for i in range(n) if held[i]]) for k in range(1, in_plane)
    ]

    tile_rows = heads_plane * HEAD
    by_core = in_plane == 4 and t == 2
    piece = tile_rows if by_core else tile_rows // t
    step_rows = length // 4
    tile_own, *tile_sends = pl.pallas_call(
        functools.partial(tile_kernel, in_plane, heads_plane, t),
        grid_spec=pltpu.PrefetchScalarGridSpec(
            num_scalar_prefetch=1,
            grid=(4,),
            in_specs=[pl.BlockSpec((step_rows, HEAD), lambda r, *_: (r, 0))] * in_plane
            + [pl.BlockSpec((step_rows, cols), lambda r, *_: (r, 0))],
            out_specs=[whole_block((piece, cols))] * t,
            scratch_shapes=[
                pltpu.VMEM((in_plane, step_rows, HEAD), BF16), pltpu.VMEM((tile_rows, cols), F32)
            ],
        ),
        out_shape=[jax.ShapeDtypeStruct((piece, cols), F32)] + [shape(piece, cols)] * (t - 1),
        compiler_params=params,
        cost_estimate=pl.CostEstimate(flops=5 * 10**9, bytes_accessed=2**22, transcendentals=0),
        name="tile",
    )(where, *travel, slice_grad)
    tile_sum = tile_own
    for s in range(1, t):
        tile_sum = tile_sum + lax.ppermute(tile_sends[s - 1], "tp", shifts(t, s)).astype(F32)
    if by_core:
        grad_weight, chunks = gather_tiles_by_core(n, t, tile_sum.astype(BF16), chip, core, chunks)
    else:
        tiles = lax.all_gather(tile_sum.astype(BF16), "ctx")
        here = n // t
        tiles_core = [tiles] + [
            lax.ppermute(
                lax.dynamic_slice_in_dim(tiles, (core + s) % t * here, here, 0), "tp", shifts(t, s)
            )
            for s in range(1, t)
        ]
        grad_weight = pl.pallas_call(
            functools.partial(place_kernel, t),
            grid_spec=pltpu.PrefetchScalarGridSpec(
                num_scalar_prefetch=1,
                grid=(here,),
                in_specs=[pl.BlockSpec((1, piece, cols), lambda r, where: (where[1] * here + r, 0, 0))]
                + [pl.BlockSpec((1, piece, cols), lambda r, *_: (r, 0, 0))] * (t - 1),
                out_specs=pl.BlockSpec((tile_rows, cols), lambda r, *_: (r // in_plane, r % in_plane)),
            ),
            out_shape=jax.ShapeDtypeStruct((width, model), F32),
            compiler_params=params,
            cost_estimate=pl.CostEstimate(flops=0, bytes_accessed=2**24, transcendentals=0),
            name="place",
        )(where, *tiles_core)

    mine = simple_call(
        functools.partial(by_core_kernel, n, t), "by_core", where, [chunks],
        [shape(heads_here, 4, sub, HEAD)] * t, [pltpu.VMEM((heads, 4, sub, HEAD), BF16)],
    )
    parts = [mine[0]] + [lax.ppermute(mine[s], "tp", shifts(t, s)) for s in range(1, t)]
    attention, grad_queries, grad_keys, grad_values = simple_call(
        functools.partial(unpack_kernel, t), "unpack", where, parts, [shape(rows, width)] * 4
    )
    projected = dot(attention, out_weight)
    own = lax.dynamic_slice_in_dim(projected, core * half, half, 1)
    for s in range(1, t):
        there = lax.dynamic_slice_in_dim(projected, (core + s) % t * half, half, 1)
        own = own + lax.ppermute(there.astype(BF16), "tp", shifts(t, s)).astype(F32)
    attention_out = own.astype(BF16)

    return attention_out, grad_queries, grad_keys, grad_values, grad_weight


def solution(mesh):
    n, t = mesh.shape["ctx"], mesh.shape["tp"]
    in_specs = (P("ctx", "tp"), P("ctx", "tp"), P("ctx", "tp"), P("tp", None), P("ctx", "tp"), P())
    out_specs = (P("ctx", "tp"), P("ctx", "tp"), P("ctx", "tp"), P("ctx", "tp"), P("tp", None))
    return jax.shard_map(
        functools.partial(per_device, n, t), mesh=mesh, in_specs=in_specs, out_specs=out_specs, check_vma=False
    )
```

```python
import functools
import math

import jax
import jax.numpy as jnp
from jax import lax
from jax.experimental import pallas as pl
from jax.experimental.pallas import tpu as pltpu
from jax.sharding import PartitionSpec as P

HEAD = 128
BLK = 128
TXT_BLK = 4
RUNS = 5
TARGET = 5
PLANES = 4
LOG2E = math.log2(math.e)
NEG_BIG = -1e30

NT = (((1,), (1,)), ((), ()))
TN = (((0,), (0,)), ((), ()))
F32 = jnp.float32
BF16 = jnp.bfloat16


def dot(a, b, dims=(((1,), (0,)), ((), ()))):
    return lax.dot_general(a, b, dims, preferred_element_type=F32)


def gather_tiles(k_ref, kidx_ref, row, dst, tile, count):
    for j in range(count):
        dst[pl.ds(j * tile, tile), :] = k_ref[kidx_ref[row, j]]


def join_parts(parts, k_all, v_all):
    shape = (k_all.shape[0] // (len(parts) // 2),) + k_all.shape[1:]
    for s in range(len(parts) // 2):
        at = pl.ds(s * shape[0], shape[0])
        k_all[at] = parts[2 * s][...].reshape(shape)
        v_all[at] = parts[2 * s + 1][...].reshape(shape)


def head_of(chip, in_plane, heads_plane):
    place = (chip % in_plane - chip // in_plane) % in_plane
    return place < heads_plane, chip // in_plane * heads_plane + min(place, heads_plane - 1)


def pack_kernel(n, t, count, where_ref, *refs):
    arrays, got, (out_ref, heads_all) = refs[:count], refs[count:count + t - 1], refs[count + t - 1:]
    core = where_ref[1]
    sub = heads_all.shape[2]
    heads_here = heads_all.shape[0] // t
    for a in range(count):
        for h in range(heads_here):
            column = pl.ds(h * HEAD, HEAD)
            heads_all[core * heads_here + h, a] = arrays[a][pl.ds(core * sub, sub), column]
            for s in range(1, t):
                first = (core + t - s) % t * heads_here
                heads_all[first + h, a] = got[s - 1][a, :, column]
    for k in range(n):
        held, head = head_of(k, n // PLANES, heads_all.shape[0] // PLANES)
        out_ref[k] = heads_all[head] if held else jnp.zeros_like(heads_all[0])


def join_kernel(n, where_ref, chunks_ref, q_ref, kv_ref):
    sub = chunks_ref.shape[2]
    for k in range(n):
        at = pl.ds(k * sub, sub)
        q_ref[at] = chunks_ref[k, 0]
        kv_ref[0, at] = chunks_ref[k, 1]
        kv_ref[1, at] = chunks_ref[k, 2]


def unjoin_kernel(n, t, where_ref, attn_ref, dq_ref, dkv_ref, *refs):
    got, out_ref = refs[:t - 1], refs[t - 1]
    sub = out_ref.shape[2]
    for k in range(n):
        at = pl.ds(k * sub, sub)
        out_ref[k, 0] = attn_ref[at]
        out_ref[k, 1] = dq_ref[at]
        for a in range(2):
            total = dkv_ref[a, at].astype(F32)
            for other in got:
                total = total + other[a, at].astype(F32)
            out_ref[k, 2 + a] = total.astype(BF16)


def by_core_kernel(n, t, where_ref, chunks_ref, *refs):
    outs, heads_all = refs[:t], refs[t]
    core = where_ref[1]
    heads_here = heads_all.shape[0] // t
    for k in range(n):
        held, head = head_of(k, n // PLANES, heads_all.shape[0] // PLANES)
        if held:
            heads_all[head] = chunks_ref[k]
    for s in range(t):
        outs[s][...] = heads_all[pl.ds((core + s) % t * heads_here, heads_here)]


def seats_kernel(in_plane, where_ref, *refs):
    got, out_ref = refs[:in_plane], refs[in_plane]
    seat = where_ref[0] % in_plane
    for k in range(in_plane):
        out_ref[seat ^ k] = got[k][...]


def tile_kernel(in_plane, heads_plane, t, where_ref, *refs):
    attns, (grad_ref, own_ref), sends = refs[:in_plane], refs[in_plane:in_plane + 2], refs[in_plane + 2:-2]
    seats, total = refs[-2:]
    chip, core = where_ref[0], where_ref[1]
    seat = chip % in_plane
    plane = chip // in_plane
    step = pl.program_id(0)
    for k in range(in_plane):
        seats[seat ^ k] = attns[k][...]

    @pl.when(step == 0)
    def _():
        total[...] = jnp.zeros_like(total)

    grad = grad_ref[...]
    for j in range(heads_plane):
        total[pl.ds(j * HEAD, HEAD)] += dot(seats[(plane + j) % in_plane], grad, TN)

    @pl.when(step == pl.num_programs(0) - 1)
    def _():
        piece = own_ref.shape[0]
        if piece == total.shape[0]:
            own_ref[...] = total[...]
            sends[0][...] = total[...].astype(BF16)
            return
        own_ref[...] = total[pl.ds(pl.multiple_of(core * piece, piece), piece)]
        for s in range(1, t):
            at = pl.ds(pl.multiple_of((core + s) % t * piece, piece), piece)
            sends[s - 1][...] = total[at].astype(BF16)


def place_kernel(t, where_ref, *refs):
    parts, out_ref = refs[:t], refs[t]
    core = where_ref[1]
    piece = parts[0].shape[1]
    for s in range(t):
        at = pl.ds(pl.multiple_of((core + t - s) % t * piece, piece), piece)
        out_ref[at] = parts[s][0].astype(F32)


def unpack_kernel(t, where_ref, *refs):
    parts, outs = refs[:t], refs[t:]
    core = where_ref[1]
    heads_here, _, sub, _ = parts[0].shape
    for s in range(t):
        at = pl.ds(pl.multiple_of((core + t - s) % t * sub, sub), sub)
        for a in range(4):
            for h in range(heads_here):
                outs[a][at, pl.ds(h * HEAD, HEAD)] = parts[s][h, a]


def forward_kernel(t, tile, count, full_ref, kcnt_ref, kidx_ref, q_ref, *refs):
    parts, (out_ref, lse_ref, k_few, v_few, k_ref, v_ref) = refs[:2 * t], refs[2 * t:]
    row = pl.program_id(0)
    q = q_ref[...]

    @pl.when(row == 0)
    def _():
        join_parts(parts, k_ref, v_ref)

    def finish(s, v):
        top = jnp.max(s, axis=1, keepdims=True)
        p = jnp.exp2(s - top)
        mass = jnp.sum(p, axis=1, keepdims=True)
        out = dot(p.astype(BF16), v)
        out_ref[...] = (out / mass).astype(BF16)
        lse_ref[...] = jnp.broadcast_to(top + jnp.log2(mass), lse_ref.shape)

    scale = HEAD ** -0.5 * LOG2E

    @pl.when(full_ref[row] == 1)
    def _():
        keys = k_ref[...].reshape(-1, HEAD)
        finish(dot(q, keys, NT) * scale, v_ref[...].reshape(-1, HEAD))

    @pl.when(full_ref[row] == 0)
    def _():
        gather_tiles(k_ref, kidx_ref, row, k_few, tile, count)
        gather_tiles(v_ref, kidx_ref, row, v_few, tile, count)
        s = dot(q, k_few[...], NT) * scale
        column = lax.broadcasted_iota(jnp.int32, s.shape, 1)
        s = jnp.where(column < kcnt_ref[row] * tile, s, NEG_BIG)
        finish(s, v_few[...])


def backward_kernel(t, tile, count, full_ref, kcnt_ref, kidx_ref, q_ref, g_ref, o_ref, lse_ref, *refs):
    parts, dkv_refs = refs[:2 * t], refs[2 * t + 1:3 * t + 1]
    dq_ref = refs[2 * t]
    k_few, v_few, k_ref, v_ref, dk_acc, dv_acc = refs[3 * t + 1:]
    row = pl.program_id(0)
    last = pl.num_programs(0) - 1

    @pl.when(row == 0)
    def _():
        join_parts(parts, k_ref, v_ref)
        dk_acc[...] = jnp.zeros_like(dk_acc)
        dv_acc[...] = jnp.zeros_like(dv_acc)

    q = q_ref[...]
    g = g_ref[...]
    delta = jnp.sum(g.astype(F32) * o_ref[...].astype(F32), axis=1, keepdims=True)
    lse = lse_ref[:, :1]
    unit = HEAD ** -0.5
    scale = unit * LOG2E

    def gradients(keys, values, mask):
        s = dot(q, keys, NT)
        p = jnp.exp2(s * scale - lse)
        if mask is not None:
            p = jnp.where(mask(p.shape), p, 0.0)
        ds = (p * (dot(g, values, NT) - delta)).astype(BF16)
        dq_ref[...] = (dot(ds, keys) * unit).astype(BF16)
        return dot(ds, q, TN) * unit, dot(p.astype(BF16), g, TN)

    @pl.when(full_ref[row] == 1)
    def _():
        dk, dv = gradients(k_ref[...].reshape(-1, HEAD), v_ref[...].reshape(-1, HEAD), None)
        dk_acc[...] += dk.reshape(dk_acc.shape)
        dv_acc[...] += dv.reshape(dv_acc.shape)

    @pl.when(full_ref[row] == 0)
    def _():
        gather_tiles(k_ref, kidx_ref, row, k_few, tile, count)
        gather_tiles(v_ref, kidx_ref, row, v_few, tile, count)

        def mask(shape):
            return lax.broadcasted_iota(jnp.int32, shape, 1) < kcnt_ref[row] * tile

        dk, dv = gradients(k_few[...], v_few[...], mask)
        for j in range(count):
            at = kidx_ref[row, j]
            dk_acc[at] += dk[j * tile:(j + 1) * tile]
            dv_acc[at] += dv[j * tile:(j + 1) * tile]

    @pl.when(row == last)
    def _():
        tiles = dk_acc.shape[0] // t
        for s, dkv_ref in enumerate(dkv_refs):
            at = pl.ds(s * tiles, tiles)
            dkv_ref[0] = dk_acc[at].reshape(dkv_ref.shape[1:]).astype(BF16)
            dkv_ref[1] = dv_acc[at].reshape(dkv_ref.shape[1:]).astype(BF16)


def whole_block(shape):
    return pl.BlockSpec(shape, lambda *_: (0,) * len(shape))


def one_array(which, length):
    return pl.BlockSpec((1, length, HEAD), lambda *_: (which, 0, 0))


def simple_call(kernel, name, scalars, inputs, outputs, scratch=()):
    size = sum(2 * math.prod(x.shape) for x in list(inputs) + list(outputs))
    return pl.pallas_call(
        kernel,
        grid_spec=pltpu.PrefetchScalarGridSpec(
            num_scalar_prefetch=1,
            grid=(1,),
            in_specs=[whole_block(x.shape) for x in inputs],
            out_specs=[whole_block(x.shape) for x in outputs],
            scratch_shapes=scratch,
        ),
        out_shape=outputs,
        compiler_params=pltpu.CompilerParams(vmem_limit_bytes=48 * 2**20),
        cost_estimate=pl.CostEstimate(flops=0, bytes_accessed=2 * size, transcendentals=0),
        name=name,
    )(scalars, *inputs)


def shifts(t, s):
    return [(c, (c + s) % t) for c in range(t)]


def place_xor_kernel(place_ref, *refs):
    sources, out_ref = refs[:-1], refs[-1]
    step = pl.program_id(0)
    for u in range(2):
        own, beside, above, upper, lower = sources[5 * u:5 * u + 5]
        for v, source in enumerate((own, beside, above)):
            @pl.when(step == 4 * u + v)
            def _(source=source):
                out_ref[...] = source[...].astype(F32)

        @pl.when(step == 4 * u + 3)
        def _(upper=upper, lower=lower):
            middle = upper.shape[0]
            out_ref[:middle] = upper[...].astype(F32)
            out_ref[middle:] = lower[...].astype(F32)


def gather_tiles_by_core(n, t, tile_sum, chip, core, sent):
    in_plane = n // PLANES
    plane, seat = chip // in_plane, chip % in_plane
    tile_rows, cols = tile_sum.shape
    across = [
        (i * t + c, (i ^ 2 * in_plane) * t + c)
        for i in range(n) for c in range(t) if i // in_plane // 2 == c
    ]
    from_half = lax.ppermute(tile_sum, ("ctx", "tp"), across)

    def swap(x, k):
        return lax.ppermute(x, "ctx", [(i, i ^ k) for i in range(n)])

    first = jnp.where(plane // 2 == core, tile_sum, from_half)
    _, sent = lax.optimization_barrier((first, sent))
    second = swap(first, in_plane)
    beside, above = swap(first, 1), swap(first, 2)
    middle = tile_rows // 2
    sources = [first, beside, above, swap(beside[:middle], 2), swap(above[middle:], 1)]
    beside, above = swap(second, 1), swap(second, 2)
    sources += [second, beside, above, swap(beside[:middle], 2), swap(above[middle:], 1)]
    chunks = lax.all_to_all(sent, "ctx", 0, 0, tiled=True)
    *_, chunks = lax.optimization_barrier((*sources, chunks))
    place = jnp.stack([plane % 2, seat]).astype(jnp.int32)
    return pl.pallas_call(
        place_xor_kernel,
        grid_spec=pltpu.PrefetchScalarGridSpec(
            num_scalar_prefetch=1,
            grid=(8,),
            in_specs=[whole_block(x.shape) for x in sources],
            out_specs=pl.BlockSpec(
                (tile_rows, cols), lambda s, place: (s // 4 ^ place[0], s % 4 ^ place[1])
            ),
        ),
        out_shape=jax.ShapeDtypeStruct((2 * tile_rows, in_plane * cols), F32),
        compiler_params=pltpu.CompilerParams(vmem_limit_bytes=48 * 2**20),
        cost_estimate=pl.CostEstimate(flops=0, bytes_accessed=2**24, transcendentals=0),
        name="place",
    )(place, *sources), chunks


def per_device(n, t, queries, key_vectors, value_vectors, out_weight, out_grad, block_segment):
    rows, width = queries.shape
    heads_here = width // HEAD
    heads = heads_here * t
    sub = rows // t
    tile = min(sub, BLK)
    per_chunk = sub // tile
    core = lax.axis_index("tp")
    chip = lax.axis_index("ctx")
    in_plane = n // PLANES
    heads_plane = heads // PLANES
    seat = chip % in_plane

    def tp_swap(pick):
        got = [pick(core)]
        for s in range(1, t):
            got.append(lax.ppermute(pick((core + s) % t), "tp", shifts(t, s)))
        return [lax.select_n((core - p) % t, *got) for p in range(t)]

    def tp_gather(x):
        return tp_swap(lambda _: x)

    def shape(*dims):
        return jax.ShapeDtypeStruct(dims, BF16)

    where = jnp.stack([chip, core]).astype(jnp.int32)
    held = [(i % in_plane - i // in_plane) % in_plane < heads_plane for i in range(n)]

    chunk_row = jnp.arange(n)[:, None] * rows + jnp.arange(per_chunk)[None, :] * tile

    def tile_segments(part):
        return jnp.take(block_segment, ((chunk_row + part * sub) // BLK).reshape(-1))

    seg_parts = [tile_segments((core - s) % t) for s in range(t)]
    seg_q = seg_parts[0]
    seg_k = jnp.concatenate(seg_parts)
    full = (seg_q == 0) | (seg_q == TARGET)
    permitted = (seg_k[None] == 0) | (seg_k[None] == seg_q[:, None])
    total_blocks = block_segment.shape[0]
    count = (TXT_BLK + -(-(total_blocks - TXT_BLK) // RUNS)) * (BLK // tile)
    kcnt = jnp.sum(permitted.astype(jnp.int32), axis=1)
    tiles_k = seg_k.shape[0]
    ids = jnp.arange(tiles_k)
    place = jnp.sum((permitted[:, None, :] & (ids[None, None, :] < ids[None, :, None])).astype(jnp.int32), axis=2)
    hit = permitted[:, None, :] & (place[:, None, :] == jnp.arange(count)[None, :, None])
    kidx = jnp.sum(jnp.where(hit, ids[None, None, :], 0), axis=2).astype(jnp.int32)
    full = full.astype(jnp.int32)

    def other_rows(*arrays):
        return [
            lax.ppermute(
                jnp.stack([
                    lax.dynamic_slice_in_dim(x, (core + s) % t * sub, sub, 0) for x in arrays
                ]),
                "tp", shifts(t, s),
            )
            for s in range(1, t)
        ]

    got_qkv = other_rows(queries, key_vectors, value_vectors)

    half = out_grad.shape[1]
    model = half * t
    full_grad = jnp.concatenate(tp_gather(out_grad), axis=1)
    grad_attn = dot(full_grad, out_weight, NT).astype(BF16)
    got_g = other_rows(grad_attn)

    cols = model // in_plane
    mine = lax.dynamic_slice_in_dim(full_grad, core * sub, sub, 0)
    plane_got = [lax.dynamic_slice_in_dim(mine, seat * cols, cols, 1)]
    for k in range(1, in_plane):
        there = lax.dynamic_slice_in_dim(mine, (seat ^ k) * cols, cols, 1)
        plane_got.append(lax.ppermute(there, "ctx", [(i, i ^ k) for i in range(n)]))
    (plane_grad,) = simple_call(
        functools.partial(seats_kernel, in_plane), "seats", where, plane_got, [shape(in_plane, sub, cols)]
    )
    def pack(arrays, got):
        (sent,) = simple_call(
            functools.partial(pack_kernel, n, t, len(arrays)), "pack", where,
            arrays + got, [shape(n, len(arrays), sub, HEAD)],
            [pltpu.VMEM((heads, len(arrays), sub, HEAD), BF16)],
        )
        return sent

    sent_qkv = pack([queries, key_vectors, value_vectors], got_qkv)
    sent_g = pack([grad_attn], got_g)
    chunks = lax.all_to_all(sent_qkv, "ctx", 0, 0, tiled=True)
    chunks, sent_g, plane_grad = lax.optimization_barrier((chunks, sent_g, plane_grad))
    lines = [[a * in_plane + b for a in range(PLANES)] for b in range(in_plane)]
    slice_grad = lax.all_gather(plane_grad, "ctx", axis_index_groups=lines)
    slice_grad = slice_grad.reshape(n * sub, cols)
    g_rows = lax.all_to_all(sent_g, "ctx", 0, 0, tiled=True).reshape(n * sub, HEAD)
    length = n * sub
    q_rows, kv = simple_call(
        functools.partial(join_kernel, n), "join", where, [chunks], [shape(length, HEAD), shape(2, length, HEAD)]
    )
    kv_all = [kv] + [lax.ppermute(kv, "tp", shifts(t, s)) for s in range(1, t)]

    tiles_q = n * per_chunk
    few = [pltpu.VMEM((count * tile, HEAD), BF16)] * 2 + [pltpu.VMEM((tiles_k, tile, HEAD), BF16)] * 2
    params = pltpu.CompilerParams(vmem_limit_bytes=48 * 2**20)
    part_blocks = [one_array(0, length), one_array(1, length)] * t
    part_arrays = [a for pack in kv_all for a in (pack, pack)]
    row_block = pl.BlockSpec((tile, HEAD), lambda r, *_: (r, 0))
    attn, lse = pl.pallas_call(
        functools.partial(forward_kernel, t, tile, count),
        grid_spec=pltpu.PrefetchScalarGridSpec(
            num_scalar_prefetch=3,
            grid=(tiles_q,),
            in_specs=[row_block] + part_blocks,
            out_specs=[row_block, row_block],
            scratch_shapes=few,
        ),
        out_shape=[shape(length, HEAD), jax.ShapeDtypeStruct((length, HEAD), F32)],
        compiler_params=params,
        cost_estimate=pl.CostEstimate(flops=16 * 10**9, bytes_accessed=5 * 2**20, transcendentals=2**22),
        name="forward",
    )(full, kcnt, kidx, q_rows, *part_arrays)

    travel = [attn] + [
        lax.ppermute(attn, "ctx", [(i, i ^ k) for i in range(n) if held[i]]) for k in range(1, in_plane)
    ]
    *travel, attn = lax.optimization_barrier((*travel, attn))

    dq, *dkv = pl.pallas_call(
        functools.partial(backward_kernel, t, tile, count),
        grid_spec=pltpu.PrefetchScalarGridSpec(
            num_scalar_prefetch=3,
            grid=(tiles_q,),
            in_specs=[row_block] * 4 + part_blocks,
            out_specs=[row_block] + [whole_block((2, length, HEAD))] * t,
            scratch_shapes=few + [pltpu.VMEM((tiles_k, tile, HEAD), F32)] * 2,
        ),
        out_shape=[shape(length, HEAD)] + [shape(2, length, HEAD)] * t,
        compiler_params=params,
        cost_estimate=pl.CostEstimate(flops=20 * 10**9, bytes_accessed=8 * 2**20, transcendentals=2**22),
        name="backward",
    )(full, kcnt, kidx, q_rows, g_rows, attn, lse, *part_arrays)

    got_dkv = [
        lax.ppermute(dkv[s], "tp", [(c, (c - s) % t) for c in range(t)]) for s in range(1, t)
    ]
    (sent,) = simple_call(
        functools.partial(unjoin_kernel, n, t), "unjoin", where,
        [attn, dq, dkv[0]] + got_dkv, [shape(n, 4, sub, HEAD)],
    )
    *travel, dq = lax.optimization_barrier((*travel, dq))

    tile_rows = heads_plane * HEAD
    by_core = in_plane == 4 and t == 2
    piece = tile_rows if by_core else tile_rows // t
    step_rows = length // 4
    tile_own, *tile_sends = pl.pallas_call(
        functools.partial(tile_kernel, in_plane, heads_plane, t),
        grid_spec=pltpu.PrefetchScalarGridSpec(
            num_scalar_prefetch=1,
            grid=(4,),
            in_specs=[pl.BlockSpec((step_rows, HEAD), lambda r, *_: (r, 0))] * in_plane
            + [pl.BlockSpec((step_rows, cols), lambda r, *_: (r, 0))],
            out_specs=[whole_block((piece, cols))] * t,
            scratch_shapes=[
                pltpu.VMEM((in_plane, step_rows, HEAD), BF16), pltpu.VMEM((tile_rows, cols), F32)
            ],
        ),
        out_shape=[jax.ShapeDtypeStruct((piece, cols), F32)] + [shape(piece, cols)] * (t - 1),
        compiler_params=params,
        cost_estimate=pl.CostEstimate(flops=5 * 10**9, bytes_accessed=2**22, transcendentals=0),
        name="tile",
    )(where, *travel, slice_grad)
    tile_sum = tile_own
    for s in range(1, t):
        tile_sum = tile_sum + lax.ppermute(tile_sends[s - 1], "tp", shifts(t, s)).astype(F32)
    if by_core:
        grad_weight, chunks = gather_tiles_by_core(n, t, tile_sum.astype(BF16), chip, core, sent)
    else:
        chunks = lax.all_to_all(sent, "ctx", 0, 0, tiled=True)
        tiles = lax.all_gather(tile_sum.astype(BF16), "ctx")
        here = n // t
        tiles_core = [tiles] + [
            lax.ppermute(
                lax.dynamic_slice_in_dim(tiles, (core + s) % t * here, here, 0), "tp", shifts(t, s)
            )
            for s in range(1, t)
        ]
        grad_weight = pl.pallas_call(
            functools.partial(place_kernel, t),
            grid_spec=pltpu.PrefetchScalarGridSpec(
                num_scalar_prefetch=1,
                grid=(here,),
                in_specs=[pl.BlockSpec((1, piece, cols), lambda r, where: (where[1] * here + r, 0, 0))]
                + [pl.BlockSpec((1, piece, cols), lambda r, *_: (r, 0, 0))] * (t - 1),
                out_specs=pl.BlockSpec((tile_rows, cols), lambda r, *_: (r // in_plane, r % in_plane)),
            ),
            out_shape=jax.ShapeDtypeStruct((width, model), F32),
            compiler_params=params,
            cost_estimate=pl.CostEstimate(flops=0, bytes_accessed=2**24, transcendentals=0),
            name="place",
        )(where, *tiles_core)

    mine = simple_call(
        functools.partial(by_core_kernel, n, t), "by_core", where, [chunks],
        [shape(heads_here, 4, sub, HEAD)] * t, [pltpu.VMEM((heads, 4, sub, HEAD), BF16)],
    )
    parts = [mine[0]] + [lax.ppermute(mine[s], "tp", shifts(t, s)) for s in range(1, t)]
    attention, grad_queries, grad_keys, grad_values = simple_call(
        functools.partial(unpack_kernel, t), "unpack", where, parts, [shape(rows, width)] * 4
    )
    projected = dot(attention, out_weight)
    own = lax.dynamic_slice_in_dim(projected, core * half, half, 1)
    for s in range(1, t):
        there = lax.dynamic_slice_in_dim(projected, (core + s) % t * half, half, 1)
        own = own + lax.ppermute(there.astype(BF16), "tp", shifts(t, s)).astype(F32)
    attention_out = own.astype(BF16)

    return attention_out, grad_queries, grad_keys, grad_values, grad_weight


def solution(mesh):
    n, t = mesh.shape["ctx"], mesh.shape["tp"]
    in_specs = (P("ctx", "tp"), P("ctx", "tp"), P("ctx", "tp"), P("tp", None), P("ctx", "tp"), P())
    out_specs = (P("ctx", "tp"), P("ctx", "tp"), P("ctx", "tp"), P("ctx", "tp"), P("tp", None))
    return jax.shard_map(
        functools.partial(per_device, n, t), mesh=mesh, in_specs=in_specs, out_specs=out_specs, check_vma=False
    )
```

```python
import functools
import math

import jax
import jax.numpy as jnp
from jax import lax
from jax.experimental import pallas as pl
from jax.experimental.pallas import tpu as pltpu
from jax.sharding import PartitionSpec as P

HEAD = 128
BLK = 128
TXT_BLK = 4
RUNS = 5
TARGET = 5
PLANES = 4
LOG2E = math.log2(math.e)
NEG_BIG = -1e30

NT = (((1,), (1,)), ((), ()))
TN = (((0,), (0,)), ((), ()))
F32 = jnp.float32
BF16 = jnp.bfloat16


def dot(a, b, dims=(((1,), (0,)), ((), ()))):
    return lax.dot_general(a, b, dims, preferred_element_type=F32)


def gather_tiles(k_ref, kidx_ref, row, dst, tile, count):
    for j in range(count):
        dst[pl.ds(j * tile, tile), :] = k_ref[kidx_ref[row, j]]


def join_parts(parts, k_all, v_all):
    shape = (k_all.shape[0] // (len(parts) // 2),) + k_all.shape[1:]
    for s in range(len(parts) // 2):
        at = pl.ds(s * shape[0], shape[0])
        k_all[at] = parts[2 * s][...].reshape(shape)
        v_all[at] = parts[2 * s + 1][...].reshape(shape)


def head_of(chip, in_plane, heads_plane):
    place = (chip % in_plane - chip // in_plane) % in_plane
    return place < heads_plane, chip // in_plane * heads_plane + min(place, heads_plane - 1)


def pack_kernel(n, t, count, where_ref, *refs):
    arrays, got, (out_ref, heads_all) = refs[:count], refs[count:count + t - 1], refs[count + t - 1:]
    core = where_ref[1]
    sub = heads_all.shape[2]
    heads_here = heads_all.shape[0] // t
    for a in range(count):
        for h in range(heads_here):
            column = pl.ds(h * HEAD, HEAD)
            heads_all[core * heads_here + h, a] = arrays[a][pl.ds(core * sub, sub), column]
            for s in range(1, t):
                first = (core + t - s) % t * heads_here
                heads_all[first + h, a] = got[s - 1][a, :, column]
    for k in range(n):
        held, head = head_of(k, n // PLANES, heads_all.shape[0] // PLANES)
        out_ref[k] = heads_all[head] if held else jnp.zeros_like(heads_all[0])


def join_kernel(n, where_ref, chunks_ref, q_ref, kv_ref):
    sub = chunks_ref.shape[2]
    for k in range(n):
        at = pl.ds(k * sub, sub)
        q_ref[at] = chunks_ref[k, 0]
        kv_ref[0, at] = chunks_ref[k, 1]
        kv_ref[1, at] = chunks_ref[k, 2]


def unjoin_kernel(n, t, where_ref, attn_ref, dq_ref, dkv_ref, *refs):
    got, out_ref = refs[:t - 1], refs[t - 1]
    sub = out_ref.shape[2]
    for k in range(n):
        at = pl.ds(k * sub, sub)
        out_ref[k, 0] = attn_ref[at]
        out_ref[k, 1] = dq_ref[at]
        for a in range(2):
            total = dkv_ref[a, at].astype(F32)
            for other in got:
                total = total + other[a, at].astype(F32)
            out_ref[k, 2 + a] = total.astype(BF16)


def by_core_kernel(n, t, where_ref, chunks_ref, *refs):
    outs, heads_all = refs[:t], refs[t]
    core = where_ref[1]
    heads_here = heads_all.shape[0] // t
    for k in range(n):
        held, head = head_of(k, n // PLANES, heads_all.shape[0] // PLANES)
        if held:
            heads_all[head] = chunks_ref[k]
    for s in range(t):
        outs[s][...] = heads_all[pl.ds((core + s) % t * heads_here, heads_here)]


def seats_kernel(in_plane, where_ref, *refs):
    got, out_ref = refs[:in_plane], refs[in_plane]
    seat = where_ref[0] % in_plane
    for k in range(in_plane):
        out_ref[seat ^ k] = got[k][...]


def tile_kernel(in_plane, heads_plane, t, where_ref, *refs):
    attns, (grad_ref, own_ref), sends = refs[:in_plane], refs[in_plane:in_plane + 2], refs[in_plane + 2:-2]
    seats, total = refs[-2:]
    chip, core = where_ref[0], where_ref[1]
    seat = chip % in_plane
    plane = chip // in_plane
    step = pl.program_id(0)
    for k in range(in_plane):
        seats[seat ^ k] = attns[k][...]

    @pl.when(step == 0)
    def _():
        total[...] = jnp.zeros_like(total)

    grad = grad_ref[...]
    for j in range(heads_plane):
        total[pl.ds(j * HEAD, HEAD)] += dot(seats[(plane + j) % in_plane], grad, TN)

    @pl.when(step == pl.num_programs(0) - 1)
    def _():
        piece = own_ref.shape[0]
        if piece == total.shape[0]:
            own_ref[...] = total[...]
            sends[0][...] = total[...].astype(BF16)
            return
        own_ref[...] = total[pl.ds(pl.multiple_of(core * piece, piece), piece)]
        for s in range(1, t):
            at = pl.ds(pl.multiple_of((core + s) % t * piece, piece), piece)
            sends[s - 1][...] = total[at].astype(BF16)


def place_kernel(t, where_ref, *refs):
    parts, out_ref = refs[:t], refs[t]
    core = where_ref[1]
    piece = parts[0].shape[1]
    for s in range(t):
        at = pl.ds(pl.multiple_of((core + t - s) % t * piece, piece), piece)
        out_ref[at] = parts[s][0].astype(F32)


def unpack_kernel(t, where_ref, *refs):
    parts, outs = refs[:t], refs[t:]
    core = where_ref[1]
    heads_here, _, sub, _ = parts[0].shape
    for s in range(t):
        at = pl.ds(pl.multiple_of((core + t - s) % t * sub, sub), sub)
        for a in range(4):
            for h in range(heads_here):
                outs[a][at, pl.ds(h * HEAD, HEAD)] = parts[s][h, a]


def forward_kernel(t, tile, count, full_ref, kcnt_ref, kidx_ref, q_ref, *refs):
    parts, (out_ref, lse_ref, k_few, v_few, k_ref, v_ref) = refs[:2 * t], refs[2 * t:]
    row = pl.program_id(0)
    q = q_ref[...]

    @pl.when(row == 0)
    def _():
        join_parts(parts, k_ref, v_ref)

    def finish(s, v):
        top = jnp.max(s, axis=1, keepdims=True)
        p = jnp.exp2(s - top)
        mass = jnp.sum(p, axis=1, keepdims=True)
        out = dot(p.astype(BF16), v)
        out_ref[...] = (out / mass).astype(BF16)
        lse_ref[...] = jnp.broadcast_to(top + jnp.log2(mass), lse_ref.shape)

    scale = HEAD ** -0.5 * LOG2E

    @pl.when(full_ref[row] == 1)
    def _():
        keys = k_ref[...].reshape(-1, HEAD)
        finish(dot(q, keys, NT) * scale, v_ref[...].reshape(-1, HEAD))

    @pl.when(full_ref[row] == 0)
    def _():
        gather_tiles(k_ref, kidx_ref, row, k_few, tile, count)
        gather_tiles(v_ref, kidx_ref, row, v_few, tile, count)
        s = dot(q, k_few[...], NT) * scale
        column = lax.broadcasted_iota(jnp.int32, s.shape, 1)
        s = jnp.where(column < kcnt_ref[row] * tile, s, NEG_BIG)
        finish(s, v_few[...])


def backward_kernel(t, tile, count, full_ref, kcnt_ref, kidx_ref, q_ref, g_ref, o_ref, lse_ref, *refs):
    parts, dkv_refs = refs[:2 * t], refs[2 * t + 1:3 * t + 1]
    dq_ref = refs[2 * t]
    k_few, v_few, k_ref, v_ref, dk_acc, dv_acc = refs[3 * t + 1:]
    row = pl.program_id(0)
    last = pl.num_programs(0) - 1

    @pl.when(row == 0)
    def _():
        join_parts(parts, k_ref, v_ref)
        dk_acc[...] = jnp.zeros_like(dk_acc)
        dv_acc[...] = jnp.zeros_like(dv_acc)

    q = q_ref[...]
    g = g_ref[...]
    delta = jnp.sum(g.astype(F32) * o_ref[...].astype(F32), axis=1, keepdims=True)
    lse = lse_ref[:, :1]
    unit = HEAD ** -0.5
    scale = unit * LOG2E

    def gradients(keys, values, mask):
        s = dot(q, keys, NT)
        p = jnp.exp2(s * scale - lse)
        if mask is not None:
            p = jnp.where(mask(p.shape), p, 0.0)
        ds = (p * (dot(g, values, NT) - delta)).astype(BF16)
        dq_ref[...] = (dot(ds, keys) * unit).astype(BF16)
        return dot(ds, q, TN) * unit, dot(p.astype(BF16), g, TN)

    @pl.when(full_ref[row] == 1)
    def _():
        dk, dv = gradients(k_ref[...].reshape(-1, HEAD), v_ref[...].reshape(-1, HEAD), None)
        dk_acc[...] += dk.reshape(dk_acc.shape)
        dv_acc[...] += dv.reshape(dv_acc.shape)

    @pl.when(full_ref[row] == 0)
    def _():
        gather_tiles(k_ref, kidx_ref, row, k_few, tile, count)
        gather_tiles(v_ref, kidx_ref, row, v_few, tile, count)

        def mask(shape):
            return lax.broadcasted_iota(jnp.int32, shape, 1) < kcnt_ref[row] * tile

        dk, dv = gradients(k_few[...], v_few[...], mask)
        for j in range(count):
            at = kidx_ref[row, j]
            dk_acc[at] += dk[j * tile:(j + 1) * tile]
            dv_acc[at] += dv[j * tile:(j + 1) * tile]

    @pl.when(row == last)
    def _():
        tiles = dk_acc.shape[0] // t
        for s, dkv_ref in enumerate(dkv_refs):
            at = pl.ds(s * tiles, tiles)
            dkv_ref[0] = dk_acc[at].reshape(dkv_ref.shape[1:]).astype(BF16)
            dkv_ref[1] = dv_acc[at].reshape(dkv_ref.shape[1:]).astype(BF16)


def whole_block(shape):
    return pl.BlockSpec(shape, lambda *_: (0,) * len(shape))


def one_array(which, length):
    return pl.BlockSpec((1, length, HEAD), lambda *_: (which, 0, 0))


def simple_call(kernel, name, scalars, inputs, outputs, scratch=()):
    size = sum(2 * math.prod(x.shape) for x in list(inputs) + list(outputs))
    return pl.pallas_call(
        kernel,
        grid_spec=pltpu.PrefetchScalarGridSpec(
            num_scalar_prefetch=1,
            grid=(1,),
            in_specs=[whole_block(x.shape) for x in inputs],
            out_specs=[whole_block(x.shape) for x in outputs],
            scratch_shapes=scratch,
        ),
        out_shape=outputs,
        compiler_params=pltpu.CompilerParams(vmem_limit_bytes=48 * 2**20),
        cost_estimate=pl.CostEstimate(flops=0, bytes_accessed=2 * size, transcendentals=0),
        name=name,
    )(scalars, *inputs)


def shifts(t, s):
    return [(c, (c + s) % t) for c in range(t)]


def place_xor_kernel(place_ref, *refs):
    sources, out_ref = refs[:-1], refs[-1]
    step = pl.program_id(0)
    for u in range(2):
        own, beside, above, upper, lower = sources[5 * u:5 * u + 5]
        for v, source in enumerate((own, beside, above)):
            @pl.when(step == 4 * u + v)
            def _(source=source):
                out_ref[...] = source[...].astype(F32)

        @pl.when(step == 4 * u + 3)
        def _(upper=upper, lower=lower):
            middle = upper.shape[0]
            out_ref[:middle] = upper[...].astype(F32)
            out_ref[middle:] = lower[...].astype(F32)


def gather_tiles_by_core(n, t, tile_sum, chip, core, sent):
    in_plane = n // PLANES
    plane, seat = chip // in_plane, chip % in_plane
    tile_rows, cols = tile_sum.shape
    across = [
        (i * t + c, (i ^ 2 * in_plane) * t + c)
        for i in range(n) for c in range(t) if i // in_plane // 2 == c
    ]
    from_half = lax.ppermute(tile_sum, ("ctx", "tp"), across)

    def swap(x, k):
        return lax.ppermute(x, "ctx", [(i, i ^ k) for i in range(n)])

    first = jnp.where(plane // 2 == core, tile_sum, from_half)
    second = swap(first, in_plane)
    _, sent = lax.optimization_barrier((second, sent))
    beside, above = swap(first, 1), swap(first, 2)
    middle = tile_rows // 2
    sources = [first, beside, above, swap(beside[:middle], 2), swap(above[middle:], 1)]
    beside, above = swap(second, 1), swap(second, 2)
    sources += [second, beside, above, swap(beside[:middle], 2), swap(above[middle:], 1)]
    chunks = lax.all_to_all(sent, "ctx", 0, 0, tiled=True)
    *_, chunks = lax.optimization_barrier((*sources, chunks))
    place = jnp.stack([plane % 2, seat]).astype(jnp.int32)
    return pl.pallas_call(
        place_xor_kernel,
        grid_spec=pltpu.PrefetchScalarGridSpec(
            num_scalar_prefetch=1,
            grid=(8,),
            in_specs=[whole_block(x.shape) for x in sources],
            out_specs=pl.BlockSpec(
                (tile_rows, cols), lambda s, place: (s // 4 ^ place[0], s % 4 ^ place[1])
            ),
        ),
        out_shape=jax.ShapeDtypeStruct((2 * tile_rows, in_plane * cols), F32),
        compiler_params=pltpu.CompilerParams(vmem_limit_bytes=48 * 2**20),
        cost_estimate=pl.CostEstimate(flops=0, bytes_accessed=2**24, transcendentals=0),
        name="place",
    )(place, *sources), chunks


def per_device(n, t, queries, key_vectors, value_vectors, out_weight, out_grad, block_segment):
    rows, width = queries.shape
    heads_here = width // HEAD
    heads = heads_here * t
    sub = rows // t
    tile = min(sub, BLK)
    per_chunk = sub // tile
    core = lax.axis_index("tp")
    chip = lax.axis_index("ctx")
    in_plane = n // PLANES
    heads_plane = heads // PLANES
    seat = chip % in_plane

    def tp_swap(pick):
        got = [pick(core)]
        for s in range(1, t):
            got.append(lax.ppermute(pick((core + s) % t), "tp", shifts(t, s)))
        return [lax.select_n((core - p) % t, *got) for p in range(t)]

    def tp_gather(x):
        return tp_swap(lambda _: x)

    def shape(*dims):
        return jax.ShapeDtypeStruct(dims, BF16)

    where = jnp.stack([chip, core]).astype(jnp.int32)
    held = [(i % in_plane - i // in_plane) % in_plane < heads_plane for i in range(n)]

    chunk_row = jnp.arange(n)[:, None] * rows + jnp.arange(per_chunk)[None, :] * tile

    def tile_segments(part):
        return jnp.take(block_segment, ((chunk_row + part * sub) // BLK).reshape(-1))

    seg_parts = [tile_segments((core - s) % t) for s in range(t)]
    seg_q = seg_parts[0]
    seg_k = jnp.concatenate(seg_parts)
    full = (seg_q == 0) | (seg_q == TARGET)
    permitted = (seg_k[None] == 0) | (seg_k[None] == seg_q[:, None])
    total_blocks = block_segment.shape[0]
    count = (TXT_BLK + -(-(total_blocks - TXT_BLK) // RUNS)) * (BLK // tile)
    kcnt = jnp.sum(permitted.astype(jnp.int32), axis=1)
    tiles_k = seg_k.shape[0]
    ids = jnp.arange(tiles_k)
    place = jnp.sum((permitted[:, None, :] & (ids[None, None, :] < ids[None, :, None])).astype(jnp.int32), axis=2)
    hit = permitted[:, None, :] & (place[:, None, :] == jnp.arange(count)[None, :, None])
    kidx = jnp.sum(jnp.where(hit, ids[None, None, :], 0), axis=2).astype(jnp.int32)
    full = full.astype(jnp.int32)

    def other_rows(*arrays):
        return [
            lax.ppermute(
                jnp.stack([
                    lax.dynamic_slice_in_dim(x, (core + s) % t * sub, sub, 0) for x in arrays
                ]),
                "tp", shifts(t, s),
            )
            for s in range(1, t)
        ]

    got_qkv = other_rows(queries, key_vectors, value_vectors)

    half = out_grad.shape[1]
    model = half * t
    full_grad = jnp.concatenate(tp_gather(out_grad), axis=1)
    grad_attn = dot(full_grad, out_weight, NT).astype(BF16)
    got_g = other_rows(grad_attn)

    cols = model // in_plane
    mine = lax.dynamic_slice_in_dim(full_grad, core * sub, sub, 0)
    plane_got = [lax.dynamic_slice_in_dim(mine, seat * cols, cols, 1)]
    for k in range(1, in_plane):
        there = lax.dynamic_slice_in_dim(mine, (seat ^ k) * cols, cols, 1)
        plane_got.append(lax.ppermute(there, "ctx", [(i, i ^ k) for i in range(n)]))
    (plane_grad,) = simple_call(
        functools.partial(seats_kernel, in_plane), "seats", where, plane_got, [shape(in_plane, sub, cols)]
    )
    def pack(arrays, got):
        (sent,) = simple_call(
            functools.partial(pack_kernel, n, t, len(arrays)), "pack", where,
            arrays + got, [shape(n, len(arrays), sub, HEAD)],
            [pltpu.VMEM((heads, len(arrays), sub, HEAD), BF16)],
        )
        return sent

    sent_qkv = pack([queries, key_vectors, value_vectors], got_qkv)
    sent_g = pack([grad_attn], got_g)
    chunks = lax.all_to_all(sent_qkv, "ctx", 0, 0, tiled=True)
    chunks, sent_g, plane_grad = lax.optimization_barrier((chunks, sent_g, plane_grad))
    lines = [[a * in_plane + b for a in range(PLANES)] for b in range(in_plane)]
    slice_grad = lax.all_gather(plane_grad, "ctx", axis_index_groups=lines)
    slice_grad = slice_grad.reshape(n * sub, cols)
    g_rows = lax.all_to_all(sent_g, "ctx", 0, 0, tiled=True).reshape(n * sub, HEAD)
    length = n * sub
    q_rows, kv = simple_call(
        functools.partial(join_kernel, n), "join", where, [chunks], [shape(length, HEAD), shape(2, length, HEAD)]
    )
    kv_all = [kv] + [lax.ppermute(kv, "tp", shifts(t, s)) for s in range(1, t)]

    tiles_q = n * per_chunk
    few = [pltpu.VMEM((count * tile, HEAD), BF16)] * 2 + [pltpu.VMEM((tiles_k, tile, HEAD), BF16)] * 2
    params = pltpu.CompilerParams(vmem_limit_bytes=48 * 2**20)
    part_blocks = [one_array(0, length), one_array(1, length)] * t
    part_arrays = [a for pack in kv_all for a in (pack, pack)]
    row_block = pl.BlockSpec((tile, HEAD), lambda r, *_: (r, 0))
    attn, lse = pl.pallas_call(
        functools.partial(forward_kernel, t, tile, count),
        grid_spec=pltpu.PrefetchScalarGridSpec(
            num_scalar_prefetch=3,
            grid=(tiles_q,),
            in_specs=[row_block] + part_blocks,
            out_specs=[row_block, row_block],
            scratch_shapes=few,
        ),
        out_shape=[shape(length, HEAD), jax.ShapeDtypeStruct((length, HEAD), F32)],
        compiler_params=params,
        cost_estimate=pl.CostEstimate(flops=16 * 10**9, bytes_accessed=5 * 2**20, transcendentals=2**22),
        name="forward",
    )(full, kcnt, kidx, q_rows, *part_arrays)

    travel = [attn] + [
        lax.ppermute(attn, "ctx", [(i, i ^ k) for i in range(n) if held[i]]) for k in range(1, in_plane)
    ]
    *travel, attn = lax.optimization_barrier((*travel, attn))

    dq, *dkv = pl.pallas_call(
        functools.partial(backward_kernel, t, tile, count),
        grid_spec=pltpu.PrefetchScalarGridSpec(
            num_scalar_prefetch=3,
            grid=(tiles_q,),
            in_specs=[row_block] * 4 + part_blocks,
            out_specs=[row_block] + [whole_block((2, length, HEAD))] * t,
            scratch_shapes=few + [pltpu.VMEM((tiles_k, tile, HEAD), F32)] * 2,
        ),
        out_shape=[shape(length, HEAD)] + [shape(2, length, HEAD)] * t,
        compiler_params=params,
        cost_estimate=pl.CostEstimate(flops=20 * 10**9, bytes_accessed=8 * 2**20, transcendentals=2**22),
        name="backward",
    )(full, kcnt, kidx, q_rows, g_rows, attn, lse, *part_arrays)

    got_dkv = [
        lax.ppermute(dkv[s], "tp", [(c, (c - s) % t) for c in range(t)]) for s in range(1, t)
    ]
    (sent,) = simple_call(
        functools.partial(unjoin_kernel, n, t), "unjoin", where,
        [attn, dq, dkv[0]] + got_dkv, [shape(n, 4, sub, HEAD)],
    )
    *travel, dq = lax.optimization_barrier((*travel, dq))

    tile_rows = heads_plane * HEAD
    by_core = in_plane == 4 and t == 2
    piece = tile_rows if by_core else tile_rows // t
    step_rows = length // 4
    tile_own, *tile_sends = pl.pallas_call(
        functools.partial(tile_kernel, in_plane, heads_plane, t),
        grid_spec=pltpu.PrefetchScalarGridSpec(
            num_scalar_prefetch=1,
            grid=(4,),
            in_specs=[pl.BlockSpec((step_rows, HEAD), lambda r, *_: (r, 0))] * in_plane
            + [pl.BlockSpec((step_rows, cols), lambda r, *_: (r, 0))],
            out_specs=[whole_block((piece, cols))] * t,
            scratch_shapes=[
                pltpu.VMEM((in_plane, step_rows, HEAD), BF16), pltpu.VMEM((tile_rows, cols), F32)
            ],
        ),
        out_shape=[jax.ShapeDtypeStruct((piece, cols), F32)] + [shape(piece, cols)] * (t - 1),
        compiler_params=params,
        cost_estimate=pl.CostEstimate(flops=5 * 10**9, bytes_accessed=2**22, transcendentals=0),
        name="tile",
    )(where, *travel, slice_grad)
    tile_sum = tile_own
    for s in range(1, t):
        tile_sum = tile_sum + lax.ppermute(tile_sends[s - 1], "tp", shifts(t, s)).astype(F32)
    if by_core:
        grad_weight, chunks = gather_tiles_by_core(n, t, tile_sum.astype(BF16), chip, core, sent)
    else:
        chunks = lax.all_to_all(sent, "ctx", 0, 0, tiled=True)
        tiles = lax.all_gather(tile_sum.astype(BF16), "ctx")
        here = n // t
        tiles_core = [tiles] + [
            lax.ppermute(
                lax.dynamic_slice_in_dim(tiles, (core + s) % t * here, here, 0), "tp", shifts(t, s)
            )
            for s in range(1, t)
        ]
        grad_weight = pl.pallas_call(
            functools.partial(place_kernel, t),
            grid_spec=pltpu.PrefetchScalarGridSpec(
                num_scalar_prefetch=1,
                grid=(here,),
                in_specs=[pl.BlockSpec((1, piece, cols), lambda r, where: (where[1] * here + r, 0, 0))]
                + [pl.BlockSpec((1, piece, cols), lambda r, *_: (r, 0, 0))] * (t - 1),
                out_specs=pl.BlockSpec((tile_rows, cols), lambda r, *_: (r // in_plane, r % in_plane)),
            ),
            out_shape=jax.ShapeDtypeStruct((width, model), F32),
            compiler_params=params,
            cost_estimate=pl.CostEstimate(flops=0, bytes_accessed=2**24, transcendentals=0),
            name="place",
        )(where, *tiles_core)

    mine = simple_call(
        functools.partial(by_core_kernel, n, t), "by_core", where, [chunks],
        [shape(heads_here, 4, sub, HEAD)] * t, [pltpu.VMEM((heads, 4, sub, HEAD), BF16)],
    )
    parts = [mine[0]] + [lax.ppermute(mine[s], "tp", shifts(t, s)) for s in range(1, t)]
    attention, grad_queries, grad_keys, grad_values = simple_call(
        functools.partial(unpack_kernel, t), "unpack", where, parts, [shape(rows, width)] * 4
    )
    projected = dot(attention, out_weight)
    own = lax.dynamic_slice_in_dim(projected, core * half, half, 1)
    for s in range(1, t):
        there = lax.dynamic_slice_in_dim(projected, (core + s) % t * half, half, 1)
        own = own + lax.ppermute(there.astype(BF16), "tp", shifts(t, s)).astype(F32)
    attention_out = own.astype(BF16)

    return attention_out, grad_queries, grad_keys, grad_values, grad_weight


def solution(mesh):
    n, t = mesh.shape["ctx"], mesh.shape["tp"]
    in_specs = (P("ctx", "tp"), P("ctx", "tp"), P("ctx", "tp"), P("tp", None), P("ctx", "tp"), P())
    out_specs = (P("ctx", "tp"), P("ctx", "tp"), P("ctx", "tp"), P("ctx", "tp"), P("tp", None))
    return jax.shard_map(
        functools.partial(per_device, n, t), mesh=mesh, in_specs=in_specs, out_specs=out_specs, check_vma=False
    )
```

```python
import functools
import math

import jax
import jax.numpy as jnp
from jax import lax
from jax.experimental import pallas as pl
from jax.experimental.pallas import tpu as pltpu
from jax.sharding import PartitionSpec as P

HEAD = 128
BLK = 128
TXT_BLK = 4
RUNS = 5
TARGET = 5
PLANES = 4
LOG2E = math.log2(math.e)
NEG_BIG = -1e30

NT = (((1,), (1,)), ((), ()))
TN = (((0,), (0,)), ((), ()))
F32 = jnp.float32
BF16 = jnp.bfloat16


def dot(a, b, dims=(((1,), (0,)), ((), ()))):
    return lax.dot_general(a, b, dims, preferred_element_type=F32)


def gather_tiles(k_ref, kidx_ref, row, dst, tile, count):
    for j in range(count):
        dst[pl.ds(j * tile, tile), :] = k_ref[kidx_ref[row, j]]


def join_parts(parts, k_all, v_all):
    shape = (k_all.shape[0] // (len(parts) // 2),) + k_all.shape[1:]
    for s in range(len(parts) // 2):
        at = pl.ds(s * shape[0], shape[0])
        k_all[at] = parts[2 * s][...].reshape(shape)
        v_all[at] = parts[2 * s + 1][...].reshape(shape)


def head_of(chip, in_plane, heads_plane):
    place = (chip % in_plane - chip // in_plane) % in_plane
    return place < heads_plane, chip // in_plane * heads_plane + min(place, heads_plane - 1)


def pack_kernel(n, t, count, where_ref, *refs):
    arrays, got, (out_ref, heads_all) = refs[:count], refs[count:count + t - 1], refs[count + t - 1:]
    core = where_ref[1]
    sub = heads_all.shape[2]
    heads_here = heads_all.shape[0] // t
    for a in range(count):
        for h in range(heads_here):
            column = pl.ds(h * HEAD, HEAD)
            heads_all[core * heads_here + h, a] = arrays[a][pl.ds(core * sub, sub), column]
            for s in range(1, t):
                first = (core + t - s) % t * heads_here
                heads_all[first + h, a] = got[s - 1][a, :, column]
    for k in range(n):
        held, head = head_of(k, n // PLANES, heads_all.shape[0] // PLANES)
        out_ref[k] = heads_all[head] if held else jnp.zeros_like(heads_all[0])


def join_kernel(n, where_ref, chunks_ref, q_ref, kv_ref):
    sub = chunks_ref.shape[2]
    for k in range(n):
        at = pl.ds(k * sub, sub)
        q_ref[at] = chunks_ref[k, 0]
        kv_ref[0, at] = chunks_ref[k, 1]
        kv_ref[1, at] = chunks_ref[k, 2]


def unjoin_kernel(n, t, where_ref, attn_ref, dq_ref, dkv_ref, *refs):
    got, out_ref = refs[:t - 1], refs[t - 1]
    sub = out_ref.shape[2]
    for k in range(n):
        at = pl.ds(k * sub, sub)
        out_ref[k, 0] = attn_ref[at]
        out_ref[k, 1] = dq_ref[at]
        for a in range(2):
            total = dkv_ref[a, at].astype(F32)
            for other in got:
                total = total + other[a, at].astype(F32)
            out_ref[k, 2 + a] = total.astype(BF16)


def by_core_kernel(n, t, where_ref, chunks_ref, *refs):
    outs, heads_all = refs[:t], refs[t]
    core = where_ref[1]
    heads_here = heads_all.shape[0] // t
    for k in range(n):
        held, head = head_of(k, n // PLANES, heads_all.shape[0] // PLANES)
        if held:
            heads_all[head] = chunks_ref[k]
    for s in range(t):
        outs[s][...] = heads_all[pl.ds((core + s) % t * heads_here, heads_here)]


def seats_kernel(in_plane, where_ref, *refs):
    got, out_ref = refs[:in_plane], refs[in_plane]
    seat = where_ref[0] % in_plane
    for k in range(in_plane):
        out_ref[seat ^ k] = got[k][...]


def tile_kernel(in_plane, heads_plane, t, where_ref, *refs):
    attns, (grad_ref, own_ref), sends = refs[:in_plane], refs[in_plane:in_plane + 2], refs[in_plane + 2:-2]
    seats, total = refs[-2:]
    chip, core = where_ref[0], where_ref[1]
    seat = chip % in_plane
    plane = chip // in_plane
    step = pl.program_id(0)
    for k in range(in_plane):
        seats[seat ^ k] = attns[k][...]

    @pl.when(step == 0)
    def _():
        total[...] = jnp.zeros_like(total)

    grad = grad_ref[...]
    for j in range(heads_plane):
        total[pl.ds(j * HEAD, HEAD)] += dot(seats[(plane + j) % in_plane], grad, TN)

    @pl.when(step == pl.num_programs(0) - 1)
    def _():
        piece = own_ref.shape[0]
        if piece == total.shape[0]:
            own_ref[...] = total[...]
            sends[0][...] = total[...].astype(BF16)
            return
        own_ref[...] = total[pl.ds(pl.multiple_of(core * piece, piece), piece)]
        for s in range(1, t):
            at = pl.ds(pl.multiple_of((core + s) % t * piece, piece), piece)
            sends[s - 1][...] = total[at].astype(BF16)


def place_kernel(t, where_ref, *refs):
    parts, out_ref = refs[:t], refs[t]
    core = where_ref[1]
    piece = parts[0].shape[1]
    for s in range(t):
        at = pl.ds(pl.multiple_of((core + t - s) % t * piece, piece), piece)
        out_ref[at] = parts[s][0].astype(F32)


def unpack_kernel(t, where_ref, *refs):
    parts, outs = refs[:t], refs[t:]
    core = where_ref[1]
    heads_here, _, sub, _ = parts[0].shape
    for s in range(t):
        at = pl.ds(pl.multiple_of((core + t - s) % t * sub, sub), sub)
        for a in range(4):
            for h in range(heads_here):
                outs[a][at, pl.ds(h * HEAD, HEAD)] = parts[s][h, a]


def forward_kernel(t, tile, count, full_ref, kcnt_ref, kidx_ref, q_ref, *refs):
    parts, (out_ref, lse_ref, k_few, v_few, k_ref, v_ref) = refs[:2 * t], refs[2 * t:]
    row = pl.program_id(0)
    q = q_ref[...]

    @pl.when(row == 0)
    def _():
        join_parts(parts, k_ref, v_ref)

    def finish(s, v):
        top = jnp.max(s, axis=1, keepdims=True)
        p = jnp.exp2(s - top)
        mass = jnp.sum(p, axis=1, keepdims=True)
        out = dot(p.astype(BF16), v)
        out_ref[...] = (out / mass).astype(BF16)
        lse_ref[...] = jnp.broadcast_to(top + jnp.log2(mass), lse_ref.shape)

    scale = HEAD ** -0.5 * LOG2E

    @pl.when(full_ref[row] == 1)
    def _():
        keys = k_ref[...].reshape(-1, HEAD)
        finish(dot(q, keys, NT) * scale, v_ref[...].reshape(-1, HEAD))

    @pl.when(full_ref[row] == 0)
    def _():
        gather_tiles(k_ref, kidx_ref, row, k_few, tile, count)
        gather_tiles(v_ref, kidx_ref, row, v_few, tile, count)
        s = dot(q, k_few[...], NT) * scale
        column = lax.broadcasted_iota(jnp.int32, s.shape, 1)
        s = jnp.where(column < kcnt_ref[row] * tile, s, NEG_BIG)
        finish(s, v_few[...])


def backward_kernel(t, tile, count, full_ref, kcnt_ref, kidx_ref, q_ref, g_ref, o_ref, lse_ref, *refs):
    parts, dkv_refs = refs[:2 * t], refs[2 * t + 1:3 * t + 1]
    dq_ref = refs[2 * t]
    k_few, v_few, k_ref, v_ref, dk_acc, dv_acc = refs[3 * t + 1:]
    row = pl.program_id(0)
    last = pl.num_programs(0) - 1

    @pl.when(row == 0)
    def _():
        join_parts(parts, k_ref, v_ref)
        dk_acc[...] = jnp.zeros_like(dk_acc)
        dv_acc[...] = jnp.zeros_like(dv_acc)

    q = q_ref[...]
    g = g_ref[...]
    delta = jnp.sum(g.astype(F32) * o_ref[...].astype(F32), axis=1, keepdims=True)
    lse = lse_ref[:, :1]
    unit = HEAD ** -0.5
    scale = unit * LOG2E

    def gradients(keys, values, mask):
        s = dot(q, keys, NT)
        p = jnp.exp2(s * scale - lse)
        if mask is not None:
            p = jnp.where(mask(p.shape), p, 0.0)
        ds = (p * (dot(g, values, NT) - delta)).astype(BF16)
        dq_ref[...] = (dot(ds, keys) * unit).astype(BF16)
        return dot(ds, q, TN) * unit, dot(p.astype(BF16), g, TN)

    @pl.when(full_ref[row] == 1)
    def _():
        dk, dv = gradients(k_ref[...].reshape(-1, HEAD), v_ref[...].reshape(-1, HEAD), None)
        dk_acc[...] += dk.reshape(dk_acc.shape)
        dv_acc[...] += dv.reshape(dv_acc.shape)

    @pl.when(full_ref[row] == 0)
    def _():
        gather_tiles(k_ref, kidx_ref, row, k_few, tile, count)
        gather_tiles(v_ref, kidx_ref, row, v_few, tile, count)

        def mask(shape):
            return lax.broadcasted_iota(jnp.int32, shape, 1) < kcnt_ref[row] * tile

        dk, dv = gradients(k_few[...], v_few[...], mask)
        for j in range(count):
            at = kidx_ref[row, j]
            dk_acc[at] += dk[j * tile:(j + 1) * tile]
            dv_acc[at] += dv[j * tile:(j + 1) * tile]

    @pl.when(row == last)
    def _():
        tiles = dk_acc.shape[0] // t
        for s, dkv_ref in enumerate(dkv_refs):
            at = pl.ds(s * tiles, tiles)
            dkv_ref[0] = dk_acc[at].reshape(dkv_ref.shape[1:]).astype(BF16)
            dkv_ref[1] = dv_acc[at].reshape(dkv_ref.shape[1:]).astype(BF16)


def whole_block(shape):
    return pl.BlockSpec(shape, lambda *_: (0,) * len(shape))


def one_array(which, length):
    return pl.BlockSpec((1, length, HEAD), lambda *_: (which, 0, 0))


def simple_call(kernel, name, scalars, inputs, outputs, scratch=()):
    size = sum(2 * math.prod(x.shape) for x in list(inputs) + list(outputs))
    return pl.pallas_call(
        kernel,
        grid_spec=pltpu.PrefetchScalarGridSpec(
            num_scalar_prefetch=1,
            grid=(1,),
            in_specs=[whole_block(x.shape) for x in inputs],
            out_specs=[whole_block(x.shape) for x in outputs],
            scratch_shapes=scratch,
        ),
        out_shape=outputs,
        compiler_params=pltpu.CompilerParams(vmem_limit_bytes=48 * 2**20),
        cost_estimate=pl.CostEstimate(flops=0, bytes_accessed=2 * size, transcendentals=0),
        name=name,
    )(scalars, *inputs)


def shifts(t, s):
    return [(c, (c + s) % t) for c in range(t)]


def place_xor_kernel(place_ref, *refs):
    sources, out_ref = refs[:-1], refs[-1]
    step = pl.program_id(0)
    for u in range(2):
        own, beside, above, upper, lower = sources[5 * u:5 * u + 5]
        for v, source in enumerate((own, beside, above)):
            @pl.when(step == 4 * u + v)
            def _(source=source):
                out_ref[...] = source[...].astype(F32)

        @pl.when(step == 4 * u + 3)
        def _(upper=upper, lower=lower):
            middle = upper.shape[0]
            out_ref[:middle] = upper[...].astype(F32)
            out_ref[middle:] = lower[...].astype(F32)


def gather_tiles_by_core(n, t, tile_sum, chip, core, beside_chunks):
    in_plane = n // PLANES
    plane, seat = chip // in_plane, chip % in_plane
    tile_rows, cols = tile_sum.shape
    across = [
        (i * t + c, (i ^ 2 * in_plane) * t + c)
        for i in range(n) for c in range(t) if i // in_plane // 2 == c
    ]
    from_half = lax.ppermute(tile_sum, ("ctx", "tp"), across)

    def swap(x, k):
        return lax.ppermute(x, "ctx", [(i, i ^ k) for i in range(n)])

    first = jnp.where(plane // 2 == core, tile_sum, from_half)
    second = swap(first, in_plane)
    beside, above = swap(first, 1), swap(first, 2)
    *_, beside_chunks = lax.optimization_barrier((second, beside, above, beside_chunks))
    middle = tile_rows // 2
    sources = [first, beside, above, swap(beside[:middle], 2), swap(above[middle:], 1)]
    beside, above = swap(second, 1), swap(second, 2)
    sources += [second, beside, above, swap(beside[:middle], 2), swap(above[middle:], 1)]
    place = jnp.stack([plane % 2, seat]).astype(jnp.int32)
    return pl.pallas_call(
        place_xor_kernel,
        grid_spec=pltpu.PrefetchScalarGridSpec(
            num_scalar_prefetch=1,
            grid=(8,),
            in_specs=[whole_block(x.shape) for x in sources],
            out_specs=pl.BlockSpec(
                (tile_rows, cols), lambda s, place: (s // 4 ^ place[0], s % 4 ^ place[1])
            ),
        ),
        out_shape=jax.ShapeDtypeStruct((2 * tile_rows, in_plane * cols), F32),
        compiler_params=pltpu.CompilerParams(vmem_limit_bytes=48 * 2**20),
        cost_estimate=pl.CostEstimate(flops=0, bytes_accessed=2**24, transcendentals=0),
        name="place",
    )(place, *sources), beside_chunks


def per_device(n, t, queries, key_vectors, value_vectors, out_weight, out_grad, block_segment):
    rows, width = queries.shape
    heads_here = width // HEAD
    heads = heads_here * t
    sub = rows // t
    tile = min(sub, BLK)
    per_chunk = sub // tile
    core = lax.axis_index("tp")
    chip = lax.axis_index("ctx")
    in_plane = n // PLANES
    heads_plane = heads // PLANES
    seat = chip % in_plane

    def tp_swap(pick):
        got = [pick(core)]
        for s in range(1, t):
            got.append(lax.ppermute(pick((core + s) % t), "tp", shifts(t, s)))
        return [lax.select_n((core - p) % t, *got) for p in range(t)]

    def tp_gather(x):
        return tp_swap(lambda _: x)

    def shape(*dims):
        return jax.ShapeDtypeStruct(dims, BF16)

    where = jnp.stack([chip, core]).astype(jnp.int32)
    held = [(i % in_plane - i // in_plane) % in_plane < heads_plane for i in range(n)]

    chunk_row = jnp.arange(n)[:, None] * rows + jnp.arange(per_chunk)[None, :] * tile

    def tile_segments(part):
        return jnp.take(block_segment, ((chunk_row + part * sub) // BLK).reshape(-1))

    seg_parts = [tile_segments((core - s) % t) for s in range(t)]
    seg_q = seg_parts[0]
    seg_k = jnp.concatenate(seg_parts)
    full = (seg_q == 0) | (seg_q == TARGET)
    permitted = (seg_k[None] == 0) | (seg_k[None] == seg_q[:, None])
    total_blocks = block_segment.shape[0]
    count = (TXT_BLK + -(-(total_blocks - TXT_BLK) // RUNS)) * (BLK // tile)
    kcnt = jnp.sum(permitted.astype(jnp.int32), axis=1)
    tiles_k = seg_k.shape[0]
    ids = jnp.arange(tiles_k)
    place = jnp.sum((permitted[:, None, :] & (ids[None, None, :] < ids[None, :, None])).astype(jnp.int32), axis=2)
    hit = permitted[:, None, :] & (place[:, None, :] == jnp.arange(count)[None, :, None])
    kidx = jnp.sum(jnp.where(hit, ids[None, None, :], 0), axis=2).astype(jnp.int32)
    full = full.astype(jnp.int32)

    def other_rows(*arrays):
        return [
            lax.ppermute(
                jnp.stack([
                    lax.dynamic_slice_in_dim(x, (core + s) % t * sub, sub, 0) for x in arrays
                ]),
                "tp", shifts(t, s),
            )
            for s in range(1, t)
        ]

    got_qkv = other_rows(queries, key_vectors, value_vectors)

    half = out_grad.shape[1]
    model = half * t
    full_grad = jnp.concatenate(tp_gather(out_grad), axis=1)
    grad_attn = dot(full_grad, out_weight, NT).astype(BF16)
    got_g = other_rows(grad_attn)

    cols = model // in_plane
    mine = lax.dynamic_slice_in_dim(full_grad, core * sub, sub, 0)
    plane_got = [lax.dynamic_slice_in_dim(mine, seat * cols, cols, 1)]
    for k in range(1, in_plane):
        there = lax.dynamic_slice_in_dim(mine, (seat ^ k) * cols, cols, 1)
        plane_got.append(lax.ppermute(there, "ctx", [(i, i ^ k) for i in range(n)]))
    (plane_grad,) = simple_call(
        functools.partial(seats_kernel, in_plane), "seats", where, plane_got, [shape(in_plane, sub, cols)]
    )
    def pack(arrays, got):
        (sent,) = simple_call(
            functools.partial(pack_kernel, n, t, len(arrays)), "pack", where,
            arrays + got, [shape(n, len(arrays), sub, HEAD)],
            [pltpu.VMEM((heads, len(arrays), sub, HEAD), BF16)],
        )
        return sent

    sent_qkv = pack([queries, key_vectors, value_vectors], got_qkv)
    sent_g = pack([grad_attn], got_g)
    chunks = lax.all_to_all(sent_qkv, "ctx", 0, 0, tiled=True)
    chunks, sent_g, plane_grad = lax.optimization_barrier((chunks, sent_g, plane_grad))
    lines = [[a * in_plane + b for a in range(PLANES)] for b in range(in_plane)]
    slice_grad = lax.all_gather(plane_grad, "ctx", axis_index_groups=lines)
    slice_grad = slice_grad.reshape(n * sub, cols)
    g_rows = lax.all_to_all(sent_g, "ctx", 0, 0, tiled=True).reshape(n * sub, HEAD)
    length = n * sub
    q_rows, kv = simple_call(
        functools.partial(join_kernel, n), "join", where, [chunks], [shape(length, HEAD), shape(2, length, HEAD)]
    )
    kv_all = [kv] + [lax.ppermute(kv, "tp", shifts(t, s)) for s in range(1, t)]

    tiles_q = n * per_chunk
    few = [pltpu.VMEM((count * tile, HEAD), BF16)] * 2 + [pltpu.VMEM((tiles_k, tile, HEAD), BF16)] * 2
    params = pltpu.CompilerParams(vmem_limit_bytes=48 * 2**20)
    part_blocks = [one_array(0, length), one_array(1, length)] * t
    part_arrays = [a for pack in kv_all for a in (pack, pack)]
    row_block = pl.BlockSpec((tile, HEAD), lambda r, *_: (r, 0))
    attn, lse = pl.pallas_call(
        functools.partial(forward_kernel, t, tile, count),
        grid_spec=pltpu.PrefetchScalarGridSpec(
            num_scalar_prefetch=3,
            grid=(tiles_q,),
            in_specs=[row_block] + part_blocks,
            out_specs=[row_block, row_block],
            scratch_shapes=few,
        ),
        out_shape=[shape(length, HEAD), jax.ShapeDtypeStruct((length, HEAD), F32)],
        compiler_params=params,
        cost_estimate=pl.CostEstimate(flops=16 * 10**9, bytes_accessed=5 * 2**20, transcendentals=2**22),
        name="forward",
    )(full, kcnt, kidx, q_rows, *part_arrays)

    travel = [attn] + [
        lax.ppermute(attn, "ctx", [(i, i ^ k) for i in range(n) if held[i]]) for k in range(1, in_plane)
    ]
    *travel, attn = lax.optimization_barrier((*travel, attn))

    dq, *dkv = pl.pallas_call(
        functools.partial(backward_kernel, t, tile, count),
        grid_spec=pltpu.PrefetchScalarGridSpec(
            num_scalar_prefetch=3,
            grid=(tiles_q,),
            in_specs=[row_block] * 4 + part_blocks,
            out_specs=[row_block] + [whole_block((2, length, HEAD))] * t,
            scratch_shapes=few + [pltpu.VMEM((tiles_k, tile, HEAD), F32)] * 2,
        ),
        out_shape=[shape(length, HEAD)] + [shape(2, length, HEAD)] * t,
        compiler_params=params,
        cost_estimate=pl.CostEstimate(flops=20 * 10**9, bytes_accessed=8 * 2**20, transcendentals=2**22),
        name="backward",
    )(full, kcnt, kidx, q_rows, g_rows, attn, lse, *part_arrays)

    got_dkv = [
        lax.ppermute(dkv[s], "tp", [(c, (c - s) % t) for c in range(t)]) for s in range(1, t)
    ]
    (sent,) = simple_call(
        functools.partial(unjoin_kernel, n, t), "unjoin", where,
        [attn, dq, dkv[0]] + got_dkv, [shape(n, 4, sub, HEAD)],
    )
    chunks = lax.all_to_all(sent, "ctx", 0, 0, tiled=True)

    tile_rows = heads_plane * HEAD
    by_core = in_plane == 4 and t == 2
    piece = tile_rows if by_core else tile_rows // t
    step_rows = length // 4
    tile_own, *tile_sends = pl.pallas_call(
        functools.partial(tile_kernel, in_plane, heads_plane, t),
        grid_spec=pltpu.PrefetchScalarGridSpec(
            num_scalar_prefetch=1,
            grid=(4,),
            in_specs=[pl.BlockSpec((step_rows, HEAD), lambda r, *_: (r, 0))] * in_plane
            + [pl.BlockSpec((step_rows, cols), lambda r, *_: (r, 0))],
            out_specs=[whole_block((piece, cols))] * t,
            scratch_shapes=[
                pltpu.VMEM((in_plane, step_rows, HEAD), BF16), pltpu.VMEM((tile_rows, cols), F32)
            ],
        ),
        out_shape=[jax.ShapeDtypeStruct((piece, cols), F32)] + [shape(piece, cols)] * (t - 1),
        compiler_params=params,
        cost_estimate=pl.CostEstimate(flops=5 * 10**9, bytes_accessed=2**22, transcendentals=0),
        name="tile",
    )(where, *travel, slice_grad)
    tile_sum = tile_own
    for s in range(1, t):
        tile_sum = tile_sum + lax.ppermute(tile_sends[s - 1], "tp", shifts(t, s)).astype(F32)
    if by_core:
        grad_weight, chunks = gather_tiles_by_core(n, t, tile_sum.astype(BF16), chip, core, chunks)
    else:
        tiles = lax.all_gather(tile_sum.astype(BF16), "ctx")
        here = n // t
        tiles_core = [tiles] + [
            lax.ppermute(
                lax.dynamic_slice_in_dim(tiles, (core + s) % t * here, here, 0), "tp", shifts(t, s)
            )
            for s in range(1, t)
        ]
        grad_weight = pl.pallas_call(
            functools.partial(place_kernel, t),
            grid_spec=pltpu.PrefetchScalarGridSpec(
                num_scalar_prefetch=1,
                grid=(here,),
                in_specs=[pl.BlockSpec((1, piece, cols), lambda r, where: (where[1] * here + r, 0, 0))]
                + [pl.BlockSpec((1, piece, cols), lambda r, *_: (r, 0, 0))] * (t - 1),
                out_specs=pl.BlockSpec((tile_rows, cols), lambda r, *_: (r // in_plane, r % in_plane)),
            ),
            out_shape=jax.ShapeDtypeStruct((width, model), F32),
            compiler_params=params,
            cost_estimate=pl.CostEstimate(flops=0, bytes_accessed=2**24, transcendentals=0),
            name="place",
        )(where, *tiles_core)

    mine = simple_call(
        functools.partial(by_core_kernel, n, t), "by_core", where, [chunks],
        [shape(heads_here, 4, sub, HEAD)] * t, [pltpu.VMEM((heads, 4, sub, HEAD), BF16)],
    )
    parts = [mine[0]] + [lax.ppermute(mine[s], "tp", shifts(t, s)) for s in range(1, t)]
    attention, grad_queries, grad_keys, grad_values = simple_call(
        functools.partial(unpack_kernel, t), "unpack", where, parts, [shape(rows, width)] * 4
    )
    projected = dot(attention, out_weight)
    own = lax.dynamic_slice_in_dim(projected, core * half, half, 1)
    for s in range(1, t):
        there = lax.dynamic_slice_in_dim(projected, (core + s) % t * half, half, 1)
        own = own + lax.ppermute(there.astype(BF16), "tp", shifts(t, s)).astype(F32)
    attention_out = own.astype(BF16)

    return attention_out, grad_queries, grad_keys, grad_values, grad_weight


def solution(mesh):
    n, t = mesh.shape["ctx"], mesh.shape["tp"]
    in_specs = (P("ctx", "tp"), P("ctx", "tp"), P("ctx", "tp"), P("tp", None), P("ctx", "tp"), P())
    out_specs = (P("ctx", "tp"), P("ctx", "tp"), P("ctx", "tp"), P("ctx", "tp"), P("tp", None))
    return jax.shard_map(
        functools.partial(per_device, n, t), mesh=mesh, in_specs=in_specs, out_specs=out_specs, check_vma=False
    )
```
